32 devices in a mesh: dp: 4 (over z), seq: 8 (over y, x, core).
Axes of the slice: x: 2, y: 2, z: 4, core: 2. Of those that a mesh axis runs over, the one named last changes fastest.
Arguments:
- tokens: bfloat16 [8, 4096, 768], P('dp', 'seq'), may hold values from -6 to 6
- w_qkv: bfloat16 [768, 2304], P(('dp', 'seq')), may hold values from -0.21875 to 0.21875
- qv_bias: bfloat16 [1536], P(('dp', 'seq')), may hold values from -1.1953125 to 1.1953125
- w_proj: bfloat16 [768, 768], P(('dp', 'seq')), may hold values from -3 to 3
- proj_bias: bfloat16 [768], P(('dp', 'seq')), may hold values from -1.1953125 to 1.1953125
- w_fc1: bfloat16 [768, 3072], P(('dp', 'seq')), may hold values from -0.21875 to 0.21875
- fc1_bias: bfloat16 [3072], P(('dp', 'seq')), may hold values from -1.1953125 to 1.1953125
- w_fc2: bfloat16 [3072, 768], P(('dp', 'seq')), may hold values from -0.15625 to 0.15625
- fc2_bias: bfloat16 [768], P(('dp', 'seq')), may hold values from -1.1953125 to 1.1953125
- norm_gains: bfloat16 [2, 768], P(None, ('dp', 'seq')), may hold values from 0.5 to 1.5
- norm_biases: bfloat16 [2, 768], P(None, ('dp', 'seq')), may hold values from -1.1953125 to 1.1953125
- rel_tables: bfloat16 [2, 127, 64], replicated, may hold values from -0.75 to 0.75
- cotangent: bfloat16 [8, 4096, 768], P('dp', 'seq'), may hold values from -6 to 6
Outputs:
- result: bfloat16 [8, 4096, 768], P('dp', 'seq')
- tokens_grad: bfloat16 [8, 4096, 768], P('dp', 'seq')
- w_qkv_grad: float32 [768, 2304], P(('dp', 'seq'))
- qv_bias_grad: float32 [1536], P(('dp', 'seq'))
- w_proj_grad: float32 [768, 768], P(('dp', 'seq'))
- proj_bias_grad: float32 [768], P(('dp', 'seq'))
- w_fc1_grad: float32 [768, 3072], P(('dp', 'seq'))
- fc1_bias_grad: float32 [3072], P(('dp', 'seq'))
- w_fc2_grad: float32 [3072, 768], P(('dp', 'seq'))
- fc2_bias_grad: float32 [768], P(('dp', 'seq'))
- norm_gains_grad: float32 [2, 768], P(None, ('dp', 'seq'))
- norm_biases_grad: float32 [2, 768], P(None, ('dp', 'seq'))
- rel_tables_grad: float32 [2, 127, 64], replicated
The draws below stay inside these ranges and needn't reach their ends.
All inputs are finite; a program needn't handle non-finite values.
Results may differ from the reference program's by a relative error of at most 0.013.
Values may be sent and summed in bfloat16 or wider, within the bound.
No kernel may reach another device: no remote copies, remote signals or barrier semaphores. Data moves between devices by JAX's collectives and lax.ppermute only.
A program may use at most 832 MiB of HBM per device.

```python
import jax
import jax.numpy as jnp
from jax import lax

D = 768
HEADS = 12
HD = 64
FF = 3072
GRID = 64
TABLE = 127
IMAGES = 8


def raised(entries, rng, source, target, shards_of, factor):
    owner, partner = [(jnp.arange(entries.shape[dim]) // (entries.shape[dim] // shards_of)).reshape([-1 if axis == dim else 1 for axis in range(entries.ndim)]) for dim in (source, target)]
    chosen = jax.random.permutation(rng, shards_of)[partner]
    strong = (owner == chosen) | (owner == (partner + shards_of // 2) % shards_of)
    return jnp.where(strong, factor * entries, entries)


def shard_levels(key, dims, cuts, least, top_value):
    level, own = 1.0, jax.random.fold_in(key, 6)
    for position, shards_of in cuts:
        heights = jnp.exp(jax.random.uniform(jax.random.fold_in(own, position), (shards_of,), jnp.float32, least / len(cuts), top_value / len(cuts)))
        level = level * jnp.repeat(heights, dims[position] // shards_of).reshape([-1 if axis == position else 1 for axis in range(len(dims))])
    return level


def centred(stream_key, shape, width, limit, split=(), held_as=jnp.bfloat16):
    entries = jax.random.normal(stream_key, shape, jnp.float32) * width
    if len(split) > 0:
        entries = shard_levels(stream_key, shape, split, -0.22, 0.18) * entries
    return jnp.clip(entries, min=-limit, max=limit).astype(held_as)


def gaussian_with(own_key, extent, scale, reach, cuts, heavy, kind=jnp.bfloat16):
    result = scale * jax.random.normal(own_key, extent, jnp.float32)
    if cuts:
        result = result * shard_levels(own_key, extent, cuts, -0.22, 0.18)
    return jnp.clip(raised(result, jax.random.fold_in(own_key, 3), *heavy), -reach, reach).astype(kind)


def setup_inputs(seed: int = 0) -> dict:
    key_list = jax.random.split(jax.random.key(seed), 14)
    tokens = gaussian_with(key_list[0], (IMAGES, GRID * GRID, D), 1.0, 6.0, ((0, 4), (1, 8)), (1, 2, 8, 2.0))
    w_qkv = centred(key_list[1], (D, 3 * D), D ** -0.5, 0.21875, ((0, 32),))
    qv_bias = centred(key_list[2], (2 * D,), 0.2, 1.1953125, ((0, 32),))
    w_proj = centred(key_list[3], (D, D), (max(D // 192, 1)) ** -0.5, 3.0, ((0, 32),))
    proj_bias = centred(key_list[4], (D,), 0.2, 1.1953125, ((0, 32),))
    w_fc1 = centred(key_list[5], (D, FF), D ** -0.5, 0.21875, ((0, 32),))
    fc1_bias = centred(key_list[6], (FF,), 0.2, 1.1953125, ((0, 32),))
    w_fc2 = centred(key_list[7], (FF, D), (FF // 2) ** -0.5, 0.15625, ((0, 32),))
    fc2_bias = centred(key_list[8], (D,), 0.2, 1.1953125, ((0, 32),))
    norm_gains = jnp.clip(1.0 + 0.1 * jax.random.normal(key_list[9], (2, D), jnp.float32), 0.5, 1.5).astype(jnp.bfloat16)
    norm_biases = centred(key_list[10], (2, D), 0.2, 1.1953125, ((1, 32),))
    rel_tables = centred(key_list[11], (2, TABLE, HD), 0.125, 0.75)
    cotangent = gaussian_with(key_list[12], (IMAGES, GRID * GRID, D), 1.0, 6.0, ((0, 4), (1, 8)), (1, 2, 8, 2.0))
    return {"tokens": tokens, "w_qkv": w_qkv, "qv_bias": qv_bias, "w_proj": w_proj, "proj_bias": proj_bias, "w_fc1": w_fc1, "fc1_bias": fc1_bias, "w_fc2": w_fc2, "fc2_bias": fc2_bias, "norm_gains": norm_gains, "norm_biases": norm_biases, "rel_tables": rel_tables, "cotangent": cotangent}


@jax.custom_vjp
def low(v):
    return lax.optimization_barrier(v.astype(jnp.bfloat16)).astype(jnp.float32)

@jax.custom_vjp
def low_back(v):
    return v

def low_keep(v):
    return (low(v), None)

def low_pass(kept, grad):
    return (grad,)

def back_keep(v):
    return (v, None)

def back_low(kept, grad):
    return (low(grad),)
low.defvjp(low_keep, low_pass)
low_back.defvjp(back_keep, back_low)
EPS = 1e-06
HIGH = lax.Precision.HIGHEST

def layer_norm(values, gain, shift):
    center = lax.optimization_barrier(jnp.mean(values, axis=-1, keepdims=True))
    centered = values - center
    spread = lax.optimization_barrier(jnp.mean(centered * centered, axis=-1, keepdims=True))
    return centered * lax.rsqrt(spread + EPS) * gain + shift

def position_tables(tables):
    number = GRID * GRID
    tokens_at = jnp.arange(number, dtype=jnp.int32)
    offsets = jnp.arange(GRID, dtype=jnp.int32)
    row_index = (tokens_at[:, None] // GRID - offsets[None, :] + GRID - 1).astype(jnp.int32)
    col_index = (tokens_at[:, None] % GRID - offsets[None, :] + GRID - 1).astype(jnp.int32)
    return (tables[0][row_index], tables[1][col_index])

def image_forward(image, weights, rel_rows, rel_cols):
    w_qkv, qv_bias, w_proj, proj_bias, w_fc1, fc1_bias, w_fc2, fc2_bias, gains, shifts = weights
    number = GRID * GRID
    normed1 = low(layer_norm(image, gains[0], shifts[0]))
    full_bias = jnp.concatenate([qv_bias[:D], jnp.zeros((D,), qv_bias.dtype), qv_bias[D:]])
    qkv = low(low_back(jnp.dot(normed1, w_qkv, precision=HIGH) + full_bias))
    queries = qkv[:, :D].reshape(number, HEADS, HD)
    keys_all = qkv[:, D:2 * D].reshape(number, HEADS, HD)
    values_all = qkv[:, 2 * D:].reshape(number, HEADS, HD)
    blocksize = min(512, number)

    def attend(pieces):
        query_block, row_block, col_block = pieces
        scores = HD ** (-0.5) * jnp.einsum('rhc,nhc->hrn', query_block, keys_all, precision=HIGH)
        bias_rows = jnp.einsum('rhc,rkc->hrk', query_block, row_block, precision=HIGH)
        bias_cols = jnp.einsum('rhc,rkc->hrk', query_block, col_block, precision=HIGH)
        scores = scores.reshape(HEADS, blocksize, GRID, GRID) + bias_rows[:, :, :, None] + bias_cols[:, :, None, :]
        scores = low_back(scores.reshape(HEADS, blocksize, number))
        shifted = jnp.exp(scores - lax.optimization_barrier(jnp.max(scores, axis=-1, keepdims=True)))
        probs = low(shifted / lax.optimization_barrier(jnp.sum(shifted, axis=-1, keepdims=True)))
        return jnp.einsum('hrn,nhc->rhc', probs, values_all, precision=HIGH)
    blocks = number // blocksize
    attended = lax.map(jax.checkpoint(attend), (queries.reshape(blocks, blocksize, HEADS, HD), rel_rows.reshape(blocks, blocksize, GRID, HD), rel_cols.reshape(blocks, blocksize, GRID, HD)))
    attended = low(low_back(attended.reshape(number, D)))
    mixed = image + low_back(jnp.dot(attended, w_proj, precision=HIGH) + proj_bias)
    normed2 = low(layer_norm(mixed, gains[1], shifts[1]))
    pre = low_back(jnp.dot(normed2, w_fc1, precision=HIGH) + fc1_bias)
    activated = low(jax.nn.gelu(pre, approximate=False))
    return mixed + low_back(jnp.dot(activated, w_fc2, precision=HIGH) + fc2_bias)

def reference(tokens, w_qkv, qv_bias, w_proj, proj_bias, w_fc1, fc1_bias, w_fc2, fc2_bias, norm_gains, norm_biases, rel_tables, cotangent):
    weights = tuple((array.astype(jnp.float32) for array in (w_qkv, qv_bias, w_proj, proj_bias, w_fc1, fc1_bias, w_fc2, fc2_bias, norm_gains, norm_biases)))
    tables = rel_tables.astype(jnp.float32)
    images = tokens.astype(jnp.float32)

    def forward(images, weights, tables):
        rel_rows, rel_cols = position_tables(tables)
        checked = jax.checkpoint(image_forward)

        def step(carried, image):
            return (carried, checked(image, weights, rel_rows, rel_cols))
        _, outputs = lax.scan(step, jnp.zeros((), jnp.float32), images)
        return outputs
    outputs, pull = jax.vjp(forward, images, weights, tables)
    grad_images, grad_weights, grad_tables = pull(cotangent.astype(jnp.float32))
    return (outputs.astype(jnp.bfloat16), grad_images.astype(jnp.bfloat16), grad_weights[0], grad_weights[1], grad_weights[2], grad_weights[3], grad_weights[4], grad_weights[5], grad_weights[6], grad_weights[7], grad_weights[8], grad_weights[9], grad_tables)
```

```python
from functools import partial
import math

import jax
import jax.numpy as jnp
from jax import lax
from jax.experimental import pallas as pl
from jax.experimental.pallas import tpu as pltpu
from jax.sharding import PartitionSpec as P

HEADS = 12
HD = 64
GRID = 64
MB = 2
TABLE = 127


EPS = 1e-06
HIGH = lax.Precision.HIGHEST
IMAGES = 8
AXES = ("dp", "seq")

TB = 512
CK = 512
ROWS = CK // GRID
LOG2E = 1.4426950408889634
NN = (((1,), (0,)), ((), ()))
NT = (((1,), (1,)), ((), ()))
TN = (((0,), (0,)), ((), ()))
BF = jnp.bfloat16
F32 = jnp.float32


def dot(a, b, dims):
    return lax.dot_general(a, b, dims, preferred_element_type=F32)


def col_hot(n):
    key = lax.broadcasted_iota(jnp.int32, (n, GRID), 0) & (GRID - 1)
    col = lax.broadcasted_iota(jnp.int32, (n, GRID), 1)
    return (key == col).astype(F32)


def build_keys(qkv_ref, kaug, start, n):
    rows = pl.ds(start, n)
    k = qkv_ref[rows, HD : 2 * HD].astype(F32)
    pair = jnp.concatenate([k, col_hot(n)], axis=1).astype(BF)
    kaug[rows, : 2 * HD] = pair
    kaug[rows, 2 * HD :] = pair


def fwd_kernel(n_chunks, qkv_ref, tab_ref, oT_ref, oTf_ref, qaT_ref, sub_ref, kaug, vta):
    i = pl.program_id(0)
    tg = TB // GRID

    @pl.when(i == 0)
    def _():
        for c in range(n_chunks):
            build_keys(qkv_ref, kaug, c * CK, CK)
            rows = pl.ds(c * CK, CK)
            vT = qkv_ref[rows, 2 * HD :].astype(F32).T
            vta[0:HD, rows] = vT.astype(BF)
            one = lax.broadcasted_iota(jnp.int32, (16, CK), 0) == 0
            vta[HD : HD + 16, rows] = one.astype(F32).astype(BF)

    q = qkv_ref[pl.ds(pl.multiple_of(i * TB, TB), TB), :HD]
    gr = dot(q, tab_ref[0], NT) * LOG2E
    gc = dot(q, tab_ref[1], NT) * LOG2E
    brs, bcs = [], []
    for g in range(tg):
        sl = slice(g * GRID, (g + 1) * GRID)
        brs.append(pltpu.roll(gr[sl], i * tg + g, 1))
        bcs.append(pltpu.roll(gc[sl], 0, 1, stride=1, stride_axis=0))
    br = jnp.concatenate(brs, axis=0)
    bc = jnp.concatenate(bcs, axis=0)
    qs = q.astype(F32) * (HD ** -0.5 * LOG2E)
    cat = jnp.concatenate([qs, bc[:, :GRID]], axis=1).T
    hi = cat.astype(BF)
    lo = (cat - hi.astype(F32)).astype(BF)
    qaT_ref[...] = jnp.concatenate([hi, lo], axis=0)
    sub_ref[...] = br.T[:GRID]
    qa = qaT_ref[...]

    m = jnp.full((1, TB), -jnp.inf, F32)
    acc = jnp.zeros((HD + 16, TB), F32)
    for c in range(n_chunks):
        s = dot(kaug[c * CK : (c + 1) * CK, :], qa, NN).reshape(ROWS, GRID, TB)
        b8 = sub_ref[c * ROWS : (c + 1) * ROWS, :]
        mc = jnp.max(jnp.max(s, axis=1) + b8, axis=0, keepdims=True)
        p = jnp.exp2(s - (mc - b8)[:, None, :]).astype(BF).reshape(CK, TB)
        o = dot(vta[:, c * CK : (c + 1) * CK], p, NN)
        new = jnp.maximum(m, mc)
        acc = acc * jnp.exp2(m - new) + o * jnp.exp2(mc - new)
        m = new
    total = acc[HD : HD + 1]
    out = acc[:HD] / total
    oT_ref[0] = out.astype(BF)
    oTf_ref[...] = out
    sub_ref[...] = (m + jnp.log2(total)) - sub_ref[...]


def heads_forward(qkv, tab):
    n = qkv.shape[0]
    steps = n // TB
    return pl.pallas_call(
        partial(fwd_kernel, n // CK),
        grid=(steps,),
        in_specs=[
            pl.BlockSpec((n, 3 * HD), lambda i: (0, 0)),
            pl.BlockSpec((2, 2 * GRID, HD), lambda i: (0, 0, 0)),
        ],
        out_specs=[
            pl.BlockSpec((1, HD, TB), lambda i: (i, 0, 0)),
            pl.BlockSpec((HD, TB), lambda i: (0, i)),
            pl.BlockSpec((4 * HD, TB), lambda i: (0, i)),
            pl.BlockSpec((GRID, TB), lambda i: (0, i)),
        ],
        out_shape=[
            jax.ShapeDtypeStruct((steps, HD, TB), BF),
            jax.ShapeDtypeStruct((HD, n), F32),
            jax.ShapeDtypeStruct((4 * HD, n), BF),
            jax.ShapeDtypeStruct((GRID, n), F32),
        ],
        scratch_shapes=[pltpu.VMEM((n, 4 * HD), BF), pltpu.VMEM((HD + 16, n), BF)],
        compiler_params=pltpu.CompilerParams(vmem_limit_bytes=56 * 2**20),
        cost_estimate=pl.CostEstimate(
            flops=4 * n * n * 4 * HD, bytes_accessed=16 * 2**20, transcendentals=n * n
        ),
    )(qkv, tab)


def bwd_kernel(
    n_chunks, qkv_ref, tab_ref, qaT_ref, sub_ref, oTf_ref, doT_ref,
    dqkv_ref, dtab_ref, kaug, vaug, kta, dkv, dqa
):
    i = pl.program_id(0)
    tg = TB // GRID
    n_steps = pl.num_programs(0)

    @pl.when(i == 0)
    def _():
        for c in range(n_chunks):
            build_keys(qkv_ref, kaug, c * CK, CK)
            rows = pl.ds(c * CK, CK)
            k = qkv_ref[rows, HD : 2 * HD].astype(F32)
            both = jnp.concatenate([k, col_hot(CK)], axis=1).T
            kta[0 : 2 * HD, rows] = both.astype(BF)
            key = lax.broadcasted_iota(jnp.int32, (16, CK), 1) >> 6
            hot = lax.broadcasted_iota(jnp.int32, (16, CK), 0) == key
            kta[2 * HD : 2 * HD + 16, rows] = hot.astype(F32).astype(BF)
            v = qkv_ref[rows, 2 * HD :].astype(F32)
            lane = lax.broadcasted_iota(jnp.int32, (CK, HD), 1)
            vaug[rows, :] = jnp.concatenate([v, (lane < 3).astype(F32)], axis=1).astype(BF)
            dkv[rows, :] = jnp.zeros((CK, 2 * HD), F32)
        dtab_ref[...] = jnp.zeros_like(dtab_ref)

    q = qkv_ref[pl.ds(pl.multiple_of(i * TB, TB), TB), :HD]
    doT = doT_ref[0].astype(F32)
    delta = -jnp.sum(doT * oTf_ref[...], axis=0, keepdims=True)
    d1 = delta.astype(BF)
    r1 = delta - d1.astype(F32)
    d2 = r1.astype(BF)
    d3 = (r1 - d2.astype(F32)).astype(BF)
    pad = jnp.concatenate(
        [d1.astype(F32), d2.astype(F32), d3.astype(F32), jnp.zeros((HD - 3, TB), F32)], axis=0
    )
    doa = jnp.concatenate([doT, pad], axis=0).astype(BF)
    do = jnp.concatenate([doT, jnp.zeros((HD, TB), F32)], axis=0).T
    qz = jnp.concatenate([jnp.zeros((TB, HD), F32), q.astype(F32)], axis=1)
    doq = jnp.concatenate([do, qz], axis=0).astype(BF)
    qa = qaT_ref[...]
    dqa[...] = jnp.zeros_like(dqa)

    for c in range(n_chunks):
        rows = slice(c * CK, (c + 1) * CK)
        s = dot(kaug[rows, :], qa, NN).reshape(ROWS, GRID, TB)
        b8 = sub_ref[c * ROWS : (c + 1) * ROWS, :]
        p = jnp.exp2(s - b8[:, None, :]).reshape(CK, TB)
        dp = dot(vaug[rows, :], doa, NN)
        ds = (p * dp).astype(BF)
        pd = jnp.concatenate([p.astype(BF), ds], axis=1)
        dkv[rows, :] += dot(pd, doq, NN)
        g = dot(kta[:, rows], ds, NN)
        dqa[0 : 2 * HD, :] += g[: 2 * HD]
        dqa[2 * HD + c * ROWS : 2 * HD + (c + 1) * ROWS, :] = g[2 * HD : 2 * HD + ROWS]

    grads = dqa[HD : 3 * HD, :].T
    lane = lax.broadcasted_iota(jnp.int32, (TB, 2 * GRID), 1)
    gcol = jnp.where(lane < GRID, grads, 0.0)
    grow = jnp.where(lane >= GRID, grads, 0.0)
    rs, cs = [], []
    col = lax.broadcasted_iota(jnp.int32, (GRID, 2 * GRID), 0)
    for g in range(tg):
        sl = slice(g * GRID, (g + 1) * GRID)
        rs.append(pltpu.roll(grow[sl], GRID - (i * tg + g), 1))
        x = gcol[sl]
        for bit in range(6):
            x = jnp.where((col >> bit) & 1 == 1, pltpu.roll(x, 2 * GRID - (1 << bit), 1), x)
        cs.append(x)
    drow = jnp.concatenate(rs, axis=0).astype(BF)
    dcol = jnp.concatenate(cs, axis=0).astype(BF)
    dq = dqa[:HD, :] * HD ** -0.5
    dq = dq + dot(tab_ref[0], drow, (((0,), (1,)), ((), ())))
    dq = dq + dot(tab_ref[1], dcol, (((0,), (1,)), ((), ())))
    dqkv_ref[i, 0:HD, :] = dq.astype(BF)
    dtab_ref[0] += dot(q, drow, TN)
    dtab_ref[1] += dot(q, dcol, TN)

    @pl.when(i == n_steps - 1)
    def _():
        for c in range(n_chunks):
            both = dkv[c * CK : (c + 1) * CK, :].T
            dqkv_ref[c, HD : 2 * HD, :] = (both[HD:] * HD ** -0.5).astype(BF)
            dqkv_ref[c, 2 * HD :, :] = both[:HD].astype(BF)


def heads_backward(qkv, tab, qaT, sub, oTf, doT):
    n = qkv.shape[0]
    steps = n // TB
    return pl.pallas_call(
        partial(bwd_kernel, n // CK),
        grid=(steps,),
        in_specs=[
            pl.BlockSpec((n, 3 * HD), lambda i: (0, 0)),
            pl.BlockSpec((2, 2 * GRID, HD), lambda i: (0, 0, 0)),
            pl.BlockSpec((4 * HD, TB), lambda i: (0, i)),
            pl.BlockSpec((GRID, TB), lambda i: (0, i)),
            pl.BlockSpec((HD, TB), lambda i: (0, i)),
            pl.BlockSpec((1, HD, TB), lambda i: (i, 0, 0)),
        ],
        out_specs=[
            pl.BlockSpec((steps, 3 * HD, TB), lambda i: (0, 0, 0)),
            pl.BlockSpec((2, HD, 2 * GRID), lambda i: (0, 0, 0)),
        ],
        out_shape=[
            jax.ShapeDtypeStruct((steps, 3 * HD, TB), BF),
            jax.ShapeDtypeStruct((2, HD, 2 * GRID), F32),
        ],
        scratch_shapes=[
            pltpu.VMEM((n, 4 * HD), BF),
            pltpu.VMEM((n, 2 * HD), BF),
            pltpu.VMEM((2 * HD + 16, n), BF),
            pltpu.VMEM((n, 2 * HD), F32),
            pltpu.VMEM((3 * HD, TB), F32),
        ],
        compiler_params=pltpu.CompilerParams(vmem_limit_bytes=56 * 2**20),
        cost_estimate=pl.CostEstimate(
            flops=10 * n * n * 4 * HD, bytes_accessed=20 * 2**20, transcendentals=n * n
        ),
    )(qkv, tab, qaT, sub, oTf, doT)


def mirror(tables):
    hole = jnp.zeros((2, 1, HD), tables.dtype)
    return jnp.concatenate([tables[:, GRID - 1 :: -1], hole, tables[:, : GRID - 1 : -1]], axis=1)


def unmirror(grads):
    return jnp.concatenate([grads[:, GRID - 1 :: -1], grads[:, : GRID : -1]], axis=1)


def swap(block, bit, size):
    return lax.ppermute(block, "seq", [(i, i ^ bit) for i in range(size)])


def spread(vector, size):
    return lax.all_to_all(
        jnp.broadcast_to(vector[None], (size,) + vector.shape), AXES, 0, 0, tiled=True
    )


def reduce_pieces(pieces):
    size, n = pieces.shape
    padded = jnp.pad(pieces, ((0, 0), (0, 1024 - n))).reshape(size, 8, 128)
    got = lax.all_to_all(padded, AXES, 0, 0, tiled=True)
    return jnp.sum(got, axis=0).reshape(1024)[:n]


def norm_parts(values):
    center = jnp.mean(values, axis=-1, keepdims=True)
    centered = values - center
    rate = lax.rsqrt(jnp.mean(centered * centered, axis=-1, keepdims=True) + EPS)
    return centered * rate, rate


def norm_back(grad, hat, rate, gain):
    u = grad * gain
    return rate * (
        u
        - jnp.mean(u, axis=-1, keepdims=True)
        - hat * jnp.mean(u * hat, axis=-1, keepdims=True)
    )


def body_heads(
    tokens,
    w_qkv,
    qv_bias,
    w_proj,
    proj_bias,
    w_fc1,
    fc1_bias,
    w_fc2,
    fc2_bias,
    norm_gains,
    norm_biases,
    rel_tables,
    cotangent,
):
    images, rows_img, features = tokens.shape
    dps, seqs = lax.axis_size("dp"), lax.axis_size("seq")
    size = dps * seqs
    slots = seqs // images
    per = HEADS // slots
    part = features // size
    wide = per * 3 * HD
    hidden = fc1_bias.shape[0] * size
    blocks = hidden // features
    here = lax.axis_index("seq")
    image, slot = here // slots, here % slots
    rows = images * rows_img

    own = lax.dynamic_index_in_dim(tokens, image, 0, keepdims=False)
    other = lax.dynamic_index_in_dim(tokens, 1 - image, 0, keepdims=False)
    got = swap(other, 4, seqs)
    near = [own, swap(own, 2, seqs), got, swap(got, 2, seqs)]
    far = [swap(block, 1, seqs) for block in near]
    by_mask = jnp.stack([near[0], far[0], near[1], far[1], near[2], far[2], near[3], far[3]])
    image_tokens = jnp.concatenate(
        [lax.dynamic_index_in_dim(by_mask, j ^ here, 0, keepdims=True) for j in range(seqs)]
    )

    small = jnp.concatenate(
        [
            qv_bias,
            proj_bias,
            fc1_bias,
            fc2_bias,
            norm_gains.reshape(-1),
            norm_biases.reshape(-1),
        ]
    )
    lengths = [2 * part, part, blocks * part, part, 2 * part, 2 * part]
    small = jnp.pad(small, (0, 1024 - small.shape[0])).reshape(8, 128)
    smalls = spread(small, size).reshape(size, 1024)
    edges = [sum(lengths[:j]) for j in range(len(lengths) + 1)]
    cut = [smalls[:, a:b].astype(F32) for a, b in zip(edges[:-1], edges[1:])]
    bqv, bp, b2 = cut[0].reshape(-1), cut[1].reshape(-1), cut[3].reshape(-1)
    b1 = cut[2].reshape(size, blocks, part).transpose(1, 0, 2).reshape(-1)
    gains = cut[4].reshape(size, 2, part).transpose(1, 0, 2).reshape(2, features)
    shifts = cut[5].reshape(size, 2, part).transpose(1, 0, 2).reshape(2, features)

    by_head = w_qkv.reshape(part, 3, slots, per, HD)
    to_slots = by_head.transpose(2, 0, 3, 1, 4).reshape(slots, part, wide)
    cols = lax.all_to_all(
        jnp.concatenate([to_slots] * images, axis=0), "seq", 0, 0, tiled=True
    ).reshape(seqs * part, wide)
    w_cols = lax.all_gather(cols, "dp", axis=0, tiled=True)

    w1_local = w_fc1.reshape(part, size, blocks, part).transpose(0, 2, 1, 3).reshape(part, hidden)
    w2_local = w_fc2.reshape(blocks, part, features).transpose(1, 0, 2).reshape(part, hidden)
    wq_local = by_head.transpose(0, 3, 2, 1, 4).reshape(part, 3 * features)
    whole = lax.all_gather(
        jnp.concatenate([w1_local, w2_local, w_proj, wq_local], axis=1), AXES, axis=0, tiled=True
    )
    w1 = whole[:, :hidden]
    w2 = (
        whole[:, hidden : 2 * hidden]
        .reshape(features, blocks, features)
        .transpose(1, 0, 2)
        .reshape(hidden, features)
    )
    wp = whole[:, 2 * hidden : 2 * hidden + features]
    wq = whole[:, 2 * hidden + features :]

    length = seqs * rows_img
    hat_all, _ = norm_parts(image_tokens.reshape(length, features).astype(F32))
    normed_all = (hat_all * gains[0] + shifts[0]).astype(BF)
    full_bias = jnp.stack(
        [
            bqv[:features].reshape(slots, per, HD),
            jnp.zeros((slots, per, HD), F32),
            bqv[features:].reshape(slots, per, HD),
        ],
        axis=2,
    ).reshape(slots, wide)
    own_bias = lax.dynamic_index_in_dim(full_bias, slot, 0, keepdims=False)
    qkv = (dot(normed_all, w_cols, NN) + own_bias).astype(BF)

    tab = mirror(rel_tables)
    kept, arrived = [], []
    for p in range(per):
        qkv_p = qkv[:, p * 3 * HD : (p + 1) * 3 * HD]
        out, *saved = heads_forward(qkv_p, tab)
        kept.append([qkv_p, tab, saved[1], saved[2], saved[0]])
        back = lax.all_to_all(out, "seq", 0, 0, tiled=True)
        arrived.append(back.reshape(images, slots, 1, HD, rows_img))
    attendedT = jnp.concatenate(arrived, axis=2).reshape(images, features, rows_img)

    inputs = tokens.astype(F32)
    mixed = inputs + jnp.einsum("yht,hc->ytc", attendedT, wp, preferred_element_type=F32) + bp
    mixed = mixed.reshape(rows, features)
    hat2, rate2 = norm_parts(mixed)
    normed2 = (hat2 * gains[1] + shifts[1]).astype(BF)
    pre = dot(normed2, w1, NN) + b1
    cdf = 0.5 * (1.0 + lax.erf(pre * 0.5**0.5))
    activated = (pre * cdf).astype(BF)
    slope = cdf + pre * jnp.exp(-0.5 * pre * pre) * (2.0 * math.pi) ** -0.5
    result = (mixed + dot(activated, w2, NN) + b2).astype(BF).reshape(tokens.shape)

    grad_out = cotangent.reshape(rows, features)
    grad_out_f = grad_out.astype(F32)
    grad_pre = (dot(grad_out, w2, NT) * slope).astype(BF)
    grad_norm2 = dot(grad_pre, w1, NT)
    grad_mixed = grad_out_f + norm_back(grad_norm2, hat2, rate2, gains[1])
    grad_branch = grad_mixed.astype(BF)
    grad_attT = jnp.einsum(
        "hc,ytc->yht",
        wp,
        grad_branch.reshape(images, rows_img, features),
        preferred_element_type=F32,
    ).astype(BF)
    grad_attT = grad_attT.reshape(images * slots, per, HD, rows_img)
    grad_w2 = dot(activated, grad_out, TN).astype(BF)
    grad_w2 = (
        grad_w2.reshape(blocks, features, features).transpose(1, 0, 2).reshape(features, hidden)
    )
    grad_w1 = dot(normed2, grad_pre, TN).astype(BF)
    grad_wp = jnp.einsum(
        "yht,ytc->hc",
        attendedT,
        grad_branch.reshape(images, rows_img, features),
        preferred_element_type=F32,
    ).astype(BF)
    summed = lax.psum_scatter(
        jnp.concatenate([grad_w1, grad_w2, grad_wp], axis=1), AXES, scatter_dimension=0, tiled=True
    ).astype(F32)
    w_fc1_grad = (
        summed[:, :hidden].reshape(part, blocks, size, part).transpose(0, 2, 1, 3)
    ).reshape(part, hidden)
    w_fc2_grad = (
        summed[:, hidden : 2 * hidden].reshape(part, blocks, features).transpose(1, 0, 2)
    ).reshape(blocks * part, features)
    w_proj_grad = summed[:, 2 * hidden :]
    grad_b1 = jnp.sum(grad_pre, axis=0, dtype=F32)
    grad_b1 = grad_b1.reshape(blocks, size, part).transpose(1, 0, 2).reshape(size, blocks * part)
    bundle = jnp.concatenate(
        [
            jnp.sum(grad_branch, axis=0, dtype=F32).reshape(size, part),
            grad_b1,
            jnp.sum(grad_out_f, axis=0).reshape(size, part),
            jnp.sum(grad_norm2 * hat2, axis=0).reshape(size, part),
            jnp.sum(grad_norm2, axis=0).reshape(size, part),
        ],
        axis=1,
    )
    bundle = reduce_pieces(bundle)
    proj_bias_grad = bundle[:part]
    fc1_bias_grad = bundle[part : (1 + blocks) * part]
    fc2_bias_grad = bundle[(1 + blocks) * part : (2 + blocks) * part]
    gain1_grad = bundle[(2 + blocks) * part : (3 + blocks) * part]
    shift1_grad = bundle[(3 + blocks) * part : (4 + blocks) * part]

    grad_norm1 = jnp.zeros((images, rows_img, features), F32)
    table_sum = jnp.zeros((2, HD, 2 * GRID), F32)
    weight_grads, bias_sums = [], []
    for p in range(per):
        do_p = lax.all_to_all(grad_attT[:, p], "seq", 0, 0, tiled=True)
        dqkv, dtab = heads_backward(*kept[p], do_p)
        table_sum = table_sum + dtab
        sent = lax.all_to_all(dqkv, "seq", 0, 0, tiled=True)
        sent = sent.reshape(images, slots * 3 * HD, rows_img)
        own_cols = wq[:, p * slots * 3 * HD : (p + 1) * slots * 3 * HD]
        grad_norm1 = grad_norm1 + jnp.einsum(
            "yht,ch->ytc", sent, own_cols, preferred_element_type=F32
        )
        bias_sums.append(
            jnp.sum(sent, axis=(0, 2), dtype=F32).reshape(slots, 3, HD)
        )
        grad_w = jnp.einsum(
            "sct,sjt->cj",
            normed_all.reshape(seqs, rows_img, features).swapaxes(1, 2),
            dqkv,
            preferred_element_type=F32,
        )
        grad_w = grad_w.reshape(dps, seqs, part, 3 * HD).swapaxes(0, 1)
        grad_w = lax.all_to_all(grad_w, "seq", 0, 0, tiled=True)
        grad_w = jnp.sum(grad_w.reshape(images, slots, dps, part, 3 * HD), axis=0).swapaxes(0, 1)
        grad_w = lax.all_to_all(grad_w, "dp", 0, 0, tiled=True)
        weight_grads.append(jnp.sum(grad_w, axis=0).reshape(slots, part, 3, HD))
    w_qkv_grad = jnp.stack(weight_grads, axis=1).transpose(2, 3, 0, 1, 4).reshape(part, 3 * features)

    hat1, rate1 = norm_parts(inputs)
    tokens_grad = grad_mixed.reshape(tokens.shape) + norm_back(grad_norm1, hat1, rate1, gains[0])
    tokens_grad = tokens_grad.astype(BF)
    bias_sum = jnp.stack(bias_sums, axis=1)
    bundle = jnp.concatenate(
        [
            jnp.concatenate([bias_sum[:, :, 0].reshape(-1), bias_sum[:, :, 2].reshape(-1)]).reshape(
                size, 2 * part
            ),
            jnp.sum(grad_norm1 * hat1, axis=(0, 1)).reshape(size, part),
            jnp.sum(grad_norm1, axis=(0, 1)).reshape(size, part),
        ],
        axis=1,
    )
    bundle = reduce_pieces(bundle)
    qv_bias_grad = bundle[: 2 * part]
    norm_gains_grad = jnp.stack([bundle[2 * part : 3 * part], gain1_grad])
    norm_biases_grad = jnp.stack([bundle[3 * part : 4 * part], shift1_grad])

    chunk = 2 * HD * 2 * GRID // size
    mine = reduce_pieces(table_sum.reshape(size, chunk))
    shared = spread(jnp.pad(mine, (0, 1024 - chunk)).reshape(8, 128), size)
    table_all = shared.reshape(size, 1024)[:, :chunk].reshape(2, HD, 2 * GRID)
    rel_tables_grad = unmirror(table_all.swapaxes(1, 2))
    return (
        result,
        tokens_grad,
        w_qkv_grad,
        qv_bias_grad,
        w_proj_grad,
        proj_bias_grad,
        w_fc1_grad,
        fc1_bias_grad,
        w_fc2_grad,
        fc2_bias_grad,
        norm_gains_grad,
        norm_biases_grad,
        rel_tables_grad,
    )


def layer_norm(values, gain, shift):
    center = jnp.mean(values, axis=-1, keepdims=True)
    centered = values - center
    spread = jnp.mean(centered * centered, axis=-1, keepdims=True)
    return centered * lax.rsqrt(spread + EPS) * gain + shift


def fetch_each(weights):
    return (
        lax.all_gather(weights[0], ("dp", "seq"), axis=0, tiled=True),
        lax.all_gather(weights[1], ("dp", "seq"), axis=0, tiled=True),
        lax.all_gather(weights[2], ("dp", "seq"), axis=0, tiled=True),
        lax.all_gather(weights[3], ("dp", "seq"), axis=0, tiled=True),
        lax.all_gather(weights[4], ("dp", "seq"), axis=0, tiled=True),
        lax.all_gather(weights[5], ("dp", "seq"), axis=0, tiled=True),
        lax.all_gather(weights[6], ("dp", "seq"), axis=0, tiled=True),
        lax.all_gather(weights[7], ("dp", "seq"), axis=0, tiled=True),
        lax.all_gather(weights[8], ("dp", "seq"), axis=1, tiled=True),
        lax.all_gather(weights[9], ("dp", "seq"), axis=1, tiled=True),
    )


def position_rows(tables, rows_img):
    beginning = lax.axis_index("seq") * rows_img
    tokens_at = beginning + jnp.arange(rows_img, dtype=jnp.int32)
    offsets = jnp.arange(GRID, dtype=jnp.int32)
    entries = jnp.arange(TABLE, dtype=jnp.int32)
    row_index = tokens_at[:, None] // GRID - offsets[None, :] + GRID - 1
    col_index = tokens_at[:, None] % GRID - offsets[None, :] + GRID - 1
    row_hot = (row_index[:, :, None] == entries[None, None, :]).astype(jnp.float32)
    col_hot = (col_index[:, :, None] == entries[None, None, :]).astype(jnp.float32)
    tables_f = tables.astype(jnp.float32)
    rel_rows = jnp.einsum("rkt,tc->rkc", row_hot, tables_f[0], precision=HIGH)
    rel_cols = jnp.einsum("rkt,tc->rkc", col_hot, tables_f[1], precision=HIGH)
    return (row_hot, col_hot, rel_rows, rel_cols)


def score_block(queries, keys_all, rows_low, cols_low):
    rows_img = queries.shape[0]
    product = jnp.einsum(
        "rhc,nhc->hrn", queries, keys_all, preferred_element_type=jnp.float32
    ) * HD ** (-0.5)
    bias_rows = jnp.einsum("rhc,rkc->hrk", queries, rows_low, preferred_element_type=jnp.float32)
    bias_cols = jnp.einsum("rhc,rkc->hrk", queries, cols_low, preferred_element_type=jnp.float32)
    joined = (
        product.reshape(HEADS, rows_img, GRID, GRID)
        + bias_rows[:, :, :, None]
        + bias_cols[:, :, None, :]
    )
    return joined.reshape(HEADS, rows_img, GRID * GRID)


def attend_forward(qkv_img, kv_pair, rows_low, cols_low):
    rows_img, triple = qkv_img.shape
    features = triple // 3
    queries = qkv_img[:, :features].reshape(rows_img, HEADS, HD)
    keys_all = kv_pair[0].reshape(-1, HEADS, HD)
    values_all = kv_pair[1].reshape(-1, HEADS, HD)
    scores = score_block(queries, keys_all, rows_low, cols_low)
    largest = jnp.max(scores, axis=-1, keepdims=True)
    shifted = jnp.exp(scores - largest)
    totals = jnp.sum(shifted, axis=-1, keepdims=True)
    probs_low = (shifted / totals).astype(jnp.bfloat16)
    attended = jnp.einsum("hrn,nhc->rhc", probs_low, values_all, preferred_element_type=jnp.float32)
    log_totals = largest[..., 0] + jnp.log(totals[..., 0])
    return (attended.reshape(rows_img, features).astype(jnp.bfloat16), log_totals)


def attend_backward(qkv_img, log_totals, grad_att, kv_pair, rel_rows, rel_cols, rows_low, cols_low):
    rows_img, triple = qkv_img.shape
    features = triple // 3
    scale = HD ** (-0.5)
    queries = qkv_img[:, :features].reshape(rows_img, HEADS, HD)
    keys_all = kv_pair[0].reshape(-1, HEADS, HD)
    values_all = kv_pair[1].reshape(-1, HEADS, HD)
    scores = score_block(queries, keys_all, rows_low, cols_low)
    probs = jnp.exp(scores - log_totals[..., None])
    probs_low = probs.astype(jnp.bfloat16)
    grad_heads = grad_att.reshape(rows_img, HEADS, HD)
    grad_probs = jnp.einsum(
        "rhc,nhc->hrn", grad_heads, values_all, preferred_element_type=jnp.float32
    )
    inner_sum = jnp.sum(probs * grad_probs, axis=-1, keepdims=True)
    grad_scores = (probs * (grad_probs - inner_sum)).astype(jnp.bfloat16)
    grad_queries = (
        jnp.einsum("hrn,nhc->rhc", grad_scores, keys_all, preferred_element_type=jnp.float32)
        * scale
    )
    grid_scores = grad_scores.reshape(HEADS, rows_img, GRID, GRID)
    grad_rows = jnp.sum(grid_scores, axis=3, dtype=jnp.float32)
    grad_cols = jnp.sum(grid_scores, axis=2, dtype=jnp.float32)
    grad_queries = grad_queries + jnp.einsum("hrk,rkc->rhc", grad_rows, rel_rows, precision=HIGH)
    grad_queries = grad_queries + jnp.einsum("hrk,rkc->rhc", grad_cols, rel_cols, precision=HIGH)
    query_f = queries.astype(jnp.float32)
    table_rows = jnp.einsum("hrk,rhc->rkc", grad_rows, query_f, precision=HIGH)
    table_cols = jnp.einsum("hrk,rhc->rkc", grad_cols, query_f, precision=HIGH)
    length = lax.axis_size("seq") * rows_img
    grad_keys = (
        jnp.einsum("hrn,rhc->nhc", grad_scores, queries, preferred_element_type=jnp.float32) * scale
    )
    grad_values = jnp.einsum(
        "hrn,rhc->nhc", probs_low, grad_heads, preferred_element_type=jnp.float32
    )
    key_grads = lax.psum_scatter(
        jnp.concatenate(
            [grad_keys.reshape(length, features), grad_values.reshape(length, features)], axis=1
        ),
        "seq",
        scatter_dimension=0,
        tiled=True,
    )
    grad_qkv = jnp.concatenate(
        [grad_queries.reshape(rows_img, features), key_grads], axis=1
    ).astype(jnp.bfloat16)
    return (grad_qkv, table_rows, table_cols)


def body(
    tokens,
    w_qkv,
    qv_bias,
    w_proj,
    proj_bias,
    w_fc1,
    fc1_bias,
    w_fc2,
    fc2_bias,
    norm_gains,
    norm_biases,
    rel_tables,
    cotangent,
):
    images, rows_img, features = tokens.shape
    per_batch = images // MB
    weights = (
        w_qkv,
        qv_bias,
        w_proj,
        proj_bias,
        w_fc1,
        fc1_bias,
        w_fc2,
        fc2_bias,
        norm_gains,
        norm_biases,
    )
    row_hot, col_hot, rel_rows, rel_cols = position_rows(rel_tables, rows_img)
    rows_low = rel_rows.astype(jnp.bfloat16)
    cols_low = rel_cols.astype(jnp.bfloat16)
    stored = []
    outputs = []
    for batch_index in range(MB):
        gathered = fetch_each(weights)
        (
            wq_full,
            bqv_full,
            wp_full,
            bp_full,
            w1_full,
            b1_full,
            w2_full,
            b2_full,
            gains_full,
            shifts_full,
        ) = gathered
        gains_f = gains_full.astype(jnp.float32)
        shifts_f = shifts_full.astype(jnp.float32)
        inputs = (
            tokens[batch_index * per_batch : (batch_index + 1) * per_batch]
            .astype(jnp.float32)
            .reshape(-1, features)
        )
        normed1 = layer_norm(inputs, gains_f[0], shifts_f[0]).astype(jnp.bfloat16)
        full_bias = jnp.concatenate(
            [bqv_full[:features], jnp.zeros((features,), bqv_full.dtype), bqv_full[features:]]
        ).astype(jnp.float32)
        qkv = (jnp.dot(normed1, wq_full, preferred_element_type=jnp.float32) + full_bias).astype(
            jnp.bfloat16
        )
        qkv_images = qkv.reshape(per_batch, rows_img, 3 * features)

        def forward_image(carried, qkv_img):
            kv_pair = (
                lax.all_gather(qkv_img[:, features : 2 * features], "seq", axis=0, tiled=True),
                lax.all_gather(qkv_img[:, 2 * features :], "seq", axis=0, tiled=True),
            )
            attended_img, log_totals = attend_forward(qkv_img, kv_pair, rows_low, cols_low)
            return (carried, (attended_img, log_totals))

        results = lax.scan(forward_image, jnp.zeros((), jnp.float32), qkv_images)[1]
        attended = results[0].reshape(-1, features)
        mixed = (
            inputs
            + jnp.dot(attended, wp_full, preferred_element_type=jnp.float32)
            + bp_full.astype(jnp.float32)
        )
        normed2 = layer_norm(mixed, gains_f[1], shifts_f[1]).astype(jnp.bfloat16)
        pre = jnp.dot(normed2, w1_full, preferred_element_type=jnp.float32) + b1_full.astype(
            jnp.float32
        )
        activated = jax.nn.gelu(pre, approximate=False).astype(jnp.bfloat16)
        block_out = (
            mixed
            + jnp.dot(activated, w2_full, preferred_element_type=jnp.float32)
            + b2_full.astype(jnp.float32)
        )
        outputs.append(block_out.astype(jnp.bfloat16).reshape(per_batch, rows_img, features))
        stored.append((normed1, qkv_images, results, mixed, normed2, pre, activated))
    gradients = [jnp.zeros(array.shape, jnp.float32) for array in gathered]
    table_rows_sum = jnp.zeros((rows_img, GRID, HD), jnp.float32)
    table_cols_sum = jnp.zeros((rows_img, GRID, HD), jnp.float32)
    input_grads = []
    for batch_index in range(MB):
        gathered = fetch_each(weights)
        (
            wq_full,
            bqv_full,
            wp_full,
            bp_full,
            w1_full,
            b1_full,
            w2_full,
            b2_full,
            gains_full,
            shifts_full,
        ) = gathered
        gains_f = gains_full.astype(jnp.float32)
        shifts_f = shifts_full.astype(jnp.float32)
        normed1, qkv_images, results, mixed, normed2, pre, activated = stored[batch_index]
        inputs = (
            tokens[batch_index * per_batch : (batch_index + 1) * per_batch]
            .astype(jnp.float32)
            .reshape(-1, features)
        )
        grad_out = cotangent[batch_index * per_batch : (batch_index + 1) * per_batch].reshape(
            -1, features
        )
        grad_out_f = grad_out.astype(jnp.float32)
        grad_w2 = jnp.dot(activated.T, grad_out, preferred_element_type=jnp.float32)
        grad_b2 = jnp.sum(grad_out_f, axis=0)
        grad_act = jnp.dot(grad_out, w2_full.T, preferred_element_type=jnp.float32)
        _, gelu_pull = jax.vjp(partial(jax.nn.gelu, approximate=False), pre)
        grad_pre = gelu_pull(grad_act)[0].astype(jnp.bfloat16)
        grad_w1 = jnp.dot(normed2.T, grad_pre, preferred_element_type=jnp.float32)
        grad_b1 = jnp.sum(grad_pre, axis=0, dtype=jnp.float32)
        grad_norm2 = jnp.dot(grad_pre, w1_full.T, preferred_element_type=jnp.float32)
        _, norm_pull2 = jax.vjp(layer_norm, mixed, gains_f[1], shifts_f[1])
        grad_mix_norm, grad_gain2, grad_shift2 = norm_pull2(grad_norm2)
        grad_mixed = grad_out_f + grad_mix_norm
        grad_branch = grad_mixed.astype(jnp.bfloat16)
        attended = results[0].reshape(-1, features)
        grad_wp = jnp.dot(attended.T, grad_branch, preferred_element_type=jnp.float32)
        grad_bp = jnp.sum(grad_branch, axis=0, dtype=jnp.float32)
        grad_att = jnp.dot(grad_branch, wp_full.T, preferred_element_type=jnp.float32).astype(
            jnp.bfloat16
        )
        grad_images = grad_att.reshape(per_batch, rows_img, features)
        image_inputs = (qkv_images, results[1], grad_images)

        def backward_image(carried, pieces):
            kv_pair = (
                lax.all_gather(pieces[0][:, features : 2 * features], "seq", axis=0, tiled=True),
                lax.all_gather(pieces[0][:, 2 * features :], "seq", axis=0, tiled=True),
            )
            grad_qkv_img, table_rows, table_cols = attend_backward(
                pieces[0], pieces[1], pieces[2], kv_pair, rel_rows, rel_cols, rows_low, cols_low
            )
            return ((carried[0] + table_rows, carried[1] + table_cols), grad_qkv_img)

        (table_rows_sum, table_cols_sum), grad_qkv_all = lax.scan(
            backward_image, (table_rows_sum, table_cols_sum), image_inputs
        )
        grad_qkv = grad_qkv_all.reshape(-1, 3 * features)
        grad_wq = jnp.dot(normed1.T, grad_qkv, preferred_element_type=jnp.float32)
        grad_bqv = jnp.concatenate(
            [
                jnp.sum(grad_qkv[:, :features], axis=0, dtype=jnp.float32),
                jnp.sum(grad_qkv[:, 2 * features :], axis=0, dtype=jnp.float32),
            ]
        )
        grad_norm1 = jnp.dot(grad_qkv, wq_full.T, preferred_element_type=jnp.float32)
        _, norm_pull1 = jax.vjp(layer_norm, inputs, gains_f[0], shifts_f[0])
        grad_in_norm, grad_gain1, grad_shift1 = norm_pull1(grad_norm1)
        input_grads.append(
            (grad_mixed + grad_in_norm).astype(jnp.bfloat16).reshape(per_batch, rows_img, features)
        )
        updates = (
            grad_wq,
            grad_bqv,
            grad_wp,
            grad_bp,
            grad_w1,
            grad_b1,
            grad_w2,
            grad_b2,
            jnp.stack([grad_gain1, grad_gain2]),
            jnp.stack([grad_shift1, grad_shift2]),
        )
        gradients = [before + update for before, update in zip(gradients, updates)]
    summed = (
        lax.psum_scatter(gradients[0], ("dp", "seq"), scatter_dimension=0, tiled=True),
        lax.psum_scatter(gradients[1], ("dp", "seq"), scatter_dimension=0, tiled=True),
        lax.psum_scatter(gradients[2], ("dp", "seq"), scatter_dimension=0, tiled=True),
        lax.psum_scatter(gradients[3], ("dp", "seq"), scatter_dimension=0, tiled=True),
        lax.psum_scatter(gradients[4], ("dp", "seq"), scatter_dimension=0, tiled=True),
        lax.psum_scatter(gradients[5], ("dp", "seq"), scatter_dimension=0, tiled=True),
        lax.psum_scatter(gradients[6], ("dp", "seq"), scatter_dimension=0, tiled=True),
        lax.psum_scatter(gradients[7], ("dp", "seq"), scatter_dimension=0, tiled=True),
        lax.psum_scatter(gradients[8], ("dp", "seq"), scatter_dimension=1, tiled=True),
        lax.psum_scatter(gradients[9], ("dp", "seq"), scatter_dimension=1, tiled=True),
    )
    table_local = jnp.stack(
        [
            jnp.einsum("rkt,rkc->tc", row_hot, table_rows_sum, precision=HIGH),
            jnp.einsum("rkt,rkc->tc", col_hot, table_cols_sum, precision=HIGH),
        ]
    )
    table_grad = lax.psum(table_local, ("dp", "seq"))
    return (
        jnp.concatenate(outputs, axis=0),
        jnp.concatenate(input_grads, axis=0),
        summed[0],
        summed[1],
        summed[2],
        summed[3],
        summed[4],
        summed[5],
        summed[6],
        summed[7],
        summed[8],
        summed[9],
        table_grad,
    )


def solution(mesh):
    placed = (
        P("dp", "seq", None),
        P(("dp", "seq"), None),
        P(("dp", "seq")),
        P(("dp", "seq"), None),
        P(("dp", "seq")),
        P(("dp", "seq"), None),
        P(("dp", "seq")),
        P(("dp", "seq"), None),
        P(("dp", "seq")),
        P(None, ("dp", "seq")),
        P(None, ("dp", "seq")),
        P(),
        P("dp", "seq", None),
    )
    seqs, images = mesh.shape["seq"], IMAGES // mesh.shape["dp"]
    by_heads = seqs == 8 and images == 2
    return jax.shard_map(
        body_heads if by_heads else body,
        mesh=mesh,
        in_specs=placed,
        out_specs=(
            P("dp", "seq", None),
            P("dp", "seq", None),
            P(("dp", "seq"), None),
            P(("dp", "seq")),
            P(("dp", "seq"), None),
            P(("dp", "seq")),
            P(("dp", "seq"), None),
            P(("dp", "seq")),
            P(("dp", "seq"), None),
            P(("dp", "seq")),
            P(None, ("dp", "seq")),
            P(None, ("dp", "seq")),
            P(),
        ),
        check_vma=False,
    )
```

```python
from functools import partial
import math

import jax
import jax.numpy as jnp
from jax import lax
from jax.experimental import pallas as pl
from jax.experimental.pallas import tpu as pltpu
from jax.sharding import PartitionSpec as P

HEADS = 12
HD = 64
GRID = 64
MB = 2
TABLE = 127


EPS = 1e-06
HIGH = lax.Precision.HIGHEST
IMAGES = 8
AXES = ("dp", "seq")

TB = 512
CK = 512
ROWS = CK // GRID
LOG2E = 1.4426950408889634
NN = (((1,), (0,)), ((), ()))
NT = (((1,), (1,)), ((), ()))
TN = (((0,), (0,)), ((), ()))
BF = jnp.bfloat16
F32 = jnp.float32


def dot(a, b, dims):
    return lax.dot_general(a, b, dims, preferred_element_type=F32)


def col_hot(n):
    key = lax.broadcasted_iota(jnp.int32, (n, GRID), 0) & (GRID - 1)
    col = lax.broadcasted_iota(jnp.int32, (n, GRID), 1)
    return (key == col).astype(F32)


def build_keys(qkv_ref, kaug, start, n):
    rows = pl.ds(start, n)
    k = qkv_ref[rows, HD : 2 * HD].astype(F32)
    pair = jnp.concatenate([k, col_hot(n)], axis=1).astype(BF)
    kaug[rows, : 2 * HD] = pair
    kaug[rows, 2 * HD :] = pair


def fwd_kernel(n_chunks, qkv_ref, tab_ref, oT_ref, oTf_ref, qaT_ref, sub_ref, kaug, vta):
    i = pl.program_id(0)
    tg = TB // GRID

    @pl.when(i == 0)
    def _():
        for c in range(n_chunks):
            build_keys(qkv_ref, kaug, c * CK, CK)
            rows = pl.ds(c * CK, CK)
            vT = qkv_ref[rows, 2 * HD :].astype(F32).T
            vta[0:HD, rows] = vT.astype(BF)
            one = lax.broadcasted_iota(jnp.int32, (16, CK), 0) == 0
            vta[HD : HD + 16, rows] = one.astype(F32).astype(BF)

    q = qkv_ref[pl.ds(pl.multiple_of(i * TB, TB), TB), :HD]
    gr = dot(q, tab_ref[0], NT) * LOG2E
    gc = dot(q, tab_ref[1], NT) * LOG2E
    brs, bcs = [], []
    for g in range(tg):
        sl = slice(g * GRID, (g + 1) * GRID)
        brs.append(pltpu.roll(gr[sl], i * tg + g, 1))
        bcs.append(pltpu.roll(gc[sl], 0, 1, stride=1, stride_axis=0))
    br = jnp.concatenate(brs, axis=0)
    bc = jnp.concatenate(bcs, axis=0)
    qs = q.astype(F32) * (HD ** -0.5 * LOG2E)
    cat = jnp.concatenate([qs, bc[:, :GRID]], axis=1).T
    hi = cat.astype(BF)
    lo = (cat - hi.astype(F32)).astype(BF)
    qaT_ref[...] = jnp.concatenate([hi, lo], axis=0)
    sub_ref[...] = br.T[:GRID]
    qa = qaT_ref[...]

    m = jnp.full((1, TB), -jnp.inf, F32)
    acc = jnp.zeros((HD + 16, TB), F32)
    for c in range(n_chunks):
        s = dot(kaug[c * CK : (c + 1) * CK, :], qa, NN).reshape(ROWS, GRID, TB)
        b8 = sub_ref[c * ROWS : (c + 1) * ROWS, :]
        mc = jnp.max(jnp.max(s, axis=1) + b8, axis=0, keepdims=True)
        p = jnp.exp2(s - (mc - b8)[:, None, :]).astype(BF).reshape(CK, TB)
        o = dot(vta[:, c * CK : (c + 1) * CK], p, NN)
        new = jnp.maximum(m, mc)
        acc = acc * jnp.exp2(m - new) + o * jnp.exp2(mc - new)
        m = new
    total = acc[HD : HD + 1]
    out = acc[:HD] / total
    oT_ref[0] = out.astype(BF)
    oTf_ref[...] = out
    sub_ref[...] = (m + jnp.log2(total)) - sub_ref[...]


def heads_forward(qkv, tab):
    n = qkv.shape[0]
    steps = n // TB
    return pl.pallas_call(
        partial(fwd_kernel, n // CK),
        grid=(steps,),
        in_specs=[
            pl.BlockSpec((n, 3 * HD), lambda i: (0, 0)),
            pl.BlockSpec((2, 2 * GRID, HD), lambda i: (0, 0, 0)),
        ],
        out_specs=[
            pl.BlockSpec((1, HD, TB), lambda i: (i, 0, 0)),
            pl.BlockSpec((HD, TB), lambda i: (0, i)),
            pl.BlockSpec((4 * HD, TB), lambda i: (0, i)),
            pl.BlockSpec((GRID, TB), lambda i: (0, i)),
        ],
        out_shape=[
            jax.ShapeDtypeStruct((steps, HD, TB), BF),
            jax.ShapeDtypeStruct((HD, n), F32),
            jax.ShapeDtypeStruct((4 * HD, n), BF),
            jax.ShapeDtypeStruct((GRID, n), F32),
        ],
        scratch_shapes=[pltpu.VMEM((n, 4 * HD), BF), pltpu.VMEM((HD + 16, n), BF)],
        compiler_params=pltpu.CompilerParams(vmem_limit_bytes=56 * 2**20),
        cost_estimate=pl.CostEstimate(
            flops=4 * n * n * 4 * HD, bytes_accessed=16 * 2**20, transcendentals=n * n
        ),
    )(qkv, tab)


def bwd_kernel(
    n_chunks, cuts, qkv_ref, tab_ref, qaT_ref, sub_ref, oTf_ref, doT_ref, x_hbm,
    msg_ref, kaug, vaug, kta, dkv, dqa, dtab_ref, x_ref, x_sem
):
    i = pl.program_id(0)
    tg = TB // GRID
    n_steps = pl.num_programs(0)
    fetch = pltpu.make_async_copy(x_hbm, x_ref, x_sem)

    @pl.when(i == 0)
    def _():
        for c in range(n_chunks):
            build_keys(qkv_ref, kaug, c * CK, CK)
            rows = pl.ds(c * CK, CK)
            k = qkv_ref[rows, HD : 2 * HD].astype(F32)
            both = jnp.concatenate([k, col_hot(CK)], axis=1).T
            kta[0 : 2 * HD, rows] = both.astype(BF)
            key = lax.broadcasted_iota(jnp.int32, (16, CK), 1) >> 6
            hot = lax.broadcasted_iota(jnp.int32, (16, CK), 0) == key
            kta[2 * HD : 2 * HD + 16, rows] = hot.astype(F32).astype(BF)
            v = qkv_ref[rows, 2 * HD :].astype(F32)
            lane = lax.broadcasted_iota(jnp.int32, (CK, HD), 1)
            vaug[rows, :] = jnp.concatenate([v, (lane < 3).astype(F32)], axis=1).astype(BF)
            dkv[rows, :] = jnp.zeros((CK, 2 * HD), F32)
        dtab_ref[...] = jnp.zeros_like(dtab_ref)
        fetch.start()

    q = qkv_ref[pl.ds(pl.multiple_of(i * TB, TB), TB), :HD]
    doT = doT_ref[0].astype(F32)
    delta = -jnp.sum(doT * oTf_ref[...], axis=0, keepdims=True)
    d1 = delta.astype(BF)
    r1 = delta - d1.astype(F32)
    d2 = r1.astype(BF)
    d3 = (r1 - d2.astype(F32)).astype(BF)
    pad = jnp.concatenate(
        [d1.astype(F32), d2.astype(F32), d3.astype(F32), jnp.zeros((HD - 3, TB), F32)], axis=0
    )
    doa = jnp.concatenate([doT, pad], axis=0).astype(BF)
    do = jnp.concatenate([doT, jnp.zeros((HD, TB), F32)], axis=0).T
    qz = jnp.concatenate([jnp.zeros((TB, HD), F32), q.astype(F32)], axis=1)
    doq = jnp.concatenate([do, qz], axis=0).astype(BF)
    qa = qaT_ref[...]
    dqa[...] = jnp.zeros_like(dqa)

    for c in range(n_chunks):
        rows = slice(c * CK, (c + 1) * CK)
        s = dot(kaug[rows, :], qa, NN).reshape(ROWS, GRID, TB)
        b8 = sub_ref[c * ROWS : (c + 1) * ROWS, :]
        p = jnp.exp2(s - b8[:, None, :]).reshape(CK, TB)
        dp = dot(vaug[rows, :], doa, NN)
        ds = (p * dp).astype(BF)
        pd = jnp.concatenate([p.astype(BF), ds], axis=1)
        dkv[rows, :] += dot(pd, doq, NN)
        g = dot(kta[:, rows], ds, NN)
        dqa[0 : 2 * HD, :] += g[: 2 * HD]
        dqa[2 * HD + c * ROWS : 2 * HD + (c + 1) * ROWS, :] = g[2 * HD : 2 * HD + ROWS]

    grads = dqa[HD : 3 * HD, :].T
    lane = lax.broadcasted_iota(jnp.int32, (TB, 2 * GRID), 1)
    gcol = jnp.where(lane < GRID, grads, 0.0)
    grow = jnp.where(lane >= GRID, grads, 0.0)
    rs, cs = [], []
    col = lax.broadcasted_iota(jnp.int32, (GRID, 2 * GRID), 0)
    for g in range(tg):
        sl = slice(g * GRID, (g + 1) * GRID)
        rs.append(pltpu.roll(grow[sl], GRID - (i * tg + g), 1))
        x = gcol[sl]
        for bit in range(6):
            x = jnp.where((col >> bit) & 1 == 1, pltpu.roll(x, 2 * GRID - (1 << bit), 1), x)
        cs.append(x)
    drow = jnp.concatenate(rs, axis=0).astype(BF)
    dcol = jnp.concatenate(cs, axis=0).astype(BF)
    dq = dqa[:HD, :] * HD ** -0.5
    dq = dq + dot(tab_ref[0], drow, (((0,), (1,)), ((), ())))
    dq = dq + dot(tab_ref[1], dcol, (((0,), (1,)), ((), ())))
    msg_ref[i, 0:HD, :] = dq.astype(BF)
    dtab_ref[0:HD, :] += dot(q, drow, TN)
    dtab_ref[HD : 2 * HD, :] += dot(q, dcol, TN)

    @pl.when(i == n_steps - 1)
    def _():
        for c in range(n_chunks):
            both = dkv[c * CK : (c + 1) * CK, :].T
            msg_ref[c, HD : 2 * HD, :] = (both[HD:] * HD ** -0.5).astype(BF)
            msg_ref[c, 2 * HD : 3 * HD, :] = both[:HD].astype(BF)
        fetch.wait()
        all_grads = jnp.concatenate([msg_ref[c, : 3 * HD, :] for c in range(n_chunks)], axis=1)
        dw = dot(all_grads, x_ref[...], NN).T
        dps, seqs, part = cuts
        half = dps // 2
        for s in range(seqs):
            sides = []
            for side in range(2):
                tops = [(d * seqs + s) * part for d in range(side * half, (side + 1) * half)]
                sides.append(jnp.concatenate([dw[top : top + part] for top in tops], axis=0))
            sides.append(jnp.zeros((half * part, CK - 6 * HD), F32))
            base = 3 * HD + half * part
            msg_ref[s, 3 * HD : base, :] = jnp.concatenate(sides, axis=1).astype(BF)
            piece = dtab_ref[s * 16 : (s + 1) * 16, :]
            hi = piece.astype(BF).astype(F32)
            fill = jnp.zeros((16, CK - 4 * HD), F32)
            msg_ref[s, base : base + 16, :] = jnp.concatenate([hi, piece - hi, fill], axis=1).astype(BF)


def heads_backward(cuts, qkv, tab, qaT, sub, oTf, x, doT):
    n, features = x.shape
    steps = n // TB
    rows = 3 * HD + cuts[0] // 2 * cuts[2] + 16
    return pl.pallas_call(
        partial(bwd_kernel, n // CK, cuts),
        grid=(steps,),
        in_specs=[
            pl.BlockSpec((n, 3 * HD), lambda i: (0, 0)),
            pl.BlockSpec((2, 2 * GRID, HD), lambda i: (0, 0, 0)),
            pl.BlockSpec((4 * HD, TB), lambda i: (0, i)),
            pl.BlockSpec((GRID, TB), lambda i: (0, i)),
            pl.BlockSpec((HD, TB), lambda i: (0, i)),
            pl.BlockSpec((1, HD, TB), lambda i: (i, 0, 0)),
            pl.BlockSpec(memory_space=pl.ANY),
        ],
        out_specs=pl.BlockSpec((steps, rows, TB), lambda i: (0, 0, 0)),
        out_shape=jax.ShapeDtypeStruct((steps, rows, TB), BF),
        scratch_shapes=[
            pltpu.VMEM((n, 4 * HD), BF),
            pltpu.VMEM((n, 2 * HD), BF),
            pltpu.VMEM((2 * HD + 16, n), BF),
            pltpu.VMEM((n, 2 * HD), F32),
            pltpu.VMEM((3 * HD, TB), F32),
            pltpu.VMEM((2 * HD, 2 * GRID), F32),
            pltpu.VMEM((n, features), BF),
            pltpu.SemaphoreType.DMA,
        ],
        compiler_params=pltpu.CompilerParams(vmem_limit_bytes=56 * 2**20),
        cost_estimate=pl.CostEstimate(
            flops=10 * n * n * 4 * HD, bytes_accessed=20 * 2**20, transcendentals=n * n
        ),
    )(qkv, tab, qaT, sub, oTf, doT, x)


def qkv_kernel(per, here_ref, *refs):
    blocks, rest = refs[:8], refs[8:]
    w_ref, par_ref, bias_ref, x_ref = rest[:4]
    outs, held, sems = rest[4 : 4 + per], rest[4 + per], rest[5 + per]
    m = pl.program_id(0)
    copies = [
        pltpu.make_async_copy(blocks[j], held.at[j], sems.at[j]) for j in range(len(blocks))
    ]

    @pl.when(m == 0)
    def _():
        for copy in copies:
            copy.start()

    for j, copy in enumerate(copies):

        @pl.when(m == j)
        def _():
            copy.wait()

    v = held[m].astype(F32)
    v = v - jnp.mean(v, axis=-1, keepdims=True)
    v = v * lax.rsqrt(jnp.mean(v * v, axis=-1, keepdims=True) + EPS)
    x = (v * par_ref[0:1, :] + par_ref[1:2, :]).astype(BF)
    x_ref[...] = x
    qkv = dot(x, w_ref[...], NN) + bias_ref[...]
    for p in range(per):
        outs[p][...] = qkv[:, p * 3 * HD : (p + 1) * 3 * HD].astype(BF)


def normed_qkv(here, blocks, w_cols, params, bias):
    rows, features = blocks[0].shape
    wide = w_cols.shape[1]
    per, steps = wide // (3 * HD), len(blocks)
    return pl.pallas_call(
        partial(qkv_kernel, per),
        grid_spec=pltpu.PrefetchScalarGridSpec(
            num_scalar_prefetch=1,
            grid=(steps,),
            in_specs=[pl.BlockSpec(memory_space=pl.ANY)] * steps
            + [
                pl.BlockSpec((features, wide), lambda m, here: (0, 0)),
                pl.BlockSpec((2, features), lambda m, here: (0, 0)),
                pl.BlockSpec((1, wide), lambda m, here: (0, 0)),
            ],
            out_specs=[pl.BlockSpec((rows, features), lambda m, here: (m ^ here[0], 0))]
            + [pl.BlockSpec((rows, 3 * HD), lambda m, here: (m ^ here[0], 0))] * per,
            scratch_shapes=[
                pltpu.VMEM((steps, rows, features), BF),
                pltpu.SemaphoreType.DMA((steps,)),
            ],
        ),
        out_shape=[jax.ShapeDtypeStruct((steps * rows, features), BF)]
        + [jax.ShapeDtypeStruct((steps * rows, 3 * HD), BF)] * per,
        compiler_params=pltpu.CompilerParams(vmem_limit_bytes=56 * 2**20),
        cost_estimate=pl.CostEstimate(
            flops=2 * steps * rows * features * wide, bytes_accessed=24 * 2**20, transcendentals=0
        ),
    )(here.reshape(1).astype(jnp.int32), *blocks, w_cols, params, bias)


def mirror(tables):
    hole = jnp.zeros((2, 1, HD), tables.dtype)
    return jnp.concatenate([tables[:, GRID - 1 :: -1], hole, tables[:, : GRID - 1 : -1]], axis=1)


def unmirror(grads):
    return jnp.concatenate([grads[:, GRID - 1 :: -1], grads[:, : GRID : -1]], axis=1)


def swap(block, bit, size):
    return lax.ppermute(block, "seq", [(i, i ^ bit) for i in range(size)])


def norm_parts(values):
    center = jnp.mean(values, axis=-1, keepdims=True)
    centered = values - center
    rate = lax.rsqrt(jnp.mean(centered * centered, axis=-1, keepdims=True) + EPS)
    return centered * rate, rate


def norm_back(grad, hat, rate, gain):
    u = grad * gain
    return rate * (
        u
        - jnp.mean(u, axis=-1, keepdims=True)
        - hat * jnp.mean(u * hat, axis=-1, keepdims=True)
    )


def body_heads(
    tokens,
    w_qkv,
    qv_bias,
    w_proj,
    proj_bias,
    w_fc1,
    fc1_bias,
    w_fc2,
    fc2_bias,
    norm_gains,
    norm_biases,
    rel_tables,
    cotangent,
):
    images, rows_img, features = tokens.shape
    dps, seqs = lax.axis_size("dp"), lax.axis_size("seq")
    size = dps * seqs
    slots = seqs // images
    per = HEADS // slots
    part = features // size
    wide = per * 3 * HD
    hidden = fc1_bias.shape[0] * size
    blocks = hidden // features
    here = lax.axis_index("seq")
    image, slot = here // slots, here % slots
    rows = images * rows_img

    own = lax.dynamic_index_in_dim(tokens, image, 0, keepdims=False)
    other = lax.dynamic_index_in_dim(tokens, 1 - image, 0, keepdims=False)
    got = swap(other, 4, seqs)
    near = [own, swap(own, 2, seqs), got, swap(got, 2, seqs)]
    far = [swap(block, 1, seqs) for block in near]
    by_mask = [near[0], far[0], near[1], far[1], near[2], far[2], near[3], far[3]]

    small = jnp.concatenate(
        [
            qv_bias,
            proj_bias,
            fc1_bias,
            fc2_bias,
            norm_gains.reshape(-1),
            norm_biases.reshape(-1),
        ]
    )
    lengths = [2 * part, part, blocks * part, part, 2 * part, 2 * part]
    small = jnp.pad(small, (0, wide - small.shape[0])).reshape(1, 1, wide)
    by_head = w_qkv.reshape(part, 3, slots, per, HD)
    to_slots = by_head.transpose(2, 0, 3, 1, 4).reshape(slots, part, wide)
    to_slots = jnp.concatenate([to_slots, jnp.broadcast_to(small, (slots, 8, wide))], axis=1)
    cols = lax.all_to_all(jnp.tile(to_slots, (dps * images, 1, 1)), AXES, 0, 0, tiled=True)
    w_cols = cols[:, :part].reshape(features, wide)
    smalls = cols[:, part]
    edges = [sum(lengths[:j]) for j in range(len(lengths) + 1)]
    cut = [smalls[:, a:b].astype(F32) for a, b in zip(edges[:-1], edges[1:])]
    bqv, bp, b2 = cut[0].reshape(-1), cut[1].reshape(-1), cut[3].reshape(-1)
    b1 = cut[2].reshape(size, blocks, part).transpose(1, 0, 2).reshape(-1)
    gains = cut[4].reshape(size, 2, part).transpose(1, 0, 2).reshape(2, features)
    shifts = cut[5].reshape(size, 2, part).transpose(1, 0, 2).reshape(2, features)

    w1_local = w_fc1.reshape(part, size, blocks, part).transpose(0, 2, 1, 3).reshape(part, hidden)
    w2_local = w_fc2.reshape(blocks, part, features).transpose(1, 0, 2).reshape(part, hidden)
    wq_local = by_head.transpose(0, 3, 2, 1, 4).reshape(part, 3 * features)
    whole = lax.all_gather(
        jnp.concatenate([w1_local, w2_local, w_proj, wq_local], axis=1), AXES, axis=0, tiled=True
    )
    w1 = whole[:, :hidden]
    w2 = (
        whole[:, hidden : 2 * hidden]
        .reshape(features, blocks, features)
        .transpose(1, 0, 2)
        .reshape(hidden, features)
    )
    wp = whole[:, 2 * hidden : 2 * hidden + features]
    wq = whole[:, 2 * hidden + features :]

    full_bias = jnp.stack(
        [
            bqv[:features].reshape(slots, per, HD),
            jnp.zeros((slots, per, HD), F32),
            bqv[features:].reshape(slots, per, HD),
        ],
        axis=2,
    ).reshape(slots, wide)
    own_bias = lax.dynamic_index_in_dim(full_bias, slot, 0, keepdims=True)
    normed_all, *qkv = normed_qkv(
        here, by_mask, w_cols, jnp.stack([gains[0], shifts[0]]), own_bias
    )

    tab = mirror(rel_tables)
    kept, arrived = [], []
    for p in range(per):
        out, *saved = heads_forward(qkv[p], tab)
        kept.append([qkv[p], tab, saved[1], saved[2], saved[0], normed_all])
        back = lax.all_to_all(out, "seq", 0, 0, tiled=True)
        arrived.append(back.reshape(images, slots, 1, HD, rows_img))
    attendedT = jnp.concatenate(arrived, axis=2).reshape(images, features, rows_img)

    inputs = tokens.astype(F32)
    mixed = inputs + jnp.einsum("yht,hc->ytc", attendedT, wp, preferred_element_type=F32) + bp
    mixed = mixed.reshape(rows, features)
    hat2, rate2 = norm_parts(mixed)
    normed2 = (hat2 * gains[1] + shifts[1]).astype(BF)
    pre = dot(normed2, w1, NN) + b1
    cdf = 0.5 * (1.0 + lax.erf(pre * 0.5**0.5))
    activated = (pre * cdf).astype(BF)
    slope = cdf + pre * jnp.exp(-0.5 * pre * pre) * (2.0 * math.pi) ** -0.5
    result = (mixed + dot(activated, w2, NN) + b2).astype(BF).reshape(tokens.shape)

    grad_out = cotangent.reshape(rows, features)
    grad_out_f = grad_out.astype(F32)
    grad_pre = (dot(grad_out, w2, NT) * slope).astype(BF)
    grad_norm2 = dot(grad_pre, w1, NT)
    grad_mixed = grad_out_f + norm_back(grad_norm2, hat2, rate2, gains[1])
    grad_branch = grad_mixed.astype(BF)
    grad_attT = jnp.einsum(
        "hc,ytc->yht",
        wp,
        grad_branch.reshape(images, rows_img, features),
        preferred_element_type=F32,
    ).astype(BF)
    grad_attT = grad_attT.reshape(images * slots, per, HD, rows_img)
    grad_w2 = dot(activated, grad_out, TN).astype(BF)
    grad_w2 = (
        grad_w2.reshape(blocks, features, features).transpose(1, 0, 2).reshape(features, hidden)
    )
    grad_w1 = dot(normed2, grad_pre, TN).astype(BF)
    grad_wp = jnp.einsum(
        "yht,ytc->hc",
        attendedT,
        grad_branch.reshape(images, rows_img, features),
        preferred_element_type=F32,
    ).astype(BF)
    summed = lax.psum_scatter(
        jnp.concatenate([grad_w1, grad_w2, grad_wp], axis=1), AXES, scatter_dimension=0, tiled=True
    ).astype(F32)
    w_fc1_grad = (
        summed[:, :hidden].reshape(part, blocks, size, part).transpose(0, 2, 1, 3)
    ).reshape(part, hidden)
    w_fc2_grad = (
        summed[:, hidden : 2 * hidden].reshape(part, blocks, features).transpose(1, 0, 2)
    ).reshape(blocks * part, features)
    w_proj_grad = summed[:, 2 * hidden :]
    grad_b1 = jnp.sum(grad_pre, axis=0, dtype=F32)
    grad_b1 = grad_b1.reshape(blocks, size, part).transpose(1, 0, 2).reshape(size, blocks * part)
    early = jnp.concatenate(
        [
            jnp.sum(grad_branch, axis=0, dtype=F32).reshape(size, part),
            grad_b1,
            jnp.sum(grad_out_f, axis=0).reshape(size, part),
            jnp.sum(grad_norm2 * hat2, axis=0).reshape(size, part),
            jnp.sum(grad_norm2, axis=0).reshape(size, part),
        ],
        axis=1,
    )
    grad_norm1 = jnp.zeros((images, rows_img, features), F32)
    first = lax.all_to_all(grad_attT[:, 0], "seq", 0, 0, tiled=True)
    others = grad_attT[:, 1:].reshape(seqs, (per - 1) * HD, rows_img)
    others = lax.all_to_all(others, "seq", 0, 0, tiled=True)
    table = jnp.zeros((16, 2 * GRID), F32)
    weight_grads, bias_sums = [], []
    for p in range(per):
        do_p = first if p == 0 else others[:, (p - 1) * HD : p * HD]
        message = heads_backward((dps, seqs, part), *kept[p], do_p)
        message = lax.all_to_all(message, "seq", 0, 0, tiled=True)
        sent = message[:, : 3 * HD].reshape(images, slots * 3 * HD, rows_img)
        own_cols = wq[:, p * slots * 3 * HD : (p + 1) * slots * 3 * HD]
        grad_norm1 = grad_norm1 + jnp.einsum(
            "yht,ch->ytc", sent, own_cols, preferred_element_type=F32
        )
        bias_sums.append(jnp.sum(sent, axis=(0, 2), dtype=F32).reshape(slots, 3, HD))
        base = 3 * HD + dps // 2 * part
        grad_w = message[:, 3 * HD : base, : 6 * HD].astype(F32)
        grad_w = jnp.sum(grad_w.reshape(images, slots, dps // 2 * part, 6 * HD), axis=0)
        weight_grads.append(grad_w.astype(BF))
        pair = message[:, base:, : 4 * GRID].astype(F32)
        table = table + jnp.sum(pair[..., : 2 * GRID] + pair[..., 2 * GRID :], axis=0)
    grad_w = jnp.stack(weight_grads).reshape(per, slots, dps // 2, part, 2, 3 * HD)
    grad_w = grad_w.transpose(4, 2, 0, 1, 3, 5).reshape(dps, per * slots * part, 3 * HD)
    grad_w = lax.all_to_all(grad_w, "dp", 0, 0, tiled=True)
    grad_w = jnp.sum(grad_w, axis=0, dtype=F32).reshape(per, slots, part, 3, HD)
    w_qkv_grad = grad_w.transpose(2, 3, 1, 0, 4).reshape(part, 3 * features)

    hat1, rate1 = norm_parts(inputs)
    tokens_grad = grad_mixed.reshape(tokens.shape) + norm_back(grad_norm1, hat1, rate1, gains[0])
    tokens_grad = tokens_grad.astype(BF)
    bias_sum = jnp.stack(bias_sums, axis=1)
    pieces = jnp.concatenate(
        [
            early,
            jnp.concatenate([bias_sum[:, :, 0].reshape(-1), bias_sum[:, :, 2].reshape(-1)]).reshape(
                size, 2 * part
            ),
            jnp.sum(grad_norm1 * hat1, axis=(0, 1)).reshape(size, part),
            jnp.sum(grad_norm1, axis=(0, 1)).reshape(size, part),
        ],
        axis=1,
    )
    pieces = jnp.pad(pieces, ((0, 0), (0, 1024 - pieces.shape[1]))).reshape(size, 8, 128)
    last = jnp.concatenate([pieces, jnp.broadcast_to(table[None], (size, 16, 128))], axis=1)
    last = lax.all_to_all(last, AXES, 0, 0, tiled=True)
    bundle = jnp.sum(last[:, :8], axis=0).reshape(1024)
    table_all = jnp.sum(last[:, 8:].reshape(dps, seqs * 16, 128), axis=0)
    rel_tables_grad = unmirror(table_all.reshape(2, HD, 2 * GRID).swapaxes(1, 2))
    ends = [0, 1, 1 + blocks, 2 + blocks, 3 + blocks, 4 + blocks, 6 + blocks, 7 + blocks, 8 + blocks]
    ends = [part * end for end in ends]
    bundle = [bundle[a:b] for a, b in zip(ends[:-1], ends[1:])]
    proj_bias_grad, fc1_bias_grad, fc2_bias_grad, gain1, shift1, qv_bias_grad, gain0, shift0 = bundle
    norm_gains_grad = jnp.stack([gain0, gain1])
    norm_biases_grad = jnp.stack([shift0, shift1])
    return (
        result,
        tokens_grad,
        w_qkv_grad,
        qv_bias_grad,
        w_proj_grad,
        proj_bias_grad,
        w_fc1_grad,
        fc1_bias_grad,
        w_fc2_grad,
        fc2_bias_grad,
        norm_gains_grad,
        norm_biases_grad,
        rel_tables_grad,
    )


def layer_norm(values, gain, shift):
    center = jnp.mean(values, axis=-1, keepdims=True)
    centered = values - center
    spread = jnp.mean(centered * centered, axis=-1, keepdims=True)
    return centered * lax.rsqrt(spread + EPS) * gain + shift


def fetch_each(weights):
    return (
        lax.all_gather(weights[0], ("dp", "seq"), axis=0, tiled=True),
        lax.all_gather(weights[1], ("dp", "seq"), axis=0, tiled=True),
        lax.all_gather(weights[2], ("dp", "seq"), axis=0, tiled=True),
        lax.all_gather(weights[3], ("dp", "seq"), axis=0, tiled=True),
        lax.all_gather(weights[4], ("dp", "seq"), axis=0, tiled=True),
        lax.all_gather(weights[5], ("dp", "seq"), axis=0, tiled=True),
        lax.all_gather(weights[6], ("dp", "seq"), axis=0, tiled=True),
        lax.all_gather(weights[7], ("dp", "seq"), axis=0, tiled=True),
        lax.all_gather(weights[8], ("dp", "seq"), axis=1, tiled=True),
        lax.all_gather(weights[9], ("dp", "seq"), axis=1, tiled=True),
    )


def position_rows(tables, rows_img):
    beginning = lax.axis_index("seq") * rows_img
    tokens_at = beginning + jnp.arange(rows_img, dtype=jnp.int32)
    offsets = jnp.arange(GRID, dtype=jnp.int32)
    entries = jnp.arange(TABLE, dtype=jnp.int32)
    row_index = tokens_at[:, None] // GRID - offsets[None, :] + GRID - 1
    col_index = tokens_at[:, None] % GRID - offsets[None, :] + GRID - 1
    row_hot = (row_index[:, :, None] == entries[None, None, :]).astype(jnp.float32)
    col_hot = (col_index[:, :, None] == entries[None, None, :]).astype(jnp.float32)
    tables_f = tables.astype(jnp.float32)
    rel_rows = jnp.einsum("rkt,tc->rkc", row_hot, tables_f[0], precision=HIGH)
    rel_cols = jnp.einsum("rkt,tc->rkc", col_hot, tables_f[1], precision=HIGH)
    return (row_hot, col_hot, rel_rows, rel_cols)


def score_block(queries, keys_all, rows_low, cols_low):
    rows_img = queries.shape[0]
    product = jnp.einsum(
        "rhc,nhc->hrn", queries, keys_all, preferred_element_type=jnp.float32
    ) * HD ** (-0.5)
    bias_rows = jnp.einsum("rhc,rkc->hrk", queries, rows_low, preferred_element_type=jnp.float32)
    bias_cols = jnp.einsum("rhc,rkc->hrk", queries, cols_low, preferred_element_type=jnp.float32)
    joined = (
        product.reshape(HEADS, rows_img, GRID, GRID)
        + bias_rows[:, :, :, None]
        + bias_cols[:, :, None, :]
    )
    return joined.reshape(HEADS, rows_img, GRID * GRID)


def attend_forward(qkv_img, kv_pair, rows_low, cols_low):
    rows_img, triple = qkv_img.shape
    features = triple // 3
    queries = qkv_img[:, :features].reshape(rows_img, HEADS, HD)
    keys_all = kv_pair[0].reshape(-1, HEADS, HD)
    values_all = kv_pair[1].reshape(-1, HEADS, HD)
    scores = score_block(queries, keys_all, rows_low, cols_low)
    largest = jnp.max(scores, axis=-1, keepdims=True)
    shifted = jnp.exp(scores - largest)
    totals = jnp.sum(shifted, axis=-1, keepdims=True)
    probs_low = (shifted / totals).astype(jnp.bfloat16)
    attended = jnp.einsum("hrn,nhc->rhc", probs_low, values_all, preferred_element_type=jnp.float32)
    log_totals = largest[..., 0] + jnp.log(totals[..., 0])
    return (attended.reshape(rows_img, features).astype(jnp.bfloat16), log_totals)


def attend_backward(qkv_img, log_totals, grad_att, kv_pair, rel_rows, rel_cols, rows_low, cols_low):
    rows_img, triple = qkv_img.shape
    features = triple // 3
    scale = HD ** (-0.5)
    queries = qkv_img[:, :features].reshape(rows_img, HEADS, HD)
    keys_all = kv_pair[0].reshape(-1, HEADS, HD)
    values_all = kv_pair[1].reshape(-1, HEADS, HD)
    scores = score_block(queries, keys_all, rows_low, cols_low)
    probs = jnp.exp(scores - log_totals[..., None])
    probs_low = probs.astype(jnp.bfloat16)
    grad_heads = grad_att.reshape(rows_img, HEADS, HD)
    grad_probs = jnp.einsum(
        "rhc,nhc->hrn", grad_heads, values_all, preferred_element_type=jnp.float32
    )
    inner_sum = jnp.sum(probs * grad_probs, axis=-1, keepdims=True)
    grad_scores = (probs * (grad_probs - inner_sum)).astype(jnp.bfloat16)
    grad_queries = (
        jnp.einsum("hrn,nhc->rhc", grad_scores, keys_all, preferred_element_type=jnp.float32)
        * scale
    )
    grid_scores = grad_scores.reshape(HEADS, rows_img, GRID, GRID)
    grad_rows = jnp.sum(grid_scores, axis=3, dtype=jnp.float32)
    grad_cols = jnp.sum(grid_scores, axis=2, dtype=jnp.float32)
    grad_queries = grad_queries + jnp.einsum("hrk,rkc->rhc", grad_rows, rel_rows, precision=HIGH)
    grad_queries = grad_queries + jnp.einsum("hrk,rkc->rhc", grad_cols, rel_cols, precision=HIGH)
    query_f = queries.astype(jnp.float32)
    table_rows = jnp.einsum("hrk,rhc->rkc", grad_rows, query_f, precision=HIGH)
    table_cols = jnp.einsum("hrk,rhc->rkc", grad_cols, query_f, precision=HIGH)
    length = lax.axis_size("seq") * rows_img
    grad_keys = (
        jnp.einsum("hrn,rhc->nhc", grad_scores, queries, preferred_element_type=jnp.float32) * scale
    )
    grad_values = jnp.einsum(
        "hrn,rhc->nhc", probs_low, grad_heads, preferred_element_type=jnp.float32
    )
    key_grads = lax.psum_scatter(
        jnp.concatenate(
            [grad_keys.reshape(length, features), grad_values.reshape(length, features)], axis=1
        ),
        "seq",
        scatter_dimension=0,
        tiled=True,
    )
    grad_qkv = jnp.concatenate(
        [grad_queries.reshape(rows_img, features), key_grads], axis=1
    ).astype(jnp.bfloat16)
    return (grad_qkv, table_rows, table_cols)


def body(
    tokens,
    w_qkv,
    qv_bias,
    w_proj,
    proj_bias,
    w_fc1,
    fc1_bias,
    w_fc2,
    fc2_bias,
    norm_gains,
    norm_biases,
    rel_tables,
    cotangent,
):
    images, rows_img, features = tokens.shape
    per_batch = images // MB
    weights = (
        w_qkv,
        qv_bias,
        w_proj,
        proj_bias,
        w_fc1,
        fc1_bias,
        w_fc2,
        fc2_bias,
        norm_gains,
        norm_biases,
    )
    row_hot, col_hot, rel_rows, rel_cols = position_rows(rel_tables, rows_img)
    rows_low = rel_rows.astype(jnp.bfloat16)
    cols_low = rel_cols.astype(jnp.bfloat16)
    stored = []
    outputs = []
    for batch_index in range(MB):
        gathered = fetch_each(weights)
        (
            wq_full,
            bqv_full,
            wp_full,
            bp_full,
            w1_full,
            b1_full,
            w2_full,
            b2_full,
            gains_full,
            shifts_full,
        ) = gathered
        gains_f = gains_full.astype(jnp.float32)
        shifts_f = shifts_full.astype(jnp.float32)
        inputs = (
            tokens[batch_index * per_batch : (batch_index + 1) * per_batch]
            .astype(jnp.float32)
            .reshape(-1, features)
        )
        normed1 = layer_norm(inputs, gains_f[0], shifts_f[0]).astype(jnp.bfloat16)
        full_bias = jnp.concatenate(
            [bqv_full[:features], jnp.zeros((features,), bqv_full.dtype), bqv_full[features:]]
        ).astype(jnp.float32)
        qkv = (jnp.dot(normed1, wq_full, preferred_element_type=jnp.float32) + full_bias).astype(
            jnp.bfloat16
        )
        qkv_images = qkv.reshape(per_batch, rows_img, 3 * features)

        def forward_image(carried, qkv_img):
            kv_pair = (
                lax.all_gather(qkv_img[:, features : 2 * features], "seq", axis=0, tiled=True),
                lax.all_gather(qkv_img[:, 2 * features :], "seq", axis=0, tiled=True),
            )
            attended_img, log_totals = attend_forward(qkv_img, kv_pair, rows_low, cols_low)
            return (carried, (attended_img, log_totals))

        results = lax.scan(forward_image, jnp.zeros((), jnp.float32), qkv_images)[1]
        attended = results[0].reshape(-1, features)
        mixed = (
            inputs
            + jnp.dot(attended, wp_full, preferred_element_type=jnp.float32)
            + bp_full.astype(jnp.float32)
        )
        normed2 = layer_norm(mixed, gains_f[1], shifts_f[1]).astype(jnp.bfloat16)
        pre = jnp.dot(normed2, w1_full, preferred_element_type=jnp.float32) + b1_full.astype(
            jnp.float32
        )
        activated = jax.nn.gelu(pre, approximate=False).astype(jnp.bfloat16)
        block_out = (
            mixed
            + jnp.dot(activated, w2_full, preferred_element_type=jnp.float32)
            + b2_full.astype(jnp.float32)
        )
        outputs.append(block_out.astype(jnp.bfloat16).reshape(per_batch, rows_img, features))
        stored.append((normed1, qkv_images, results, mixed, normed2, pre, activated))
    gradients = [jnp.zeros(array.shape, jnp.float32) for array in gathered]
    table_rows_sum = jnp.zeros((rows_img, GRID, HD), jnp.float32)
    table_cols_sum = jnp.zeros((rows_img, GRID, HD), jnp.float32)
    input_grads = []
    for batch_index in range(MB):
        gathered = fetch_each(weights)
        (
            wq_full,
            bqv_full,
            wp_full,
            bp_full,
            w1_full,
            b1_full,
            w2_full,
            b2_full,
            gains_full,
            shifts_full,
        ) = gathered
        gains_f = gains_full.astype(jnp.float32)
        shifts_f = shifts_full.astype(jnp.float32)
        normed1, qkv_images, results, mixed, normed2, pre, activated = stored[batch_index]
        inputs = (
            tokens[batch_index * per_batch : (batch_index + 1) * per_batch]
            .astype(jnp.float32)
            .reshape(-1, features)
        )
        grad_out = cotangent[batch_index * per_batch : (batch_index + 1) * per_batch].reshape(
            -1, features
        )
        grad_out_f = grad_out.astype(jnp.float32)
        grad_w2 = jnp.dot(activated.T, grad_out, preferred_element_type=jnp.float32)
        grad_b2 = jnp.sum(grad_out_f, axis=0)
        grad_act = jnp.dot(grad_out, w2_full.T, preferred_element_type=jnp.float32)
        _, gelu_pull = jax.vjp(partial(jax.nn.gelu, approximate=False), pre)
        grad_pre = gelu_pull(grad_act)[0].astype(jnp.bfloat16)
        grad_w1 = jnp.dot(normed2.T, grad_pre, preferred_element_type=jnp.float32)
        grad_b1 = jnp.sum(grad_pre, axis=0, dtype=jnp.float32)
        grad_norm2 = jnp.dot(grad_pre, w1_full.T, preferred_element_type=jnp.float32)
        _, norm_pull2 = jax.vjp(layer_norm, mixed, gains_f[1], shifts_f[1])
        grad_mix_norm, grad_gain2, grad_shift2 = norm_pull2(grad_norm2)
        grad_mixed = grad_out_f + grad_mix_norm
        grad_branch = grad_mixed.astype(jnp.bfloat16)
        attended = results[0].reshape(-1, features)
        grad_wp = jnp.dot(attended.T, grad_branch, preferred_element_type=jnp.float32)
        grad_bp = jnp.sum(grad_branch, axis=0, dtype=jnp.float32)
        grad_att = jnp.dot(grad_branch, wp_full.T, preferred_element_type=jnp.float32).astype(
            jnp.bfloat16
        )
        grad_images = grad_att.reshape(per_batch, rows_img, features)
        image_inputs = (qkv_images, results[1], grad_images)

        def backward_image(carried, pieces):
            kv_pair = (
                lax.all_gather(pieces[0][:, features : 2 * features], "seq", axis=0, tiled=True),
                lax.all_gather(pieces[0][:, 2 * features :], "seq", axis=0, tiled=True),
            )
            grad_qkv_img, table_rows, table_cols = attend_backward(
                pieces[0], pieces[1], pieces[2], kv_pair, rel_rows, rel_cols, rows_low, cols_low
            )
            return ((carried[0] + table_rows, carried[1] + table_cols), grad_qkv_img)

        (table_rows_sum, table_cols_sum), grad_qkv_all = lax.scan(
            backward_image, (table_rows_sum, table_cols_sum), image_inputs
        )
        grad_qkv = grad_qkv_all.reshape(-1, 3 * features)
        grad_wq = jnp.dot(normed1.T, grad_qkv, preferred_element_type=jnp.float32)
        grad_bqv = jnp.concatenate(
            [
                jnp.sum(grad_qkv[:, :features], axis=0, dtype=jnp.float32),
                jnp.sum(grad_qkv[:, 2 * features :], axis=0, dtype=jnp.float32),
            ]
        )
        grad_norm1 = jnp.dot(grad_qkv, wq_full.T, preferred_element_type=jnp.float32)
        _, norm_pull1 = jax.vjp(layer_norm, inputs, gains_f[0], shifts_f[0])
        grad_in_norm, grad_gain1, grad_shift1 = norm_pull1(grad_norm1)
        input_grads.append(
            (grad_mixed + grad_in_norm).astype(jnp.bfloat16).reshape(per_batch, rows_img, features)
        )
        updates = (
            grad_wq,
            grad_bqv,
            grad_wp,
            grad_bp,
            grad_w1,
            grad_b1,
            grad_w2,
            grad_b2,
            jnp.stack([grad_gain1, grad_gain2]),
            jnp.stack([grad_shift1, grad_shift2]),
        )
        gradients = [before + update for before, update in zip(gradients, updates)]
    summed = (
        lax.psum_scatter(gradients[0], ("dp", "seq"), scatter_dimension=0, tiled=True),
        lax.psum_scatter(gradients[1], ("dp", "seq"), scatter_dimension=0, tiled=True),
        lax.psum_scatter(gradients[2], ("dp", "seq"), scatter_dimension=0, tiled=True),
        lax.psum_scatter(gradients[3], ("dp", "seq"), scatter_dimension=0, tiled=True),
        lax.psum_scatter(gradients[4], ("dp", "seq"), scatter_dimension=0, tiled=True),
        lax.psum_scatter(gradients[5], ("dp", "seq"), scatter_dimension=0, tiled=True),
        lax.psum_scatter(gradients[6], ("dp", "seq"), scatter_dimension=0, tiled=True),
        lax.psum_scatter(gradients[7], ("dp", "seq"), scatter_dimension=0, tiled=True),
        lax.psum_scatter(gradients[8], ("dp", "seq"), scatter_dimension=1, tiled=True),
        lax.psum_scatter(gradients[9], ("dp", "seq"), scatter_dimension=1, tiled=True),
    )
    table_local = jnp.stack(
        [
            jnp.einsum("rkt,rkc->tc", row_hot, table_rows_sum, precision=HIGH),
            jnp.einsum("rkt,rkc->tc", col_hot, table_cols_sum, precision=HIGH),
        ]
    )
    table_grad = lax.psum(table_local, ("dp", "seq"))
    return (
        jnp.concatenate(outputs, axis=0),
        jnp.concatenate(input_grads, axis=0),
        summed[0],
        summed[1],
        summed[2],
        summed[3],
        summed[4],
        summed[5],
        summed[6],
        summed[7],
        summed[8],
        summed[9],
        table_grad,
    )


def solution(mesh):
    placed = (
        P("dp", "seq", None),
        P(("dp", "seq"), None),
        P(("dp", "seq")),
        P(("dp", "seq"), None),
        P(("dp", "seq")),
        P(("dp", "seq"), None),
        P(("dp", "seq")),
        P(("dp", "seq"), None),
        P(("dp", "seq")),
        P(None, ("dp", "seq")),
        P(None, ("dp", "seq")),
        P(),
        P("dp", "seq", None),
    )
    seqs, images = mesh.shape["seq"], IMAGES // mesh.shape["dp"]
    by_heads = (mesh.shape["dp"], seqs, images) == (4, 8, 2)
    return jax.shard_map(
        body_heads if by_heads else body,
        mesh=mesh,
        in_specs=placed,
        out_specs=(
            P("dp", "seq", None),
            P("dp", "seq", None),
            P(("dp", "seq"), None),
            P(("dp", "seq")),
            P(("dp", "seq"), None),
            P(("dp", "seq")),
            P(("dp", "seq"), None),
            P(("dp", "seq")),
            P(("dp", "seq"), None),
            P(("dp", "seq")),
            P(None, ("dp", "seq")),
            P(None, ("dp", "seq")),
            P(),
        ),
        check_vma=False,
    )
```

```python
from functools import partial
import math

import jax
import jax.numpy as jnp
from jax import lax
from jax.experimental import pallas as pl
from jax.experimental.pallas import tpu as pltpu
from jax.sharding import PartitionSpec as P

HEADS = 12
HD = 64
GRID = 64
MB = 2
TABLE = 127


EPS = 1e-06
HIGH = lax.Precision.HIGHEST
IMAGES = 8
AXES = ("dp", "seq")

TB = 1024
CK = 512
ROWS = CK // GRID
LOG2E = 1.4426950408889634
NN = (((1,), (0,)), ((), ()))
NT = (((1,), (1,)), ((), ()))
TN = (((0,), (0,)), ((), ()))
BF = jnp.bfloat16
F32 = jnp.float32


def dot(a, b, dims):
    return lax.dot_general(a, b, dims, preferred_element_type=F32)


def col_hot(n):
    key = lax.broadcasted_iota(jnp.int32, (n, GRID), 0) & (GRID - 1)
    col = lax.broadcasted_iota(jnp.int32, (n, GRID), 1)
    return (key == col).astype(F32)


def fwd_kernel(n_chunks, qkv_ref, tab_ref, oT_ref, oTf_ref, p_ref, f_ref, kaug, vta, br_ref, qa_ref):
    i = pl.program_id(0)
    tg = TB // GRID

    @pl.when(i == 0)
    def _():
        for c in range(n_chunks):
            rows = pl.ds(c * CK, CK)
            k = qkv_ref[rows, HD : 2 * HD].astype(F32)
            pair = jnp.concatenate([k, col_hot(CK)], axis=1).astype(BF)
            kaug[rows, : 2 * HD] = pair
            kaug[rows, 2 * HD :] = pair
            vT = qkv_ref[rows, 2 * HD :].astype(F32).T
            vta[0:HD, rows] = vT.astype(BF)
            one = lax.broadcasted_iota(jnp.int32, (16, CK), 0) == 0
            vta[HD : HD + 16, rows] = one.astype(F32).astype(BF)

    q = qkv_ref[pl.ds(pl.multiple_of(i * TB, TB), TB), :HD]
    gr = dot(q, tab_ref[0], NT) * LOG2E
    gc = dot(q, tab_ref[1], NT) * LOG2E
    brs, bcs = [], []
    for g in range(tg):
        sl = slice(g * GRID, (g + 1) * GRID)
        brs.append(pltpu.roll(gr[sl], i * tg + g, 1))
        bcs.append(pltpu.roll(gc[sl], 0, 1, stride=1, stride_axis=0))
    br = jnp.concatenate(brs, axis=0)
    bc = jnp.concatenate(bcs, axis=0)
    qs = q.astype(F32) * (HD ** -0.5 * LOG2E)
    cat = jnp.concatenate([qs, bc[:, :GRID]], axis=1).T
    hi = cat.astype(BF)
    lo = (cat - hi.astype(F32)).astype(BF)
    qa_ref[...] = jnp.concatenate([hi, lo], axis=0)
    br_ref[...] = br.T[:GRID]
    qa = qa_ref[...]

    def scores(c):
        return dot(kaug[c * CK : (c + 1) * CK, :], qa, NN)

    def soften(c, s):
        s = s.reshape(ROWS, GRID, TB)
        b8 = br_ref[c * ROWS : (c + 1) * ROWS, :]
        top = jnp.max(jnp.max(s, axis=1) + b8, axis=0, keepdims=True)
        p = jnp.exp2(s - (top - b8)[:, None, :]).astype(BF).reshape(CK, TB)
        p_ref[0, c * CK : (c + 1) * CK, :] = p
        return top, p

    def gather(m, acc, c, top, p):
        out = dot(vta[:, c * CK : (c + 1) * CK], p, NN)
        new = jnp.maximum(m, top)
        return new, acc * jnp.exp2(m - new) + out * jnp.exp2(top - new)

    m = jnp.full((1, TB), -jnp.inf, F32)
    acc = jnp.zeros((HD + 16, TB), F32)
    tops = []
    s, before = scores(0), None
    for c in range(n_chunks):
        following = scores(c + 1) if c + 1 < n_chunks else None
        if before is not None:
            m, acc = gather(m, acc, c - 1, *before)
        before, s = soften(c, s), following
        tops.append(before[0])
    m, acc = gather(m, acc, n_chunks - 1, *before)
    total = acc[HD : HD + 1]
    out = acc[:HD] / total
    for j in range(TB // CK):
        oT_ref[j] = out[:, j * CK : (j + 1) * CK].astype(BF)
    oTf_ref[...] = out
    f_ref[...] = jnp.exp2(jnp.concatenate(tops, axis=0) - (m + jnp.log2(total)))


def heads_forward(qkv, tab):
    n = qkv.shape[0]
    steps, chunks, side = n // TB, n // CK, TB // CK
    return pl.pallas_call(
        partial(fwd_kernel, chunks),
        grid=(steps,),
        in_specs=[
            pl.BlockSpec((n, 3 * HD), lambda i: (0, 0)),
            pl.BlockSpec((2, 2 * GRID, HD), lambda i: (0, 0, 0)),
        ],
        out_specs=[
            pl.BlockSpec((side, HD, CK), lambda i: (i, 0, 0)),
            pl.BlockSpec((HD, TB), lambda i: (0, i)),
            pl.BlockSpec((1, n, TB), lambda i: (i, 0, 0)),
            pl.BlockSpec((chunks, TB), lambda i: (0, i)),
        ],
        out_shape=[
            jax.ShapeDtypeStruct((chunks, HD, CK), BF),
            jax.ShapeDtypeStruct((HD, n), F32),
            jax.ShapeDtypeStruct((steps, n, TB), BF),
            jax.ShapeDtypeStruct((chunks, n), F32),
        ],
        scratch_shapes=[
            pltpu.VMEM((n, 4 * HD), BF),
            pltpu.VMEM((HD + 16, n), BF),
            pltpu.VMEM((GRID, TB), F32),
            pltpu.VMEM((4 * HD, TB), BF),
        ],
        compiler_params=pltpu.CompilerParams(vmem_limit_bytes=56 * 2**20),
        cost_estimate=pl.CostEstimate(
            flops=4 * n * n * 4 * HD, bytes_accessed=48 * 2**20, transcendentals=n * n
        ),
    )(qkv, tab)


def bwd_kernel(
    n_chunks, dps, seqs, qkv_ref, tab_ref, p_ref, f_ref, oTf_ref, doT_ref, x_hbm, msg_ref, *refs
):
    *far_ref, vaug, kta, dkv, dqa, dtab_ref, x_ref, x_sem = refs
    i = pl.program_id(0)
    tg, side = TB // GRID, TB // CK
    n_steps = pl.num_programs(0)
    fetch = pltpu.make_async_copy(x_hbm, x_ref, x_sem)

    @pl.when(i == 0)
    def _():
        for c in range(n_chunks):
            rows = pl.ds(c * CK, CK)
            k = qkv_ref[rows, HD : 2 * HD].astype(F32)
            both = jnp.concatenate([k, col_hot(CK)], axis=1).T
            kta[0 : 2 * HD, rows] = both.astype(BF)
            key = lax.broadcasted_iota(jnp.int32, (16, CK), 1) >> 6
            hot = lax.broadcasted_iota(jnp.int32, (16, CK), 0) == key
            kta[2 * HD : 2 * HD + 16, rows] = hot.astype(F32).astype(BF)
            v = qkv_ref[rows, 2 * HD :].astype(F32)
            lane = lax.broadcasted_iota(jnp.int32, (CK, HD), 1)
            vaug[rows, :] = jnp.concatenate([v, (lane < 3).astype(F32)], axis=1).astype(BF)
            dkv[rows, :] = jnp.zeros((CK, 2 * HD), F32)
        dtab_ref[...] = jnp.zeros_like(dtab_ref)
        fetch.start()

    q = qkv_ref[pl.ds(pl.multiple_of(i * TB, TB), TB), :HD]
    doT = jnp.concatenate([doT_ref[j].astype(F32) for j in range(side)], axis=1)
    delta = -jnp.sum(doT * oTf_ref[...], axis=0, keepdims=True)
    d1 = delta.astype(BF).astype(F32)
    d2 = (delta - d1).astype(BF).astype(F32)
    pad = jnp.concatenate([d1, d2, delta - d1 - d2, jnp.zeros((HD - 3, TB), F32)], axis=0)
    doa = jnp.concatenate([doT, pad], axis=0).astype(BF)
    do = jnp.concatenate([doT, jnp.zeros((HD, TB), F32)], axis=0).T
    qz = jnp.concatenate([jnp.zeros((TB, HD), F32), q.astype(F32)], axis=1)
    doq = jnp.concatenate([do, qz], axis=0).astype(BF)
    dqa[...] = jnp.zeros_like(dqa)

    def grad_probs(c):
        return dot(vaug[c * CK : (c + 1) * CK, :], doa, NN)

    def grad_scores(c, dp):
        p = p_ref[0, c * CK : (c + 1) * CK, :].astype(F32) * f_ref[c : c + 1, :]
        return jnp.concatenate([p.astype(BF), (p * dp).astype(BF)], axis=1)

    def gather(c, pd):
        rows = slice(c * CK, (c + 1) * CK)
        dkv[rows, :] += dot(pd, doq, NN)
        g = dot(kta[:, rows], pd[:, TB:], NN)
        dqa[0 : 2 * HD, :] += g[: 2 * HD]
        dqa[2 * HD + c * ROWS : 2 * HD + (c + 1) * ROWS, :] = g[2 * HD : 2 * HD + ROWS]

    dp, before = grad_probs(0), None
    for c in range(n_chunks):
        following = grad_probs(c + 1) if c + 1 < n_chunks else None
        if before is not None:
            gather(c - 1, before)
        before, dp = grad_scores(c, dp), following
    gather(n_chunks - 1, before)

    grads = dqa[HD : 3 * HD, :].T
    lane = lax.broadcasted_iota(jnp.int32, (TB, 2 * GRID), 1)
    gcol = jnp.where(lane < GRID, grads, 0.0)
    grow = jnp.where(lane >= GRID, grads, 0.0)
    rs, cs = [], []
    col = lax.broadcasted_iota(jnp.int32, (GRID, 2 * GRID), 0)
    for g in range(tg):
        sl = slice(g * GRID, (g + 1) * GRID)
        rs.append(pltpu.roll(grow[sl], GRID - (i * tg + g), 1))
        x = gcol[sl]
        for bit in range(6):
            x = jnp.where((col >> bit) & 1 == 1, pltpu.roll(x, 2 * GRID - (1 << bit), 1), x)
        cs.append(x)
    drow = jnp.concatenate(rs, axis=0).astype(BF)
    dcol = jnp.concatenate(cs, axis=0).astype(BF)
    dq = dqa[:HD, :] * HD ** -0.5
    dq = dq + dot(tab_ref[0], drow, (((0,), (1,)), ((), ())))
    dq = dq + dot(tab_ref[1], dcol, (((0,), (1,)), ((), ())))
    for j in range(side):
        msg_ref[i * side + j, 0:HD, :] = dq[:, j * CK : (j + 1) * CK].astype(BF)
    dtab_ref[0:HD, :] += dot(q, drow, TN)
    dtab_ref[HD : 2 * HD, :] += dot(q, dcol, TN)

    @pl.when(i == n_steps - 1)
    def _():
        for c in range(n_chunks):
            both = dkv[c * CK : (c + 1) * CK, :].T
            msg_ref[c, HD : 2 * HD, :] = (both[HD:] * HD ** -0.5).astype(BF)
            msg_ref[c, 2 * HD : 3 * HD, :] = both[:HD].astype(BF)
        fetch.wait()
        all_grads = jnp.concatenate([msg_ref[c, : 3 * HD, :] for c in range(n_chunks)], axis=1)
        moment = dot(all_grads, x_ref[...], NN).T
        total = dot(jnp.ones((8, all_grads.shape[1]), BF), all_grads, NT)
        hi = total.astype(BF).astype(F32)
        row = lax.broadcasted_iota(jnp.int32, total.shape, 0)
        ending = jnp.where(row == 0, hi, jnp.where(row == 1, total - hi, 0.0))
        part = moment.shape[0] // (dps * seqs)
        half = dps // 2
        base = msg_ref.shape[1] - 16
        for d in range(dps * seqs if far_ref else 0):
            piece = jnp.concatenate([moment[d * part : (d + 1) * part], ending], axis=0)
            fill = jnp.zeros((part + 8, HD), F32)
            far_ref[0][d] = jnp.concatenate([piece, fill], axis=1).astype(BF)
        for s in range(seqs):
            if not far_ref:
                sides = []
                for side in range(2):
                    tops = [(d * seqs + s) * part for d in range(side * half, (side + 1) * half)]
                    sides.append(jnp.concatenate([moment[t : t + part] for t in tops], axis=0))
                sides.append(jnp.zeros((half * part, CK - 6 * HD), F32))
                msg_ref[s, 3 * HD : base, :] = jnp.concatenate(sides, axis=1).astype(BF)
            piece = dtab_ref[s * 16 : (s + 1) * 16, :]
            hi = piece.astype(BF).astype(F32)
            sums = jnp.concatenate([ending, jnp.zeros((8, 3 * HD), F32)], axis=0)
            fill = jnp.zeros((16, CK - 7 * HD), F32)
            row = jnp.concatenate([hi, piece - hi, sums, fill], axis=1)
            msg_ref[s, base:, :] = row.astype(BF)


def heads_backward(dps, seqs, last, qkv, tab, probs, factors, oTf, x, doT):
    n, features = x.shape
    steps, chunks, side = n // TB, n // CK, TB // CK
    part = features // (dps * seqs)
    shapes = [(chunks, 3 * HD + 16 + (0 if last else dps // 2 * part), CK)]
    if last:
        shapes.append((dps * seqs, part + 8, 4 * HD))
    return pl.pallas_call(
        partial(bwd_kernel, n // CK, dps, seqs),
        grid=(steps,),
        in_specs=[
            pl.BlockSpec((n, 3 * HD), lambda i: (0, 0)),
            pl.BlockSpec((2, 2 * GRID, HD), lambda i: (0, 0, 0)),
            pl.BlockSpec((1, n, TB), lambda i: (i, 0, 0)),
            pl.BlockSpec((chunks, TB), lambda i: (0, i)),
            pl.BlockSpec((HD, TB), lambda i: (0, i)),
            pl.BlockSpec((side, HD, CK), lambda i: (i, 0, 0)),
            pl.BlockSpec(memory_space=pl.ANY),
        ],
        out_specs=[pl.BlockSpec(shape, lambda i: (0, 0, 0)) for shape in shapes],
        out_shape=[jax.ShapeDtypeStruct(shape, BF) for shape in shapes],
        scratch_shapes=[
            pltpu.VMEM((n, 2 * HD), BF),
            pltpu.VMEM((2 * HD + 16, n), BF),
            pltpu.VMEM((n, 2 * HD), F32),
            pltpu.VMEM((3 * HD, TB), F32),
            pltpu.VMEM((2 * HD, 2 * GRID), F32),
            pltpu.VMEM((n, features), BF),
            pltpu.SemaphoreType.DMA,
        ],
        compiler_params=pltpu.CompilerParams(vmem_limit_bytes=56 * 2**20),
        cost_estimate=pl.CostEstimate(
            flops=8 * n * n * 4 * HD, bytes_accessed=48 * 2**20, transcendentals=0
        ),
    )(qkv, tab, probs, factors, oTf, doT, x)


def qkv_kernel(per, steps, n_held, here_ref, *refs):
    blocks, rest = refs[:steps], refs[steps:]
    w_ref, par_ref, bias_ref = rest[:3]
    x_ref, *outs, held, sems = rest[3 + n_held :]
    m = pl.program_id(0)
    copies = [
        pltpu.make_async_copy(blocks[j], held.at[j], sems.at[j]) for j in range(len(blocks))
    ]

    @pl.when(m == 0)
    def _():
        for copy in copies:
            copy.start()

    for j, copy in enumerate(copies):

        @pl.when(m == j)
        def _():
            copy.wait()

    v = held[m].astype(F32)
    v = v - jnp.mean(v, axis=-1, keepdims=True)
    v = v * lax.rsqrt(jnp.mean(v * v, axis=-1, keepdims=True) + EPS)
    x_ref[...] = v.astype(BF)
    x = (v * par_ref[0:1, :] + par_ref[1:2, :]).astype(BF)
    qkv = dot(x, w_ref[...], NN) + bias_ref[...]
    for p in range(per):
        outs[p][...] = qkv[:, p * 3 * HD : (p + 1) * 3 * HD].astype(BF)


def normed_qkv(here, first, total, blocks, w_cols, params, bias, before):
    rows, features = blocks[0].shape
    wide = w_cols.shape[1]
    per, steps = wide // (3 * HD), len(blocks)
    place = lambda m, here: ((m + first) ^ here[0], 0)
    return pl.pallas_call(
        partial(qkv_kernel, per, steps, len(before)),
        grid_spec=pltpu.PrefetchScalarGridSpec(
            num_scalar_prefetch=1,
            grid=(steps,),
            in_specs=[pl.BlockSpec(memory_space=pl.ANY)] * steps
            + [
                pl.BlockSpec((features, wide), lambda m, here: (0, 0)),
                pl.BlockSpec((2, features), lambda m, here: (0, 0)),
                pl.BlockSpec((1, wide), lambda m, here: (0, 0)),
            ]
            + [pl.BlockSpec(memory_space=pl.ANY)] * len(before),
            out_specs=[pl.BlockSpec((rows, features), place)]
            + [pl.BlockSpec((rows, 3 * HD), place)] * per,
            scratch_shapes=[
                pltpu.VMEM((steps, rows, features), BF),
                pltpu.SemaphoreType.DMA((steps,)),
            ],
        ),
        out_shape=[jax.ShapeDtypeStruct((total * rows, features), BF)]
        + [jax.ShapeDtypeStruct((total * rows, 3 * HD), BF)] * per,
        input_output_aliases={4 + steps + j: j for j in range(len(before))},
        compiler_params=pltpu.CompilerParams(vmem_limit_bytes=56 * 2**20),
        cost_estimate=pl.CostEstimate(
            flops=2 * steps * rows * features * wide, bytes_accessed=24 * 2**20, transcendentals=0
        ),
    )(here.reshape(1).astype(jnp.int32), *blocks, w_cols, params, bias, *before)


def mirror(tables):
    hole = jnp.zeros((2, 1, HD), tables.dtype)
    return jnp.concatenate([tables[:, GRID - 1 :: -1], hole, tables[:, : GRID - 1 : -1]], axis=1)


def unmirror(grads):
    return jnp.concatenate([grads[:, GRID - 1 :: -1], grads[:, : GRID : -1]], axis=1)


def attended_rows(ahead_ref, ending_ref, slots):
    images = ahead_ref.shape[0] // slots
    sides = []
    for y in range(images):
        parts = []
        for g in range(slots):
            parts += [ahead_ref[y * slots + g], ending_ref[y * slots + g]]
        sides.append(jnp.concatenate(parts, axis=0))
    return jnp.concatenate(sides, axis=1)


def mlp_kernel(
    slots, ahead_ref, ending_ref, tok_ref, cot_ref, w1_ref, w2_ref, wp_ref, par_ref, b1_ref,
    act_ref, gp_ref, n2_ref, mixed_ref, gm_ref, gb_ref, g0_ref, g12_ref, sum_ref, sb1_ref,
    hat_ref, rate_ref, gn_ref
):
    k, last = pl.program_id(0), pl.num_programs(0) - 1
    width = w1_ref.shape[1]
    sub = width // 3

    @pl.when(k == 0)
    def _():
        att = attended_rows(ahead_ref, ending_ref, slots)
        mixed = tok_ref[...].astype(F32) + dot(att, wp_ref[...], TN) + par_ref[0:1, :]
        mixed_ref[...] = mixed
        v = mixed - jnp.mean(mixed, axis=-1, keepdims=True)
        rate = lax.rsqrt(jnp.mean(v * v, axis=-1, keepdims=True) + EPS)
        hat = v * rate
        hat_ref[...] = hat
        rate_ref[...] = rate
        n2_ref[...] = (hat * par_ref[1:2, :] + par_ref[2:3, :]).astype(BF)
        gn_ref[...] = jnp.zeros_like(gn_ref)

    def products(j):
        cols = slice(j * sub, (j + 1) * sub)
        pre = dot(n2_ref[...], w1_ref[:, cols], NN) + b1_ref[:, cols]
        return pre, dot(cot_ref[...], w2_ref[cols, :], NT)

    def curves(j, pre, grad):
        cols = slice(j * sub, (j + 1) * sub)
        cdf = 0.5 + 0.5 * lax.erf(pre * 0.5**0.5)
        act_ref[:, cols] = (pre * cdf).astype(BF)
        slope = cdf + pre * (jnp.exp(-0.5 * pre * pre) * (2.0 * math.pi) ** -0.5)
        g = (grad * slope).astype(BF)
        gp_ref[:, cols] = g
        sb1_ref[:, cols] = jnp.sum(g.astype(F32), axis=0, keepdims=True)

    now = products(0)
    for j in range(3):
        following = products(j + 1) if j < 2 else None
        curves(j, *now)
        now = following
    gn_ref[...] += dot(gp_ref[...], w1_ref[...], NT)

    @pl.when(k == last)
    def _():
        gn, hat, cot = gn_ref[...], hat_ref[...], cot_ref[...].astype(F32)
        u = gn * par_ref[1:2, :]
        back = u - jnp.mean(u, axis=-1, keepdims=True)
        back = back - hat * jnp.mean(u * hat, axis=-1, keepdims=True)
        gm = cot + rate_ref[...] * back
        gm_ref[...] = gm
        gb = gm.astype(BF)
        gb_ref[...] = gb
        sum_ref[0:1, :] = jnp.sum(gb.astype(F32), axis=0, keepdims=True)
        sum_ref[1:2, :] = jnp.sum(cot, axis=0, keepdims=True)
        sum_ref[2:3, :] = jnp.sum(gn * hat, axis=0, keepdims=True)
        sum_ref[3:4, :] = jnp.sum(gn, axis=0, keepdims=True)
        sum_ref[4:8, :] = jnp.zeros((4, gn.shape[1]), F32)
        att = dot(wp_ref[...], gb_ref[...], NT).astype(BF)
        rows = g0_ref.shape[2]
        for s in range(g0_ref.shape[0]):
            y, g = s // slots, s % slots
            wide = HD + g12_ref.shape[1]
            piece = att[g * wide : (g + 1) * wide, y * rows : (y + 1) * rows]
            g0_ref[s] = piece[:HD]
            g12_ref[s] = piece[HD:]


def mlp_critical(slots, ahead, ending, tokens, cot, whole, params, b1):
    seqs, ahead_rows, rows_img = ahead.shape
    rows, features = tokens.shape
    blocks = (whole.shape[1] // features - 1) // 2
    hidden = blocks * features
    const2 = lambda k: (0, 0)
    const3 = lambda k: (0, 0, 0)
    return pl.pallas_call(
        partial(mlp_kernel, slots),
        grid=(blocks,),
        in_specs=[
            pl.BlockSpec(ahead.shape, const3),
            pl.BlockSpec(ending.shape, const3),
            pl.BlockSpec((rows, features), const2),
            pl.BlockSpec((rows, features), const2),
            pl.BlockSpec((features, features), lambda k: (0, k)),
            pl.BlockSpec((features, features), lambda k: (0, blocks + k)),
            pl.BlockSpec((features, features), lambda k: (0, 2 * blocks)),
            pl.BlockSpec((8, features), const2),
            pl.BlockSpec((1, features), lambda k: (0, k)),
        ],
        out_specs=[
            pl.BlockSpec((rows, features), lambda k: (0, k)),
            pl.BlockSpec((rows, features), lambda k: (0, k)),
            pl.BlockSpec((rows, features), const2),
            pl.BlockSpec((rows, features), const2),
            pl.BlockSpec((rows, features), const2),
            pl.BlockSpec((rows, features), const2),
            pl.BlockSpec((seqs, HD, rows_img), const3),
            pl.BlockSpec((seqs, ahead_rows, rows_img), const3),
            pl.BlockSpec((8, features), const2),
            pl.BlockSpec((1, features), lambda k: (0, k)),
        ],
        out_shape=[
            jax.ShapeDtypeStruct((rows, hidden), BF),
            jax.ShapeDtypeStruct((rows, hidden), BF),
            jax.ShapeDtypeStruct((rows, features), BF),
            jax.ShapeDtypeStruct((rows, features), F32),
            jax.ShapeDtypeStruct((rows, features), F32),
            jax.ShapeDtypeStruct((rows, features), BF),
            jax.ShapeDtypeStruct((seqs, HD, rows_img), BF),
            jax.ShapeDtypeStruct((seqs, ahead_rows, rows_img), BF),
            jax.ShapeDtypeStruct((8, features), F32),
            jax.ShapeDtypeStruct((1, hidden), F32),
        ],
        scratch_shapes=[
            pltpu.VMEM((rows, features), F32),
            pltpu.VMEM((rows, 1), F32),
            pltpu.VMEM((rows, features), F32),
        ],
        compiler_params=pltpu.CompilerParams(vmem_limit_bytes=60 * 2**20),
        cost_estimate=pl.CostEstimate(
            flops=2 * rows * features * (3 * hidden + 2 * features),
            bytes_accessed=40 * 2**20,
            transcendentals=2 * rows * hidden,
        ),
    )(ahead, ending, tokens, cot, whole, whole, whole, params, b1)


def grads_kernel(
    slots, blocks, ahead_ref, ending_ref, cot_ref, act_ref, gp_ref, n2_ref, gb_ref, mixed_ref,
    w2_ref, par_ref, out_ref, res_ref, n2T_ref, acc_ref
):
    k = pl.program_id(0)

    @pl.when(k == 0)
    def _():
        n2T_ref[...] = n2_ref[...].T
        acc_ref[...] = mixed_ref[...] + par_ref[3:4, :]

    @pl.when(k < blocks)
    def _():
        out_ref[...] = dot(n2T_ref[...], gp_ref[...], NN).astype(BF)

    @pl.when((k >= blocks) & (k < 2 * blocks))
    def _():
        act = act_ref[...]
        out_ref[...] = dot(act, cot_ref[...], TN).astype(BF)
        acc_ref[...] += dot(act, w2_ref[...], NN)

    @pl.when(k == 2 * blocks)
    def _():
        att = attended_rows(ahead_ref, ending_ref, slots)
        out_ref[...] = dot(att, gb_ref[...], NN).astype(BF)
        res_ref[...] = acc_ref[...].astype(BF)


def mlp_grads(slots, ahead, ending, cot, act, gp, n2, gb, mixed, whole, params):
    rows, features = cot.shape
    blocks = act.shape[1] // features
    const2 = lambda k: (0, 0)
    const3 = lambda k: (0, 0, 0)
    at1 = lambda k: jnp.minimum(k, blocks - 1)
    at2 = lambda k: jnp.clip(k - blocks, 0, blocks - 1)
    return pl.pallas_call(
        partial(grads_kernel, slots, blocks),
        grid=(2 * blocks + 1,),
        in_specs=[
            pl.BlockSpec(ahead.shape, const3),
            pl.BlockSpec(ending.shape, const3),
            pl.BlockSpec((rows, features), const2),
            pl.BlockSpec((rows, features), lambda k: (0, at2(k))),
            pl.BlockSpec((rows, features), lambda k: (0, at1(k))),
            pl.BlockSpec((rows, features), const2),
            pl.BlockSpec((rows, features), const2),
            pl.BlockSpec((rows, features), const2),
            pl.BlockSpec((features, features), lambda k: (0, blocks + at2(k))),
            pl.BlockSpec((8, features), const2),
        ],
        out_specs=[
            pl.BlockSpec((features, features), lambda k: (0, k)),
            pl.BlockSpec((rows, features), const2),
        ],
        out_shape=[
            jax.ShapeDtypeStruct((features, (2 * blocks + 1) * features), BF),
            jax.ShapeDtypeStruct((rows, features), BF),
        ],
        scratch_shapes=[pltpu.VMEM((features, rows), BF), pltpu.VMEM((rows, features), F32)],
        compiler_params=pltpu.CompilerParams(vmem_limit_bytes=56 * 2**20),
        cost_estimate=pl.CostEstimate(
            flops=2 * rows * features * features * (3 * blocks + 1),
            bytes_accessed=40 * 2**20,
            transcendentals=0,
        ),
    )(ahead, ending, cot, act, gp, n2, gb, mixed, whole, params)


def swap(block, bit, size):
    return lax.ppermute(block, "seq", [(i, i ^ bit) for i in range(size)])


def halves(values):
    hi = lax.reduce_precision(values, 8, 7)
    return [hi.astype(BF), (values - hi).astype(BF)]


def norm_parts(values):
    center = jnp.mean(values, axis=-1, keepdims=True)
    centered = values - center
    rate = lax.rsqrt(jnp.mean(centered * centered, axis=-1, keepdims=True) + EPS)
    return centered * rate, rate


def norm_back(grad, hat, rate, gain):
    u = grad * gain
    return rate * (
        u
        - jnp.mean(u, axis=-1, keepdims=True)
        - hat * jnp.mean(u * hat, axis=-1, keepdims=True)
    )


def body_heads(
    tokens,
    w_qkv,
    qv_bias,
    w_proj,
    proj_bias,
    w_fc1,
    fc1_bias,
    w_fc2,
    fc2_bias,
    norm_gains,
    norm_biases,
    rel_tables,
    cotangent,
):
    images, rows_img, features = tokens.shape
    dps, seqs = lax.axis_size("dp"), lax.axis_size("seq")
    size = dps * seqs
    slots = seqs // images
    per = HEADS // slots
    part = features // size
    wide = per * 3 * HD
    hidden = fc1_bias.shape[0] * size
    blocks = hidden // features
    here = lax.axis_index("seq")
    image, slot = here // slots, here % slots
    rows = images * rows_img

    own = lax.dynamic_index_in_dim(tokens, image, 0, keepdims=False)
    other = lax.dynamic_index_in_dim(tokens, 1 - image, 0, keepdims=False)
    small = jnp.concatenate(
        [
            qv_bias,
            proj_bias,
            fc1_bias,
            fc2_bias,
            norm_gains.reshape(-1),
            norm_biases.reshape(-1),
        ]
    )
    lengths = [2 * part, part, blocks * part, part, 2 * part, 2 * part]
    small = jnp.pad(small, (0, wide - small.shape[0])).reshape(1, 1, wide)
    by_head = w_qkv.reshape(part, 3, slots, per, HD)
    to_slots = by_head.transpose(2, 0, 3, 1, 4).reshape(slots, part, wide)
    to_slots = jnp.concatenate([to_slots, jnp.broadcast_to(small, (slots, 8, wide))], axis=1)
    cols = lax.all_to_all(jnp.tile(to_slots, (dps * images, 1, 1)), AXES, 0, 0, tiled=True)
    own_x, got = swap(own, 2, seqs), swap(other, 4, seqs)
    cols, own_x, got = lax.optimization_barrier((cols, own_x, got))
    got_x = swap(got, 2, seqs)
    w_cols = cols[:, :part].reshape(features, wide)
    smalls = cols[:, part]
    edges = [sum(lengths[:j]) for j in range(len(lengths) + 1)]
    cut = [smalls[:, a:b].astype(F32) for a, b in zip(edges[:-1], edges[1:])]
    bqv, bp, b2 = cut[0].reshape(-1), cut[1].reshape(-1), cut[3].reshape(-1)
    b1 = cut[2].reshape(size, blocks, part).transpose(1, 0, 2).reshape(-1)
    gains = cut[4].reshape(size, 2, part).transpose(1, 0, 2).reshape(2, features)
    shifts = cut[5].reshape(size, 2, part).transpose(1, 0, 2).reshape(2, features)

    full_bias = jnp.stack(
        [
            bqv[:features].reshape(slots, per, HD),
            jnp.zeros((slots, per, HD), F32),
            bqv[features:].reshape(slots, per, HD),
        ],
        axis=2,
    ).reshape(slots, wide)
    own_bias = lax.dynamic_index_in_dim(full_bias, slot, 0, keepdims=True)
    first_norm = jnp.stack([gains[0], shifts[0]])
    by_mask = [own, swap(own, 1, seqs), own_x, swap(own_x, 1, seqs), got, swap(got, 1, seqs)]
    held = normed_qkv(here, 0, seqs, by_mask, w_cols, first_norm, own_bias, [])
    by_mask = [got_x, swap(got_x, 1, seqs)]
    hat_all, *qkv = normed_qkv(here, 6, seqs, by_mask, w_cols, first_norm, own_bias, held)

    w1_local = w_fc1.reshape(part, size, blocks, part).transpose(0, 2, 1, 3).reshape(part, hidden)
    w2_local = w_fc2.reshape(blocks, part, features).transpose(1, 0, 2).reshape(part, hidden)
    wq_local = by_head.transpose(0, 3, 2, 1, 4).reshape(part, 3 * features)
    whole = jnp.concatenate([w1_local, w2_local, w_proj], axis=1)
    whole = lax.optimization_barrier((whole, got_x, held[1]))[0]
    whole = lax.all_gather(whole, AXES, axis=0, tiled=True)

    tab = mirror(rel_tables)
    kept, outs = [], []
    for p in range(per):
        out, *saved = heads_forward(qkv[p], tab)
        kept.append([qkv[p], tab, saved[1], saved[2], saved[0], hat_all])
        outs.append(out)
    ahead = lax.all_to_all(jnp.concatenate(outs[:-1], axis=1), "seq", 0, 0, tiled=True)
    ending = lax.all_to_all(outs[-1], "seq", 0, 0, tiled=True)
    wq_local = lax.optimization_barrier((wq_local, ahead, ending))[0]
    wq = lax.all_gather(wq_local, AXES, axis=0, tiled=True)

    params = jnp.concatenate(
        [jnp.stack([bp, gains[1], shifts[1], b2]), jnp.zeros((4, features), F32)]
    )
    cot = cotangent.reshape(rows, features)
    act, grad_pre, normed2, mixed, grad_mixed, grad_branch, send0, send12, sums, sum_b1 = mlp_critical(
        slots, ahead, ending, tokens.reshape(rows, features), cot, whole, params, b1[None]
    )
    first = lax.all_to_all(send0, "seq", 0, 0, tiled=True)
    others = lax.all_to_all(send12, "seq", 0, 0, tiled=True)
    grads, result = mlp_grads(
        slots, ahead, ending, cot, act, grad_pre, normed2, grad_branch, mixed, whole, params
    )
    result = result.reshape(tokens.shape)
    summed = lax.psum_scatter(grads, AXES, scatter_dimension=0, tiled=True).astype(F32)
    w_fc1_grad = (
        summed[:, :hidden].reshape(part, blocks, size, part).transpose(0, 2, 1, 3)
    ).reshape(part, hidden)
    w_fc2_grad = (
        summed[:, hidden : 2 * hidden].reshape(part, blocks, features).transpose(1, 0, 2)
    ).reshape(blocks * part, features)
    w_proj_grad = summed[:, 2 * hidden :]
    sum_b1 = sum_b1.reshape(blocks, size, part).transpose(1, 0, 2).reshape(size, blocks * part)
    early = jnp.concatenate(
        [
            sums[0].reshape(size, part),
            sum_b1,
            sums[1].reshape(size, part),
            sums[2].reshape(size, part),
            sums[3].reshape(size, part),
        ],
        axis=1,
    )

    grad_norm1 = jnp.zeros((images, rows_img, features), F32)
    table = jnp.zeros((16, 2 * GRID), F32)
    sent_on = []
    for p in range(per):
        do_p = first if p == 0 else others[:, (p - 1) * HD : p * HD]
        message, *far = heads_backward(dps, seqs, p == per - 1, *kept[p], do_p)
        message = lax.all_to_all(message, "seq", 0, 0, tiled=True)
        sent = message[:, : 3 * HD].reshape(images, slots * 3 * HD, rows_img)
        own_cols = wq[:, p * slots * 3 * HD : (p + 1) * slots * 3 * HD]
        grad_norm1 = grad_norm1 + jnp.einsum(
            "yht,ch->ytc", sent, own_cols, preferred_element_type=F32
        )
        base = message.shape[1] - 16
        pair = message[:, base:, : 4 * GRID].astype(F32)
        table = table + jnp.sum(pair[..., : 2 * GRID] + pair[..., 2 * GRID :], axis=0)
        if p < per - 1:
            moment = message[:, 3 * HD : base, : 6 * HD].astype(F32)
            moment = jnp.sum(moment.reshape(images, slots, dps // 2 * part, 6 * HD), axis=0)
            moment = moment.reshape(slots, dps // 2, part, 2, 3 * HD).transpose(3, 1, 0, 2, 4)
            total = message[:, base : base + 2, 4 * GRID : 4 * GRID + 3 * HD].astype(F32)
            total = jnp.sum(total.reshape(images, slots, 2, 3 * HD), axis=(0, 2))
            total = jnp.pad(jnp.stack(halves(total), axis=1), ((0, 0), (0, 6), (0, 0)))
            total = jnp.broadcast_to(total, (dps,) + total.shape)
            by_owner = jnp.concatenate(
                [moment.reshape(dps, slots, part, 3 * HD).astype(BF), total], axis=2
            )
            sent_on.append(by_owner)
    sent_on = jnp.stack(sent_on, axis=1)
    level = lax.axis_index("dp")
    products = lax.dynamic_index_in_dim(sent_on, level, 0, keepdims=False).astype(F32)
    for m in range(1, dps):
        block = lax.dynamic_index_in_dim(sent_on, level ^ m, 0, keepdims=False)
        block = lax.ppermute(block, "dp", [(i, i ^ m) for i in range(dps)])
        products = products + block.astype(F32)
    pieces = jnp.concatenate(halves(table), axis=1)
    pieces = jnp.broadcast_to(pieces, (size,) + pieces.shape)
    sums = jnp.stack(halves(early), axis=1)
    sums = jnp.pad(sums, ((0, 0), (0, 6), (0, 4 * GRID - 8 * part)))
    far = jnp.concatenate([far[0], sums, pieces], axis=1)
    far = lax.all_to_all(far, AXES, 0, 0, tiled=True)
    final = far[:, : part + 8, : 3 * HD].astype(F32).reshape(dps * images, slots, part + 8, 3 * HD)
    products = jnp.concatenate([products, jnp.sum(final, axis=0)[None]])
    moments = products[:, :, :part].swapaxes(0, 1)
    totals = (products[:, :, part] + products[:, :, part + 1]).swapaxes(0, 1)
    bundle = jnp.sum(far[:, part + 8 : part + 10, : 8 * part].astype(F32), axis=(0, 1))
    pair = far[:, part + 16 :].astype(F32)
    pair = (pair[..., : 2 * GRID] + pair[..., 2 * GRID :]).reshape(dps, -1, 2 * GRID)
    table = jnp.sum(pair, axis=0).reshape(2, HD, 2 * GRID)
    rel_tables_grad = unmirror(table.swapaxes(1, 2))

    moment = moments.reshape(slots, per, part, 3, HD)
    moment = moment.transpose(2, 3, 0, 1, 4).reshape(part, 3 * features)
    total = totals.reshape(slots, per, 3, HD)
    total = total.transpose(2, 0, 1, 3).reshape(3 * features)
    own_gain, own_shift = norm_gains[0].astype(F32), norm_biases[0].astype(F32)
    w_qkv_grad = own_gain[:, None] * moment + own_shift[:, None] * total
    w_own = w_qkv.astype(F32)
    gain0, shift0 = jnp.sum(w_own * moment, axis=1), jnp.sum(w_own * total, axis=1)
    device = lax.axis_index("dp") * seqs + here
    total = jnp.concatenate([total[:features], total[2 * features :]]).reshape(size, 2 * part)
    qv_bias_grad = lax.dynamic_index_in_dim(total, device, 0, keepdims=False)

    hat1, rate1 = norm_parts(tokens.astype(F32))
    tokens_grad = grad_mixed.reshape(tokens.shape) + norm_back(grad_norm1, hat1, rate1, gains[0])
    tokens_grad = tokens_grad.astype(BF)
    ends = [part * end for end in [0, 1, 1 + blocks, 2 + blocks, 3 + blocks, 4 + blocks]]
    bundle = [bundle[a:b] for a, b in zip(ends[:-1], ends[1:])]
    proj_bias_grad, fc1_bias_grad, fc2_bias_grad, gain1, shift1 = bundle
    norm_gains_grad = jnp.stack([gain0, gain1])
    norm_biases_grad = jnp.stack([shift0, shift1])
    return (
        result,
        tokens_grad,
        w_qkv_grad,
        qv_bias_grad,
        w_proj_grad,
        proj_bias_grad,
        w_fc1_grad,
        fc1_bias_grad,
        w_fc2_grad,
        fc2_bias_grad,
        norm_gains_grad,
        norm_biases_grad,
        rel_tables_grad,
    )


def layer_norm(values, gain, shift):
    center = jnp.mean(values, axis=-1, keepdims=True)
    centered = values - center
    spread = jnp.mean(centered * centered, axis=-1, keepdims=True)
    return centered * lax.rsqrt(spread + EPS) * gain + shift


def fetch_each(weights):
    return (
        lax.all_gather(weights[0], ("dp", "seq"), axis=0, tiled=True),
        lax.all_gather(weights[1], ("dp", "seq"), axis=0, tiled=True),
        lax.all_gather(weights[2], ("dp", "seq"), axis=0, tiled=True),
        lax.all_gather(weights[3], ("dp", "seq"), axis=0, tiled=True),
        lax.all_gather(weights[4], ("dp", "seq"), axis=0, tiled=True),
        lax.all_gather(weights[5], ("dp", "seq"), axis=0, tiled=True),
        lax.all_gather(weights[6], ("dp", "seq"), axis=0, tiled=True),
        lax.all_gather(weights[7], ("dp", "seq"), axis=0, tiled=True),
        lax.all_gather(weights[8], ("dp", "seq"), axis=1, tiled=True),
        lax.all_gather(weights[9], ("dp", "seq"), axis=1, tiled=True),
    )


def position_rows(tables, rows_img):
    beginning = lax.axis_index("seq") * rows_img
    tokens_at = beginning + jnp.arange(rows_img, dtype=jnp.int32)
    offsets = jnp.arange(GRID, dtype=jnp.int32)
    entries = jnp.arange(TABLE, dtype=jnp.int32)
    row_index = tokens_at[:, None] // GRID - offsets[None, :] + GRID - 1
    col_index = tokens_at[:, None] % GRID - offsets[None, :] + GRID - 1
    row_hot = (row_index[:, :, None] == entries[None, None, :]).astype(jnp.float32)
    col_hot = (col_index[:, :, None] == entries[None, None, :]).astype(jnp.float32)
    tables_f = tables.astype(jnp.float32)
    rel_rows = jnp.einsum("rkt,tc->rkc", row_hot, tables_f[0], precision=HIGH)
    rel_cols = jnp.einsum("rkt,tc->rkc", col_hot, tables_f[1], precision=HIGH)
    return (row_hot, col_hot, rel_rows, rel_cols)


def score_block(queries, keys_all, rows_low, cols_low):
    rows_img = queries.shape[0]
    product = jnp.einsum(
        "rhc,nhc->hrn", queries, keys_all, preferred_element_type=jnp.float32
    ) * HD ** (-0.5)
    bias_rows = jnp.einsum("rhc,rkc->hrk", queries, rows_low, preferred_element_type=jnp.float32)
    bias_cols = jnp.einsum("rhc,rkc->hrk", queries, cols_low, preferred_element_type=jnp.float32)
    joined = (
        product.reshape(HEADS, rows_img, GRID, GRID)
        + bias_rows[:, :, :, None]
        + bias_cols[:, :, None, :]
    )
    return joined.reshape(HEADS, rows_img, GRID * GRID)


def attend_forward(qkv_img, kv_pair, rows_low, cols_low):
    rows_img, triple = qkv_img.shape
    features = triple // 3
    queries = qkv_img[:, :features].reshape(rows_img, HEADS, HD)
    keys_all = kv_pair[0].reshape(-1, HEADS, HD)
    values_all = kv_pair[1].reshape(-1, HEADS, HD)
    scores = score_block(queries, keys_all, rows_low, cols_low)
    largest = jnp.max(scores, axis=-1, keepdims=True)
    shifted = jnp.exp(scores - largest)
    totals = jnp.sum(shifted, axis=-1, keepdims=True)
    probs_low = (shifted / totals).astype(jnp.bfloat16)
    attended = jnp.einsum("hrn,nhc->rhc", probs_low, values_all, preferred_element_type=jnp.float32)
    log_totals = largest[..., 0] + jnp.log(totals[..., 0])
    return (attended.reshape(rows_img, features).astype(jnp.bfloat16), log_totals)


def attend_backward(qkv_img, log_totals, grad_att, kv_pair, rel_rows, rel_cols, rows_low, cols_low):
    rows_img, triple = qkv_img.shape
    features = triple // 3
    scale = HD ** (-0.5)
    queries = qkv_img[:, :features].reshape(rows_img, HEADS, HD)
    keys_all = kv_pair[0].reshape(-1, HEADS, HD)
    values_all = kv_pair[1].reshape(-1, HEADS, HD)
    scores = score_block(queries, keys_all, rows_low, cols_low)
    probs = jnp.exp(scores - log_totals[..., None])
    probs_low = probs.astype(jnp.bfloat16)
    grad_heads = grad_att.reshape(rows_img, HEADS, HD)
    grad_probs = jnp.einsum(
        "rhc,nhc->hrn", grad_heads, values_all, preferred_element_type=jnp.float32
    )
    inner_sum = jnp.sum(probs * grad_probs, axis=-1, keepdims=True)
    grad_scores = (probs * (grad_probs - inner_sum)).astype(jnp.bfloat16)
    grad_queries = (
        jnp.einsum("hrn,nhc->rhc", grad_scores, keys_all, preferred_element_type=jnp.float32)
        * scale
    )
    grid_scores = grad_scores.reshape(HEADS, rows_img, GRID, GRID)
    grad_rows = jnp.sum(grid_scores, axis=3, dtype=jnp.float32)
    grad_cols = jnp.sum(grid_scores, axis=2, dtype=jnp.float32)
    grad_queries = grad_queries + jnp.einsum("hrk,rkc->rhc", grad_rows, rel_rows, precision=HIGH)
    grad_queries = grad_queries + jnp.einsum("hrk,rkc->rhc", grad_cols, rel_cols, precision=HIGH)
    query_f = queries.astype(jnp.float32)
    table_rows = jnp.einsum("hrk,rhc->rkc", grad_rows, query_f, precision=HIGH)
    table_cols = jnp.einsum("hrk,rhc->rkc", grad_cols, query_f, precision=HIGH)
    length = lax.axis_size("seq") * rows_img
    grad_keys = (
        jnp.einsum("hrn,rhc->nhc", grad_scores, queries, preferred_element_type=jnp.float32) * scale
    )
    grad_values = jnp.einsum(
        "hrn,rhc->nhc", probs_low, grad_heads, preferred_element_type=jnp.float32
    )
    key_grads = lax.psum_scatter(
        jnp.concatenate(
            [grad_keys.reshape(length, features), grad_values.reshape(length, features)], axis=1
        ),
        "seq",
        scatter_dimension=0,
        tiled=True,
    )
    grad_qkv = jnp.concatenate(
        [grad_queries.reshape(rows_img, features), key_grads], axis=1
    ).astype(jnp.bfloat16)
    return (grad_qkv, table_rows, table_cols)


def body(
    tokens,
    w_qkv,
    qv_bias,
    w_proj,
    proj_bias,
    w_fc1,
    fc1_bias,
    w_fc2,
    fc2_bias,
    norm_gains,
    norm_biases,
    rel_tables,
    cotangent,
):
    images, rows_img, features = tokens.shape
    per_batch = images // MB
    weights = (
        w_qkv,
        qv_bias,
        w_proj,
        proj_bias,
        w_fc1,
        fc1_bias,
        w_fc2,
        fc2_bias,
        norm_gains,
        norm_biases,
    )
    row_hot, col_hot, rel_rows, rel_cols = position_rows(rel_tables, rows_img)
    rows_low = rel_rows.astype(jnp.bfloat16)
    cols_low = rel_cols.astype(jnp.bfloat16)
    stored = []
    outputs = []
    for batch_index in range(MB):
        gathered = fetch_each(weights)
        (
            wq_full,
            bqv_full,
            wp_full,
            bp_full,
            w1_full,
            b1_full,
            w2_full,
            b2_full,
            gains_full,
            shifts_full,
        ) = gathered
        gains_f = gains_full.astype(jnp.float32)
        shifts_f = shifts_full.astype(jnp.float32)
        inputs = (
            tokens[batch_index * per_batch : (batch_index + 1) * per_batch]
            .astype(jnp.float32)
            .reshape(-1, features)
        )
        normed1 = layer_norm(inputs, gains_f[0], shifts_f[0]).astype(jnp.bfloat16)
        full_bias = jnp.concatenate(
            [bqv_full[:features], jnp.zeros((features,), bqv_full.dtype), bqv_full[features:]]
        ).astype(jnp.float32)
        qkv = (jnp.dot(normed1, wq_full, preferred_element_type=jnp.float32) + full_bias).astype(
            jnp.bfloat16
        )
        qkv_images = qkv.reshape(per_batch, rows_img, 3 * features)

        def forward_image(carried, qkv_img):
            kv_pair = (
                lax.all_gather(qkv_img[:, features : 2 * features], "seq", axis=0, tiled=True),
                lax.all_gather(qkv_img[:, 2 * features :], "seq", axis=0, tiled=True),
            )
            attended_img, log_totals = attend_forward(qkv_img, kv_pair, rows_low, cols_low)
            return (carried, (attended_img, log_totals))

        results = lax.scan(forward_image, jnp.zeros((), jnp.float32), qkv_images)[1]
        attended = results[0].reshape(-1, features)
        mixed = (
            inputs
            + jnp.dot(attended, wp_full, preferred_element_type=jnp.float32)
            + bp_full.astype(jnp.float32)
        )
        normed2 = layer_norm(mixed, gains_f[1], shifts_f[1]).astype(jnp.bfloat16)
        pre = jnp.dot(normed2, w1_full, preferred_element_type=jnp.float32) + b1_full.astype(
            jnp.float32
        )
        activated = jax.nn.gelu(pre, approximate=False).astype(jnp.bfloat16)
        block_out = (
            mixed
            + jnp.dot(activated, w2_full, preferred_element_type=jnp.float32)
            + b2_full.astype(jnp.float32)
        )
        outputs.append(block_out.astype(jnp.bfloat16).reshape(per_batch, rows_img, features))
        stored.append((normed1, qkv_images, results, mixed, normed2, pre, activated))
    gradients = [jnp.zeros(array.shape, jnp.float32) for array in gathered]
    table_rows_sum = jnp.zeros((rows_img, GRID, HD), jnp.float32)
    table_cols_sum = jnp.zeros((rows_img, GRID, HD), jnp.float32)
    input_grads = []
    for batch_index in range(MB):
        gathered = fetch_each(weights)
        (
            wq_full,
            bqv_full,
            wp_full,
            bp_full,
            w1_full,
            b1_full,
            w2_full,
            b2_full,
            gains_full,
            shifts_full,
        ) = gathered
        gains_f = gains_full.astype(jnp.float32)
        shifts_f = shifts_full.astype(jnp.float32)
        normed1, qkv_images, results, mixed, normed2, pre, activated = stored[batch_index]
        inputs = (
            tokens[batch_index * per_batch : (batch_index + 1) * per_batch]
            .astype(jnp.float32)
            .reshape(-1, features)
        )
        grad_out = cotangent[batch_index * per_batch : (batch_index + 1) * per_batch].reshape(
            -1, features
        )
        grad_out_f = grad_out.astype(jnp.float32)
        grad_w2 = jnp.dot(activated.T, grad_out, preferred_element_type=jnp.float32)
        grad_b2 = jnp.sum(grad_out_f, axis=0)
        grad_act = jnp.dot(grad_out, w2_full.T, preferred_element_type=jnp.float32)
        _, gelu_pull = jax.vjp(partial(jax.nn.gelu, approximate=False), pre)
        grad_pre = gelu_pull(grad_act)[0].astype(jnp.bfloat16)
        grad_w1 = jnp.dot(normed2.T, grad_pre, preferred_element_type=jnp.float32)
        grad_b1 = jnp.sum(grad_pre, axis=0, dtype=jnp.float32)
        grad_norm2 = jnp.dot(grad_pre, w1_full.T, preferred_element_type=jnp.float32)
        _, norm_pull2 = jax.vjp(layer_norm, mixed, gains_f[1], shifts_f[1])
        grad_mix_norm, grad_gain2, grad_shift2 = norm_pull2(grad_norm2)
        grad_mixed = grad_out_f + grad_mix_norm
        grad_branch = grad_mixed.astype(jnp.bfloat16)
        attended = results[0].reshape(-1, features)
        grad_wp = jnp.dot(attended.T, grad_branch, preferred_element_type=jnp.float32)
        grad_bp = jnp.sum(grad_branch, axis=0, dtype=jnp.float32)
        grad_att = jnp.dot(grad_branch, wp_full.T, preferred_element_type=jnp.float32).astype(
            jnp.bfloat16
        )
        grad_images = grad_att.reshape(per_batch, rows_img, features)
        image_inputs = (qkv_images, results[1], grad_images)

        def backward_image(carried, pieces):
            kv_pair = (
                lax.all_gather(pieces[0][:, features : 2 * features], "seq", axis=0, tiled=True),
                lax.all_gather(pieces[0][:, 2 * features :], "seq", axis=0, tiled=True),
            )
            grad_qkv_img, table_rows, table_cols = attend_backward(
                pieces[0], pieces[1], pieces[2], kv_pair, rel_rows, rel_cols, rows_low, cols_low
            )
            return ((carried[0] + table_rows, carried[1] + table_cols), grad_qkv_img)

        (table_rows_sum, table_cols_sum), grad_qkv_all = lax.scan(
            backward_image, (table_rows_sum, table_cols_sum), image_inputs
        )
        grad_qkv = grad_qkv_all.reshape(-1, 3 * features)
        grad_wq = jnp.dot(normed1.T, grad_qkv, preferred_element_type=jnp.float32)
        grad_bqv = jnp.concatenate(
            [
                jnp.sum(grad_qkv[:, :features], axis=0, dtype=jnp.float32),
                jnp.sum(grad_qkv[:, 2 * features :], axis=0, dtype=jnp.float32),
            ]
        )
        grad_norm1 = jnp.dot(grad_qkv, wq_full.T, preferred_element_type=jnp.float32)
        _, norm_pull1 = jax.vjp(layer_norm, inputs, gains_f[0], shifts_f[0])
        grad_in_norm, grad_gain1, grad_shift1 = norm_pull1(grad_norm1)
        input_grads.append(
            (grad_mixed + grad_in_norm).astype(jnp.bfloat16).reshape(per_batch, rows_img, features)
        )
        updates = (
            grad_wq,
            grad_bqv,
            grad_wp,
            grad_bp,
            grad_w1,
            grad_b1,
            grad_w2,
            grad_b2,
            jnp.stack([grad_gain1, grad_gain2]),
            jnp.stack([grad_shift1, grad_shift2]),
        )
        gradients = [before + update for before, update in zip(gradients, updates)]
    summed = (
        lax.psum_scatter(gradients[0], ("dp", "seq"), scatter_dimension=0, tiled=True),
        lax.psum_scatter(gradients[1], ("dp", "seq"), scatter_dimension=0, tiled=True),
        lax.psum_scatter(gradients[2], ("dp", "seq"), scatter_dimension=0, tiled=True),
        lax.psum_scatter(gradients[3], ("dp", "seq"), scatter_dimension=0, tiled=True),
        lax.psum_scatter(gradients[4], ("dp", "seq"), scatter_dimension=0, tiled=True),
        lax.psum_scatter(gradients[5], ("dp", "seq"), scatter_dimension=0, tiled=True),
        lax.psum_scatter(gradients[6], ("dp", "seq"), scatter_dimension=0, tiled=True),
        lax.psum_scatter(gradients[7], ("dp", "seq"), scatter_dimension=0, tiled=True),
        lax.psum_scatter(gradients[8], ("dp", "seq"), scatter_dimension=1, tiled=True),
        lax.psum_scatter(gradients[9], ("dp", "seq"), scatter_dimension=1, tiled=True),
    )
    table_local = jnp.stack(
        [
            jnp.einsum("rkt,rkc->tc", row_hot, table_rows_sum, precision=HIGH),
            jnp.einsum("rkt,rkc->tc", col_hot, table_cols_sum, precision=HIGH),
        ]
    )
    table_grad = lax.psum(table_local, ("dp", "seq"))
    return (
        jnp.concatenate(outputs, axis=0),
        jnp.concatenate(input_grads, axis=0),
        summed[0],
        summed[1],
        summed[2],
        summed[3],
        summed[4],
        summed[5],
        summed[6],
        summed[7],
        summed[8],
        summed[9],
        table_grad,
    )


def solution(mesh):
    placed = (
        P("dp", "seq", None),
        P(("dp", "seq"), None),
        P(("dp", "seq")),
        P(("dp", "seq"), None),
        P(("dp", "seq")),
        P(("dp", "seq"), None),
        P(("dp", "seq")),
        P(("dp", "seq"), None),
        P(("dp", "seq")),
        P(None, ("dp", "seq")),
        P(None, ("dp", "seq")),
        P(),
        P("dp", "seq", None),
    )
    seqs, images = mesh.shape["seq"], IMAGES // mesh.shape["dp"]
    by_heads = (mesh.shape["dp"], seqs, images) == (4, 8, 2)
    return jax.shard_map(
        body_heads if by_heads else body,
        mesh=mesh,
        in_specs=placed,
        out_specs=(
            P("dp", "seq", None),
            P("dp", "seq", None),
            P(("dp", "seq"), None),
            P(("dp", "seq")),
            P(("dp", "seq"), None),
            P(("dp", "seq")),
            P(("dp", "seq"), None),
            P(("dp", "seq")),
            P(("dp", "seq"), None),
            P(("dp", "seq")),
            P(None, ("dp", "seq")),
            P(None, ("dp", "seq")),
            P(),
        ),
        check_vma=False,
    )
```

```python
from functools import partial
import math

import jax
import jax.numpy as jnp
from jax import lax
from jax.experimental import pallas as pl
from jax.experimental.pallas import tpu as pltpu
from jax.sharding import PartitionSpec as P

HEADS = 12
HD = 64
GRID = 64
MB = 2
TABLE = 127


EPS = 1e-06
HIGH = lax.Precision.HIGHEST
IMAGES = 8
AXES = ("dp", "seq")

TB = 1024
CK = 512
ROWS = CK // GRID
LOG2E = 1.4426950408889634
NN = (((1,), (0,)), ((), ()))
NT = (((1,), (1,)), ((), ()))
TN = (((0,), (0,)), ((), ()))
BF = jnp.bfloat16
F32 = jnp.float32


def dot(a, b, dims):
    return lax.dot_general(a, b, dims, preferred_element_type=F32)


def col_hot(n):
    key = lax.broadcasted_iota(jnp.int32, (n, GRID), 0) & (GRID - 1)
    col = lax.broadcasted_iota(jnp.int32, (n, GRID), 1)
    return (key == col).astype(F32)


def fwd_kernel(n_chunks, qkv_ref, tab_ref, *refs):
    oT_ref, oTf_ref, p_ref, f_ref, kaug, vta, br_ref, qa_ref = refs[-8:]
    i = pl.program_id(0)
    tg = TB // GRID

    @pl.when(i == 0)
    def _():
        for c in range(n_chunks):
            rows = pl.ds(c * CK, CK)
            k = qkv_ref[rows, HD : 2 * HD].astype(F32)
            pair = jnp.concatenate([k, col_hot(CK)], axis=1).astype(BF)
            kaug[rows, : 2 * HD] = pair
            kaug[rows, 2 * HD :] = pair
            vT = qkv_ref[rows, 2 * HD :].astype(F32).T
            vta[0:HD, rows] = vT.astype(BF)
            one = lax.broadcasted_iota(jnp.int32, (16, CK), 0) == 0
            vta[HD : HD + 16, rows] = one.astype(F32).astype(BF)

    q = qkv_ref[pl.ds(pl.multiple_of(i * TB, TB), TB), :HD]
    gr = dot(q, tab_ref[0], NT) * LOG2E
    gc = dot(q, tab_ref[1], NT) * LOG2E
    brs, bcs = [], []
    for g in range(tg):
        sl = slice(g * GRID, (g + 1) * GRID)
        brs.append(pltpu.roll(gr[sl], i * tg + g, 1))
        bcs.append(pltpu.roll(gc[sl], 0, 1, stride=1, stride_axis=0))
    br = jnp.concatenate(brs, axis=0)
    bc = jnp.concatenate(bcs, axis=0)
    qs = q.astype(F32) * (HD ** -0.5 * LOG2E)
    cat = jnp.concatenate([qs, bc[:, :GRID]], axis=1).T
    hi = cat.astype(BF)
    lo = (cat - hi.astype(F32)).astype(BF)
    qa_ref[...] = jnp.concatenate([hi, lo], axis=0)
    br_ref[...] = br.T[:GRID]
    qa = qa_ref[...]

    def scores(c):
        return dot(kaug[c * CK : (c + 1) * CK, :], qa, NN)

    def soften(c, s):
        s = s.reshape(ROWS, GRID, TB)
        b8 = br_ref[c * ROWS : (c + 1) * ROWS, :]
        top = jnp.max(jnp.max(s, axis=1) + b8, axis=0, keepdims=True)
        p = jnp.exp2(s - (top - b8)[:, None, :]).astype(BF).reshape(CK, TB)
        p_ref[0, c * CK : (c + 1) * CK, :] = p
        return top, p

    def gather(m, acc, c, top, p):
        out = dot(vta[:, c * CK : (c + 1) * CK], p, NN)
        new = jnp.maximum(m, top)
        return new, acc * jnp.exp2(m - new) + out * jnp.exp2(top - new)

    m = jnp.full((1, TB), -jnp.inf, F32)
    acc = jnp.zeros((HD + 16, TB), F32)
    tops = []
    s, before = scores(0), None
    for c in range(n_chunks):
        following = scores(c + 1) if c + 1 < n_chunks else None
        if before is not None:
            m, acc = gather(m, acc, c - 1, *before)
        before, s = soften(c, s), following
        tops.append(before[0])
    m, acc = gather(m, acc, n_chunks - 1, *before)
    total = acc[HD : HD + 1]
    out = acc[:HD] / total
    for j in range(TB // CK):
        oT_ref[j] = out[:, j * CK : (j + 1) * CK].astype(BF)
    oTf_ref[...] = out
    f_ref[...] = jnp.exp2(jnp.concatenate(tops, axis=0) - (m + jnp.log2(total)))


def heads_forward(qkv, tab, places=1, place=0, before=()):
    n = qkv.shape[0]
    steps, chunks, side = n // TB, n // CK, TB // CK
    return pl.pallas_call(
        partial(fwd_kernel, chunks),
        grid=(steps,),
        in_specs=[
            pl.BlockSpec((n, 3 * HD), lambda i: (0, 0)),
            pl.BlockSpec((2, 2 * GRID, HD), lambda i: (0, 0, 0)),
        ]
        + [pl.BlockSpec(memory_space=pl.ANY)] * len(before),
        out_specs=[
            pl.BlockSpec((side, HD, CK), lambda i: (i, place, 0)),
            pl.BlockSpec((HD, TB), lambda i: (0, i)),
            pl.BlockSpec((1, n, TB), lambda i: (i, 0, 0)),
            pl.BlockSpec((chunks, TB), lambda i: (0, i)),
        ],
        out_shape=[
            jax.ShapeDtypeStruct((chunks, places * HD, CK), BF),
            jax.ShapeDtypeStruct((HD, n), F32),
            jax.ShapeDtypeStruct((steps, n, TB), BF),
            jax.ShapeDtypeStruct((chunks, n), F32),
        ],
        scratch_shapes=[
            pltpu.VMEM((n, 4 * HD), BF),
            pltpu.VMEM((HD + 16, n), BF),
            pltpu.VMEM((GRID, TB), F32),
            pltpu.VMEM((4 * HD, TB), BF),
        ],
        compiler_params=pltpu.CompilerParams(vmem_limit_bytes=56 * 2**20),
        cost_estimate=pl.CostEstimate(
            flops=4 * n * n * 4 * HD, bytes_accessed=48 * 2**20, transcendentals=n * n
        ),
        input_output_aliases={2 + j: 0 for j in range(len(before))},
    )(qkv, tab, *before)


def bwd_kernel(
    n_chunks, dps, seqs, qkv_ref, tab_ref, p_ref, f_ref, oTf_ref, doT_ref, x_hbm, msg_ref, *refs
):
    *far_ref, vaug, kta, dkv, dqa, dtab_ref, x_ref, x_sem = refs
    i = pl.program_id(0)
    tg, side = TB // GRID, TB // CK
    n_steps = pl.num_programs(0)
    fetch = pltpu.make_async_copy(x_hbm, x_ref, x_sem)

    @pl.when(i == 0)
    def _():
        for c in range(n_chunks):
            rows = pl.ds(c * CK, CK)
            k = qkv_ref[rows, HD : 2 * HD].astype(F32)
            both = jnp.concatenate([k, col_hot(CK)], axis=1).T
            kta[0 : 2 * HD, rows] = both.astype(BF)
            key = lax.broadcasted_iota(jnp.int32, (16, CK), 1) >> 6
            hot = lax.broadcasted_iota(jnp.int32, (16, CK), 0) == key
            kta[2 * HD : 2 * HD + 16, rows] = hot.astype(F32).astype(BF)
            v = qkv_ref[rows, 2 * HD :].astype(F32)
            lane = lax.broadcasted_iota(jnp.int32, (CK, HD), 1)
            vaug[rows, :] = jnp.concatenate([v, (lane < 3).astype(F32)], axis=1).astype(BF)
            dkv[rows, :] = jnp.zeros((CK, 2 * HD), F32)
        dtab_ref[...] = jnp.zeros_like(dtab_ref)
        fetch.start()

    q = qkv_ref[pl.ds(pl.multiple_of(i * TB, TB), TB), :HD]
    doT = jnp.concatenate([doT_ref[j].astype(F32) for j in range(side)], axis=1)
    delta = -jnp.sum(doT * oTf_ref[...], axis=0, keepdims=True)
    d1 = delta.astype(BF).astype(F32)
    d2 = (delta - d1).astype(BF).astype(F32)
    pad = jnp.concatenate([d1, d2, delta - d1 - d2, jnp.zeros((HD - 3, TB), F32)], axis=0)
    doa = jnp.concatenate([doT, pad], axis=0).astype(BF)
    do = jnp.concatenate([doT, jnp.zeros((HD, TB), F32)], axis=0).T
    qz = jnp.concatenate([jnp.zeros((TB, HD), F32), q.astype(F32)], axis=1)
    doq = jnp.concatenate([do, qz], axis=0).astype(BF)
    dqa[...] = jnp.zeros_like(dqa)

    def grad_probs(c):
        return dot(vaug[c * CK : (c + 1) * CK, :], doa, NN)

    def grad_scores(c, dp):
        p = p_ref[0, c * CK : (c + 1) * CK, :].astype(F32) * f_ref[c : c + 1, :]
        return jnp.concatenate([p.astype(BF), (p * dp).astype(BF)], axis=1)

    def gather(c, pd):
        rows = slice(c * CK, (c + 1) * CK)
        dkv[rows, :] += dot(pd, doq, NN)
        g = dot(kta[:, rows], pd[:, TB:], NN)
        dqa[0 : 2 * HD, :] += g[: 2 * HD]
        dqa[2 * HD + c * ROWS : 2 * HD + (c + 1) * ROWS, :] = g[2 * HD : 2 * HD + ROWS]

    dp, before = grad_probs(0), None
    for c in range(n_chunks):
        following = grad_probs(c + 1) if c + 1 < n_chunks else None
        if before is not None:
            gather(c - 1, before)
        before, dp = grad_scores(c, dp), following
    gather(n_chunks - 1, before)

    grads = dqa[HD : 3 * HD, :].T
    lane = lax.broadcasted_iota(jnp.int32, (TB, 2 * GRID), 1)
    gcol = jnp.where(lane < GRID, grads, 0.0)
    grow = jnp.where(lane >= GRID, grads, 0.0)
    rs, cs = [], []
    col = lax.broadcasted_iota(jnp.int32, (GRID, 2 * GRID), 0)
    for g in range(tg):
        sl = slice(g * GRID, (g + 1) * GRID)
        rs.append(pltpu.roll(grow[sl], GRID - (i * tg + g), 1))
        x = gcol[sl]
        for bit in range(6):
            x = jnp.where((col >> bit) & 1 == 1, pltpu.roll(x, 2 * GRID - (1 << bit), 1), x)
        cs.append(x)
    drow = jnp.concatenate(rs, axis=0).astype(BF)
    dcol = jnp.concatenate(cs, axis=0).astype(BF)
    dq = dqa[:HD, :] * HD ** -0.5
    dq = dq + dot(tab_ref[0], drow, (((0,), (1,)), ((), ())))
    dq = dq + dot(tab_ref[1], dcol, (((0,), (1,)), ((), ())))
    for j in range(side):
        msg_ref[i * side + j, 0:HD, :] = dq[:, j * CK : (j + 1) * CK].astype(BF)
    dtab_ref[0:HD, :] += dot(q, drow, TN)
    dtab_ref[HD : 2 * HD, :] += dot(q, dcol, TN)

    @pl.when(i == n_steps - 1)
    def _():
        for c in range(n_chunks):
            both = dkv[c * CK : (c + 1) * CK, :].T
            msg_ref[c, HD : 2 * HD, :] = (both[HD:] * HD ** -0.5).astype(BF)
            msg_ref[c, 2 * HD : 3 * HD, :] = both[:HD].astype(BF)
        fetch.wait()
        all_grads = jnp.concatenate([msg_ref[c, : 3 * HD, :] for c in range(n_chunks)], axis=1)
        moment = dot(all_grads, x_ref[...], NN).T
        total = dot(jnp.ones((8, all_grads.shape[1]), BF), all_grads, NT)
        hi = total.astype(BF).astype(F32)
        row = lax.broadcasted_iota(jnp.int32, total.shape, 0)
        ending = jnp.where(row == 0, hi, jnp.where(row == 1, total - hi, 0.0))
        part = moment.shape[0] // (dps * seqs)
        half = dps // 2
        base = msg_ref.shape[1] - 16
        for d in range(dps * seqs if far_ref else 0):
            piece = jnp.concatenate([moment[d * part : (d + 1) * part], ending], axis=0)
            fill = jnp.zeros((part + 8, HD), F32)
            far_ref[0][d] = jnp.concatenate([piece, fill], axis=1).astype(BF)
        for s in range(seqs):
            if not far_ref:
                sides = []
                for side in range(2):
                    tops = [(d * seqs + s) * part for d in range(side * half, (side + 1) * half)]
                    sides.append(jnp.concatenate([moment[t : t + part] for t in tops], axis=0))
                sides.append(jnp.zeros((half * part, CK - 6 * HD), F32))
                msg_ref[s, 3 * HD : base, :] = jnp.concatenate(sides, axis=1).astype(BF)
            piece = dtab_ref[s * 16 : (s + 1) * 16, :]
            hi = piece.astype(BF).astype(F32)
            sums = jnp.concatenate([ending, jnp.zeros((8, 3 * HD), F32)], axis=0)
            fill = jnp.zeros((16, CK - 7 * HD), F32)
            row = jnp.concatenate([hi, piece - hi, sums, fill], axis=1)
            msg_ref[s, base:, :] = row.astype(BF)


def heads_backward(dps, seqs, p, last, qkv, tab, probs, factors, oTf, x, doT):
    n, features = x.shape
    steps, chunks, side = n // TB, n // CK, TB // CK
    part = features // (dps * seqs)
    shapes = [(chunks, 3 * HD + 16 + (0 if last else dps // 2 * part), CK)]
    if last:
        shapes.append((dps * seqs, part + 8, 4 * HD))
    return pl.pallas_call(
        partial(bwd_kernel, n // CK, dps, seqs),
        grid=(steps,),
        in_specs=[
            pl.BlockSpec((n, 3 * HD), lambda i: (0, 0)),
            pl.BlockSpec((2, 2 * GRID, HD), lambda i: (0, 0, 0)),
            pl.BlockSpec((1, n, TB), lambda i: (i, 0, 0)),
            pl.BlockSpec((chunks, TB), lambda i: (0, i)),
            pl.BlockSpec((HD, TB), lambda i: (0, i)),
            pl.BlockSpec((side, HD, CK), lambda i: (i, max(p - 1, 0), 0)),
            pl.BlockSpec(memory_space=pl.ANY),
        ],
        out_specs=[pl.BlockSpec(shape, lambda i: (0, 0, 0)) for shape in shapes],
        out_shape=[jax.ShapeDtypeStruct(shape, BF) for shape in shapes],
        scratch_shapes=[
            pltpu.VMEM((n, 2 * HD), BF),
            pltpu.VMEM((2 * HD + 16, n), BF),
            pltpu.VMEM((n, 2 * HD), F32),
            pltpu.VMEM((3 * HD, TB), F32),
            pltpu.VMEM((2 * HD, 2 * GRID), F32),
            pltpu.VMEM((n, features), BF),
            pltpu.SemaphoreType.DMA,
        ],
        compiler_params=pltpu.CompilerParams(vmem_limit_bytes=56 * 2**20),
        cost_estimate=pl.CostEstimate(
            flops=8 * n * n * 4 * HD, bytes_accessed=48 * 2**20, transcendentals=0
        ),
    )(qkv, tab, probs, factors, oTf, doT, x)


def qkv_kernel(per, steps, n_held, here_ref, *refs):
    blocks, rest = refs[:steps], refs[steps:]
    w_ref, par_ref, bias_ref = rest[:3]
    x_ref, *outs, held, sems = rest[3 + n_held :]
    m = pl.program_id(0)
    copies = [
        pltpu.make_async_copy(blocks[j], held.at[j], sems.at[j]) for j in range(len(blocks))
    ]

    @pl.when(m == 0)
    def _():
        for copy in copies:
            copy.start()

    for j, copy in enumerate(copies):

        @pl.when(m == j)
        def _():
            copy.wait()

    v = held[m].astype(F32)
    v = v - jnp.mean(v, axis=-1, keepdims=True)
    v = v * lax.rsqrt(jnp.mean(v * v, axis=-1, keepdims=True) + EPS)
    x_ref[...] = v.astype(BF)
    x = (v * par_ref[0:1, :] + par_ref[1:2, :]).astype(BF)
    qkv = dot(x, w_ref[...], NN) + bias_ref[...]
    for p in range(per):
        outs[p][...] = qkv[:, p * 3 * HD : (p + 1) * 3 * HD].astype(BF)


def normed_qkv(here, first, total, blocks, w_cols, params, bias, before):
    rows, features = blocks[0].shape
    wide = w_cols.shape[1]
    per, steps = wide // (3 * HD), len(blocks)
    place = lambda m, here: ((m + first) ^ here[0], 0)
    return pl.pallas_call(
        partial(qkv_kernel, per, steps, len(before)),
        grid_spec=pltpu.PrefetchScalarGridSpec(
            num_scalar_prefetch=1,
            grid=(steps,),
            in_specs=[pl.BlockSpec(memory_space=pl.ANY)] * steps
            + [
                pl.BlockSpec((features, wide), lambda m, here: (0, 0)),
                pl.BlockSpec((2, features), lambda m, here: (0, 0)),
                pl.BlockSpec((1, wide), lambda m, here: (0, 0)),
            ]
            + [pl.BlockSpec(memory_space=pl.ANY)] * len(before),
            out_specs=[pl.BlockSpec((rows, features), place)]
            + [pl.BlockSpec((rows, 3 * HD), place)] * per,
            scratch_shapes=[
                pltpu.VMEM((steps, rows, features), BF),
                pltpu.SemaphoreType.DMA((steps,)),
            ],
        ),
        out_shape=[jax.ShapeDtypeStruct((total * rows, features), BF)]
        + [jax.ShapeDtypeStruct((total * rows, 3 * HD), BF)] * per,
        input_output_aliases={4 + steps + j: j for j in range(len(before))},
        compiler_params=pltpu.CompilerParams(vmem_limit_bytes=56 * 2**20),
        cost_estimate=pl.CostEstimate(
            flops=2 * steps * rows * features * wide, bytes_accessed=24 * 2**20, transcendentals=0
        ),
    )(here.reshape(1).astype(jnp.int32), *blocks, w_cols, params, bias, *before)


def mirror(tables):
    hole = jnp.zeros((2, 1, HD), tables.dtype)
    return jnp.concatenate([tables[:, GRID - 1 :: -1], hole, tables[:, : GRID - 1 : -1]], axis=1)


def unmirror(grads):
    return jnp.concatenate([grads[:, GRID - 1 :: -1], grads[:, : GRID : -1]], axis=1)


def attended_rows(ahead_ref, ending_ref, slots):
    images = ahead_ref.shape[0] // slots
    sides = []
    for y in range(images):
        parts = []
        for g in range(slots):
            parts += [ahead_ref[y * slots + g], ending_ref[y * slots + g]]
        sides.append(jnp.concatenate(parts, axis=0))
    return jnp.concatenate(sides, axis=1)


def mlp_kernel(
    slots, ahead_ref, ending_ref, tok_ref, cot_ref, w1_ref, w2_ref, wp_ref, par_ref, b1_ref,
    act_ref, gp_ref, n2_ref, mixed_ref, gm_ref, gb_ref, g0_ref, g12_ref, sum_ref, sb1_ref,
    hat_ref, rate_ref, gn_ref
):
    k, last = pl.program_id(0), pl.num_programs(0) - 1
    width = w1_ref.shape[1]
    sub = width // 3

    @pl.when(k == 0)
    def _():
        att = attended_rows(ahead_ref, ending_ref, slots)
        mixed = tok_ref[...].astype(F32) + dot(att, wp_ref[...], TN) + par_ref[0:1, :]
        mixed_ref[...] = mixed
        v = mixed - jnp.mean(mixed, axis=-1, keepdims=True)
        rate = lax.rsqrt(jnp.mean(v * v, axis=-1, keepdims=True) + EPS)
        hat = v * rate
        hat_ref[...] = hat
        rate_ref[...] = rate
        n2_ref[...] = (hat * par_ref[1:2, :] + par_ref[2:3, :]).astype(BF)
        gn_ref[...] = jnp.zeros_like(gn_ref)

    def products(j):
        cols = slice(j * sub, (j + 1) * sub)
        pre = dot(n2_ref[...], w1_ref[:, cols], NN) + b1_ref[:, cols]
        return pre, dot(cot_ref[...], w2_ref[cols, :], NT)

    def curves(j, pre, grad):
        cols = slice(j * sub, (j + 1) * sub)
        cdf = 0.5 + 0.5 * lax.erf(pre * 0.5**0.5)
        act_ref[:, cols] = (pre * cdf).astype(BF)
        slope = cdf + pre * (jnp.exp(-0.5 * pre * pre) * (2.0 * math.pi) ** -0.5)
        g = (grad * slope).astype(BF)
        gp_ref[:, cols] = g
        sb1_ref[:, cols] = jnp.sum(g.astype(F32), axis=0, keepdims=True)

    now = products(0)
    for j in range(3):
        following = products(j + 1) if j < 2 else None
        curves(j, *now)
        now = following
    gn_ref[...] += dot(gp_ref[...], w1_ref[...], NT)

    @pl.when(k == last)
    def _():
        gn, hat, cot = gn_ref[...], hat_ref[...], cot_ref[...].astype(F32)
        u = gn * par_ref[1:2, :]
        back = u - jnp.mean(u, axis=-1, keepdims=True)
        back = back - hat * jnp.mean(u * hat, axis=-1, keepdims=True)
        gm = cot + rate_ref[...] * back
        gm_ref[...] = gm
        gb = gm.astype(BF)
        gb_ref[...] = gb
        sum_ref[0:1, :] = jnp.sum(gb.astype(F32), axis=0, keepdims=True)
        sum_ref[1:2, :] = jnp.sum(cot, axis=0, keepdims=True)
        sum_ref[2:3, :] = jnp.sum(gn * hat, axis=0, keepdims=True)
        sum_ref[3:4, :] = jnp.sum(gn, axis=0, keepdims=True)
        sum_ref[4:8, :] = jnp.zeros((4, gn.shape[1]), F32)
        att = dot(wp_ref[...], gb_ref[...], NT).astype(BF)
        rows = g0_ref.shape[2]
        for s in range(g0_ref.shape[0]):
            y, g = s // slots, s % slots
            wide = HD + g12_ref.shape[1]
            piece = att[g * wide : (g + 1) * wide, y * rows : (y + 1) * rows]
            g0_ref[s] = piece[:HD]
            g12_ref[s] = piece[HD:]


def mlp_critical(slots, ahead, ending, tokens, cot, whole, params, b1):
    seqs, ahead_rows, rows_img = ahead.shape
    rows, features = tokens.shape
    blocks = (whole.shape[1] // features - 1) // 2
    hidden = blocks * features
    const2 = lambda k: (0, 0)
    const3 = lambda k: (0, 0, 0)
    return pl.pallas_call(
        partial(mlp_kernel, slots),
        grid=(blocks,),
        in_specs=[
            pl.BlockSpec(ahead.shape, const3),
            pl.BlockSpec(ending.shape, const3),
            pl.BlockSpec((rows, features), const2),
            pl.BlockSpec((rows, features), const2),
            pl.BlockSpec((features, features), lambda k: (0, k)),
            pl.BlockSpec((features, features), lambda k: (0, blocks + k)),
            pl.BlockSpec((features, features), lambda k: (0, 2 * blocks)),
            pl.BlockSpec((8, features), const2),
            pl.BlockSpec((1, features), lambda k: (0, k)),
        ],
        out_specs=[
            pl.BlockSpec((rows, features), lambda k: (0, k)),
            pl.BlockSpec((rows, features), lambda k: (0, k)),
            pl.BlockSpec((rows, features), const2),
            pl.BlockSpec((rows, features), const2),
            pl.BlockSpec((rows, features), const2),
            pl.BlockSpec((rows, features), const2),
            pl.BlockSpec((seqs, HD, rows_img), const3),
            pl.BlockSpec((seqs, ahead_rows, rows_img), const3),
            pl.BlockSpec((8, features), const2),
            pl.BlockSpec((1, features), lambda k: (0, k)),
        ],
        out_shape=[
            jax.ShapeDtypeStruct((rows, hidden), BF),
            jax.ShapeDtypeStruct((rows, hidden), BF),
            jax.ShapeDtypeStruct((rows, features), BF),
            jax.ShapeDtypeStruct((rows, features), F32),
            jax.ShapeDtypeStruct((rows, features), F32),
            jax.ShapeDtypeStruct((rows, features), BF),
            jax.ShapeDtypeStruct((seqs, HD, rows_img), BF),
            jax.ShapeDtypeStruct((seqs, ahead_rows, rows_img), BF),
            jax.ShapeDtypeStruct((8, features), F32),
            jax.ShapeDtypeStruct((1, hidden), F32),
        ],
        scratch_shapes=[
            pltpu.VMEM((rows, features), F32),
            pltpu.VMEM((rows, 1), F32),
            pltpu.VMEM((rows, features), F32),
        ],
        compiler_params=pltpu.CompilerParams(vmem_limit_bytes=60 * 2**20),
        cost_estimate=pl.CostEstimate(
            flops=2 * rows * features * (3 * hidden + 2 * features),
            bytes_accessed=40 * 2**20,
            transcendentals=2 * rows * hidden,
        ),
    )(ahead, ending, tokens, cot, whole, whole, whole, params, b1)


def grads_kernel(
    slots, blocks, ahead_ref, ending_ref, cot_ref, act_ref, gp_ref, n2_ref, gb_ref, mixed_ref,
    w2_ref, par_ref, out_ref, res_ref, n2T_ref, acc_ref
):
    k = pl.program_id(0)

    @pl.when(k == 0)
    def _():
        n2T_ref[...] = n2_ref[...].T
        acc_ref[...] = mixed_ref[...] + par_ref[3:4, :]

    @pl.when(k < blocks)
    def _():
        out_ref[...] = dot(n2T_ref[...], gp_ref[...], NN).astype(BF)

    @pl.when((k >= blocks) & (k < 2 * blocks))
    def _():
        act = act_ref[...]
        out_ref[...] = dot(act, cot_ref[...], TN).astype(BF)
        acc_ref[...] += dot(act, w2_ref[...], NN)

    @pl.when(k == 2 * blocks)
    def _():
        att = attended_rows(ahead_ref, ending_ref, slots)
        out_ref[...] = dot(att, gb_ref[...], NN).astype(BF)
        res_ref[...] = acc_ref[...].astype(BF)


def mlp_grads(slots, ahead, ending, cot, act, gp, n2, gb, mixed, whole, params):
    rows, features = cot.shape
    blocks = act.shape[1] // features
    const2 = lambda k: (0, 0)
    const3 = lambda k: (0, 0, 0)
    at1 = lambda k: jnp.minimum(k, blocks - 1)
    at2 = lambda k: jnp.clip(k - blocks, 0, blocks - 1)
    return pl.pallas_call(
        partial(grads_kernel, slots, blocks),
        grid=(2 * blocks + 1,),
        in_specs=[
            pl.BlockSpec(ahead.shape, const3),
            pl.BlockSpec(ending.shape, const3),
            pl.BlockSpec((rows, features), const2),
            pl.BlockSpec((rows, features), lambda k: (0, at2(k))),
            pl.BlockSpec((rows, features), lambda k: (0, at1(k))),
            pl.BlockSpec((rows, features), const2),
            pl.BlockSpec((rows, features), const2),
            pl.BlockSpec((rows, features), const2),
            pl.BlockSpec((features, features), lambda k: (0, blocks + at2(k))),
            pl.BlockSpec((8, features), const2),
        ],
        out_specs=[
            pl.BlockSpec((features, features), lambda k: (0, k)),
            pl.BlockSpec((rows, features), const2),
        ],
        out_shape=[
            jax.ShapeDtypeStruct((features, (2 * blocks + 1) * features), BF),
            jax.ShapeDtypeStruct((rows, features), BF),
        ],
        scratch_shapes=[pltpu.VMEM((features, rows), BF), pltpu.VMEM((rows, features), F32)],
        compiler_params=pltpu.CompilerParams(vmem_limit_bytes=56 * 2**20),
        cost_estimate=pl.CostEstimate(
            flops=2 * rows * features * features * (3 * blocks + 1),
            bytes_accessed=40 * 2**20,
            transcendentals=0,
        ),
    )(ahead, ending, cot, act, gp, n2, gb, mixed, whole, params)


def inputs_kernel(per, *refs):
    sent, (w_ref, tok_ref, gm_ref, gain_ref, out_ref) = refs[:per], refs[per:]
    rows = [ref[g, : 3 * HD, :] for ref in sent for g in range(ref.shape[0])]
    grad = dot(w_ref[...], jnp.concatenate(rows, axis=0), NN).T
    v = tok_ref[...].astype(F32)
    v = v - jnp.mean(v, axis=-1, keepdims=True)
    rate = lax.rsqrt(jnp.mean(v * v, axis=-1, keepdims=True) + EPS)
    hat = v * rate
    u = grad * gain_ref[...]
    back = u - jnp.mean(u, axis=-1, keepdims=True)
    back = back - hat * jnp.mean(u * hat, axis=-1, keepdims=True)
    out_ref[...] = (gm_ref[...] + rate * back).astype(BF)


def input_grads(slots, sent, w, tokens, grad_mixed, gain):
    rows, features = tokens.shape
    images = sent[0].shape[0] // slots
    side = rows // images
    const = lambda y: (0, 0)
    own = lambda y: (y, 0)
    return pl.pallas_call(
        partial(inputs_kernel, len(sent)),
        grid=(images,),
        in_specs=[pl.BlockSpec((slots,) + s.shape[1:], lambda y: (y, 0, 0)) for s in sent]
        + [
            pl.BlockSpec(w.shape, const),
            pl.BlockSpec((side, features), own),
            pl.BlockSpec((side, features), own),
            pl.BlockSpec((1, features), const),
        ],
        out_specs=pl.BlockSpec((side, features), own),
        out_shape=jax.ShapeDtypeStruct((rows, features), BF),
        compiler_params=pltpu.CompilerParams(vmem_limit_bytes=56 * 2**20),
        cost_estimate=pl.CostEstimate(
            flops=2 * rows * features * w.shape[1], bytes_accessed=16 * 2**20, transcendentals=0
        ),
    )(*sent, w, tokens, grad_mixed, gain)


def ordered_kernel(size, blocks, sum_ref, w1_ref, w2_ref, wp_ref):
    part = sum_ref.shape[0]
    features = part * size
    hidden = blocks * features
    sums = sum_ref[...].astype(F32)
    pieces = []
    for d in range(size):
        for k in range(blocks):
            at = k * features + d * part
            pieces.append(sums[:, at : at + part])
    w1_ref[...] = jnp.concatenate(pieces, axis=1)
    for k in range(blocks):
        w2_ref[k * part : (k + 1) * part, :] = sums[:, hidden + k * features :][:, :features]
    wp_ref[...] = sums[:, 2 * hidden :]


def ordered_grads(size, blocks, sums):
    part = sums.shape[0]
    features = part * size
    return pl.pallas_call(
        partial(ordered_kernel, size, blocks),
        out_shape=[
            jax.ShapeDtypeStruct((part, blocks * features), F32),
            jax.ShapeDtypeStruct((blocks * part, features), F32),
            jax.ShapeDtypeStruct((part, features), F32),
        ],
        compiler_params=pltpu.CompilerParams(vmem_limit_bytes=32 * 2**20),
        cost_estimate=pl.CostEstimate(flops=0, bytes_accessed=2**20, transcendentals=0),
    )(sums)


def swap(block, bit, size):
    return lax.ppermute(block, "seq", [(i, i ^ bit) for i in range(size)])


def halves(values):
    hi = lax.reduce_precision(values, 8, 7)
    return [hi.astype(BF), (values - hi).astype(BF)]


def body_heads(
    tokens,
    w_qkv,
    qv_bias,
    w_proj,
    proj_bias,
    w_fc1,
    fc1_bias,
    w_fc2,
    fc2_bias,
    norm_gains,
    norm_biases,
    rel_tables,
    cotangent,
):
    images, rows_img, features = tokens.shape
    dps, seqs = lax.axis_size("dp"), lax.axis_size("seq")
    size = dps * seqs
    slots = seqs // images
    per = HEADS // slots
    part = features // size
    wide = per * 3 * HD
    hidden = fc1_bias.shape[0] * size
    blocks = hidden // features
    here = lax.axis_index("seq")
    image, slot = here // slots, here % slots
    rows = images * rows_img

    own = lax.dynamic_index_in_dim(tokens, image, 0, keepdims=False)
    other = lax.dynamic_index_in_dim(tokens, 1 - image, 0, keepdims=False)
    small = jnp.concatenate(
        [
            qv_bias,
            proj_bias,
            fc1_bias,
            fc2_bias,
            norm_gains.reshape(-1),
            norm_biases.reshape(-1),
        ]
    )
    lengths = [2 * part, part, blocks * part, part, 2 * part, 2 * part]
    small = jnp.pad(small, (0, wide - small.shape[0])).reshape(1, 1, wide)
    by_head = w_qkv.reshape(part, 3, slots, per, HD)
    to_slots = by_head.transpose(2, 0, 3, 1, 4).reshape(slots, part, wide)
    to_slots = jnp.concatenate([to_slots, jnp.broadcast_to(small, (slots, 8, wide))], axis=1)
    to_slots, own, other = lax.optimization_barrier(
        (jnp.tile(to_slots, (dps * images, 1, 1)), own, other)
    )
    cols = lax.all_to_all(to_slots, AXES, 0, 0, tiled=True)
    own_x, got = swap(own, 2, seqs), swap(other, 4, seqs)
    own_x, got = lax.optimization_barrier((own_x, got))
    got_x = swap(got, 2, seqs)
    w_cols = cols[:, :part].reshape(features, wide)
    smalls = cols[:, part]
    edges = [sum(lengths[:j]) for j in range(len(lengths) + 1)]
    cut = [smalls[:, a:b].astype(F32) for a, b in zip(edges[:-1], edges[1:])]
    bqv, bp, b2 = cut[0].reshape(-1), cut[1].reshape(-1), cut[3].reshape(-1)
    b1 = cut[2].reshape(size, blocks, part).transpose(1, 0, 2).reshape(-1)
    gains = cut[4].reshape(size, 2, part).transpose(1, 0, 2).reshape(2, features)
    shifts = cut[5].reshape(size, 2, part).transpose(1, 0, 2).reshape(2, features)

    full_bias = jnp.stack(
        [
            bqv[:features].reshape(slots, per, HD),
            jnp.zeros((slots, per, HD), F32),
            bqv[features:].reshape(slots, per, HD),
        ],
        axis=2,
    ).reshape(slots, wide)
    own_bias = lax.dynamic_index_in_dim(full_bias, slot, 0, keepdims=True)
    first_norm = jnp.stack([gains[0], shifts[0]])
    by_mask = [own, swap(own, 1, seqs), own_x, swap(own_x, 1, seqs), got, swap(got, 1, seqs)]
    held = normed_qkv(here, 0, seqs, by_mask, w_cols, first_norm, own_bias, [])
    by_mask = [got_x, swap(got_x, 1, seqs)]
    hat_all, *qkv = normed_qkv(here, 6, seqs, by_mask, w_cols, first_norm, own_bias, held)

    w1_local = w_fc1.reshape(part, size, blocks, part).transpose(0, 2, 1, 3).reshape(part, hidden)
    w2_local = w_fc2.reshape(blocks, part, features).transpose(1, 0, 2).reshape(part, hidden)
    wq_local = by_head.transpose(0, 3, 2, 1, 4).reshape(part, 3 * features)
    whole = jnp.concatenate([w1_local, w2_local, w_proj], axis=1)
    whole = lax.optimization_barrier((whole, got_x, held[1]))[0]
    whole = lax.all_gather(whole, AXES, axis=0, tiled=True)

    tab = mirror(rel_tables)
    kept, joint = [], ()
    for p in range(per - 1):
        out, *saved = heads_forward(qkv[p], tab, per - 1, p, joint)
        kept.append([qkv[p], tab, saved[1], saved[2], saved[0], hat_all])
        joint = (out,)
    qkv[-1] = lax.optimization_barrier((qkv[-1], out))[0]
    ahead = lax.all_to_all(out, "seq", 0, 0, tiled=True)
    ending, *saved = heads_forward(qkv[-1], tab)
    kept.append([qkv[-1], tab, saved[1], saved[2], saved[0], hat_all])
    ending = lax.optimization_barrier((ending, ahead))[0]
    ending = lax.all_to_all(ending, "seq", 0, 0, tiled=True)

    wq_local = lax.optimization_barrier((wq_local, ahead, ending))[0]
    wq = lax.all_gather(wq_local, AXES, axis=0, tiled=True)

    params = jnp.concatenate(
        [jnp.stack([bp, gains[1], shifts[1], b2]), jnp.zeros((4, features), F32)]
    )
    b1 = b1[None]
    ending, params, b1 = lax.optimization_barrier((ending, params, b1))
    cot = cotangent.reshape(rows, features)
    act, grad_pre, normed2, mixed, grad_mixed, grad_branch, send0, send12, sums, sum_b1 = mlp_critical(
        slots, ahead, ending, tokens.reshape(rows, features), cot, whole, params, b1
    )
    first = lax.all_to_all(send0, "seq", 0, 0, tiled=True)
    others = lax.all_to_all(send12, "seq", 0, 0, tiled=True)
    grads, result = mlp_grads(
        slots, ahead, ending, cot, act, grad_pre, normed2, grad_branch, mixed, whole, params
    )
    result = result.reshape(tokens.shape)
    summed = lax.psum_scatter(grads, AXES, scatter_dimension=0, tiled=True)
    w_fc1_grad, w_fc2_grad, w_proj_grad = ordered_grads(size, blocks, summed)
    sum_b1 = sum_b1.reshape(blocks, size, part).transpose(1, 0, 2).reshape(size, blocks * part)
    early = jnp.concatenate(
        [
            sums[0].reshape(size, part),
            sum_b1,
            sums[1].reshape(size, part),
            sums[2].reshape(size, part),
            sums[3].reshape(size, part),
        ],
        axis=1,
    )

    table = jnp.zeros((16, 2 * GRID), F32)
    sent_on, messages = [], []
    for p in range(per):
        do_p = first if p == 0 else others
        if p == 0:
            kept[0][0] = lax.optimization_barrier((kept[0][0], grads))[0]
        message, *far = heads_backward(dps, seqs, p, p == per - 1, *kept[p], do_p)
        message = lax.all_to_all(message, "seq", 0, 0, tiled=True)
        if p == per - 1:
            sent_on = jnp.stack(sent_on, axis=1)
            level = lax.axis_index("dp")
            products = lax.dynamic_index_in_dim(sent_on, level, 0, keepdims=False).astype(F32)
            for m in range(1, dps):
                block = lax.dynamic_index_in_dim(sent_on, level ^ m, 0, keepdims=False)
                block = lax.ppermute(block, "dp", [(i, i ^ m) for i in range(dps)])
                products = products + block.astype(F32)
            message, products = lax.optimization_barrier((message, products))
        messages.append(message)
        base = message.shape[1] - 16
        pair = message[:, base:, : 4 * GRID].astype(F32)
        table = table + jnp.sum(pair[..., : 2 * GRID] + pair[..., 2 * GRID :], axis=0)
        if p < per - 1:
            moment = message[:, 3 * HD : base, : 6 * HD].astype(F32)
            moment = jnp.sum(moment.reshape(images, slots, dps // 2 * part, 6 * HD), axis=0)
            moment = moment.reshape(slots, dps // 2, part, 2, 3 * HD).transpose(3, 1, 0, 2, 4)
            total = message[:, base : base + 2, 4 * GRID : 4 * GRID + 3 * HD].astype(F32)
            total = jnp.sum(total.reshape(images, slots, 2, 3 * HD), axis=(0, 2))
            total = jnp.pad(jnp.stack(halves(total), axis=1), ((0, 0), (0, 6), (0, 0)))
            total = jnp.broadcast_to(total, (dps,) + total.shape)
            by_owner = jnp.concatenate(
                [moment.reshape(dps, slots, part, 3 * HD).astype(BF), total], axis=2
            )
            sent_on.append(by_owner)
    pieces = table.astype(BF).reshape(8, 4 * GRID)
    pieces = jnp.broadcast_to(pieces, (size,) + pieces.shape)
    sums = jnp.stack(halves(early), axis=1)
    sums = jnp.pad(sums, ((0, 0), (2, 4), (0, 4 * GRID - 8 * part)))
    far = jnp.concatenate([far[0][:, :part], far[0][:, part:] + sums, pieces], axis=1)
    far = lax.all_to_all(far, AXES, 0, 0, tiled=True)
    tokens_grad = input_grads(
        slots, messages, wq, tokens.reshape(rows, features), grad_mixed, gains[:1]
    ).reshape(tokens.shape)
    far, tokens_grad = lax.optimization_barrier((far, tokens_grad))
    final = far[:, : part + 8, : 3 * HD].astype(F32).reshape(dps * images, slots, part + 8, 3 * HD)
    products = jnp.concatenate([products, jnp.sum(final, axis=0)[None]])
    moments = products[:, :, :part].swapaxes(0, 1)
    totals = (products[:, :, part] + products[:, :, part + 1]).swapaxes(0, 1)
    bundle = jnp.sum(far[:, part + 2 : part + 4, : 8 * part].astype(F32), axis=(0, 1))
    table = far[:, part + 8 :].astype(F32).reshape(dps, seqs * 16, 2 * GRID)
    table = jnp.sum(table, axis=0).reshape(2, HD, 2 * GRID)
    rel_tables_grad = unmirror(table.swapaxes(1, 2))

    moment = moments.reshape(slots, per, part, 3, HD)
    moment = moment.transpose(2, 3, 0, 1, 4).reshape(part, 3 * features)
    total = totals.reshape(slots, per, 3, HD)
    total = total.transpose(2, 0, 1, 3).reshape(3 * features)
    own_gain, own_shift = norm_gains[0].astype(F32), norm_biases[0].astype(F32)
    w_qkv_grad = own_gain[:, None] * moment + own_shift[:, None] * total
    w_own = w_qkv.astype(F32)
    gain0, shift0 = jnp.sum(w_own * moment, axis=1), jnp.sum(w_own * total, axis=1)
    device = lax.axis_index("dp") * seqs + here
    total = jnp.concatenate([total[:features], total[2 * features :]]).reshape(size, 2 * part)
    qv_bias_grad = lax.dynamic_index_in_dim(total, device, 0, keepdims=False)

    ends = [part * end for end in [0, 1, 1 + blocks, 2 + blocks, 3 + blocks, 4 + blocks]]
    bundle = [bundle[a:b] for a, b in zip(ends[:-1], ends[1:])]
    proj_bias_grad, fc1_bias_grad, fc2_bias_grad, gain1, shift1 = bundle
    norm_gains_grad = jnp.stack([gain0, gain1])
    norm_biases_grad = jnp.stack([shift0, shift1])
    return (
        result,
        tokens_grad,
        w_qkv_grad,
        qv_bias_grad,
        w_proj_grad,
        proj_bias_grad,
        w_fc1_grad,
        fc1_bias_grad,
        w_fc2_grad,
        fc2_bias_grad,
        norm_gains_grad,
        norm_biases_grad,
        rel_tables_grad,
    )


def layer_norm(values, gain, shift):
    center = jnp.mean(values, axis=-1, keepdims=True)
    centered = values - center
    spread = jnp.mean(centered * centered, axis=-1, keepdims=True)
    return centered * lax.rsqrt(spread + EPS) * gain + shift


def fetch_each(weights):
    return (
        lax.all_gather(weights[0], ("dp", "seq"), axis=0, tiled=True),
        lax.all_gather(weights[1], ("dp", "seq"), axis=0, tiled=True),
        lax.all_gather(weights[2], ("dp", "seq"), axis=0, tiled=True),
        lax.all_gather(weights[3], ("dp", "seq"), axis=0, tiled=True),
        lax.all_gather(weights[4], ("dp", "seq"), axis=0, tiled=True),
        lax.all_gather(weights[5], ("dp", "seq"), axis=0, tiled=True),
        lax.all_gather(weights[6], ("dp", "seq"), axis=0, tiled=True),
        lax.all_gather(weights[7], ("dp", "seq"), axis=0, tiled=True),
        lax.all_gather(weights[8], ("dp", "seq"), axis=1, tiled=True),
        lax.all_gather(weights[9], ("dp", "seq"), axis=1, tiled=True),
    )


def position_rows(tables, rows_img):
    beginning = lax.axis_index("seq") * rows_img
    tokens_at = beginning + jnp.arange(rows_img, dtype=jnp.int32)
    offsets = jnp.arange(GRID, dtype=jnp.int32)
    entries = jnp.arange(TABLE, dtype=jnp.int32)
    row_index = tokens_at[:, None] // GRID - offsets[None, :] + GRID - 1
    col_index = tokens_at[:, None] % GRID - offsets[None, :] + GRID - 1
    row_hot = (row_index[:, :, None] == entries[None, None, :]).astype(jnp.float32)
    col_hot = (col_index[:, :, None] == entries[None, None, :]).astype(jnp.float32)
    tables_f = tables.astype(jnp.float32)
    rel_rows = jnp.einsum("rkt,tc->rkc", row_hot, tables_f[0], precision=HIGH)
    rel_cols = jnp.einsum("rkt,tc->rkc", col_hot, tables_f[1], precision=HIGH)
    return (row_hot, col_hot, rel_rows, rel_cols)


def score_block(queries, keys_all, rows_low, cols_low):
    rows_img = queries.shape[0]
    product = jnp.einsum(
        "rhc,nhc->hrn", queries, keys_all, preferred_element_type=jnp.float32
    ) * HD ** (-0.5)
    bias_rows = jnp.einsum("rhc,rkc->hrk", queries, rows_low, preferred_element_type=jnp.float32)
    bias_cols = jnp.einsum("rhc,rkc->hrk", queries, cols_low, preferred_element_type=jnp.float32)
    joined = (
        product.reshape(HEADS, rows_img, GRID, GRID)
        + bias_rows[:, :, :, None]
        + bias_cols[:, :, None, :]
    )
    return joined.reshape(HEADS, rows_img, GRID * GRID)


def attend_forward(qkv_img, kv_pair, rows_low, cols_low):
    rows_img, triple = qkv_img.shape
    features = triple // 3
    queries = qkv_img[:, :features].reshape(rows_img, HEADS, HD)
    keys_all = kv_pair[0].reshape(-1, HEADS, HD)
    values_all = kv_pair[1].reshape(-1, HEADS, HD)
    scores = score_block(queries, keys_all, rows_low, cols_low)
    largest = jnp.max(scores, axis=-1, keepdims=True)
    shifted = jnp.exp(scores - largest)
    totals = jnp.sum(shifted, axis=-1, keepdims=True)
    probs_low = (shifted / totals).astype(jnp.bfloat16)
    attended = jnp.einsum("hrn,nhc->rhc", probs_low, values_all, preferred_element_type=jnp.float32)
    log_totals = largest[..., 0] + jnp.log(totals[..., 0])
    return (attended.reshape(rows_img, features).astype(jnp.bfloat16), log_totals)


def attend_backward(qkv_img, log_totals, grad_att, kv_pair, rel_rows, rel_cols, rows_low, cols_low):
    rows_img, triple = qkv_img.shape
    features = triple // 3
    scale = HD ** (-0.5)
    queries = qkv_img[:, :features].reshape(rows_img, HEADS, HD)
    keys_all = kv_pair[0].reshape(-1, HEADS, HD)
    values_all = kv_pair[1].reshape(-1, HEADS, HD)
    scores = score_block(queries, keys_all, rows_low, cols_low)
    probs = jnp.exp(scores - log_totals[..., None])
    probs_low = probs.astype(jnp.bfloat16)
    grad_heads = grad_att.reshape(rows_img, HEADS, HD)
    grad_probs = jnp.einsum(
        "rhc,nhc->hrn", grad_heads, values_all, preferred_element_type=jnp.float32
    )
    inner_sum = jnp.sum(probs * grad_probs, axis=-1, keepdims=True)
    grad_scores = (probs * (grad_probs - inner_sum)).astype(jnp.bfloat16)
    grad_queries = (
        jnp.einsum("hrn,nhc->rhc", grad_scores, keys_all, preferred_element_type=jnp.float32)
        * scale
    )
    grid_scores = grad_scores.reshape(HEADS, rows_img, GRID, GRID)
    grad_rows = jnp.sum(grid_scores, axis=3, dtype=jnp.float32)
    grad_cols = jnp.sum(grid_scores, axis=2, dtype=jnp.float32)
    grad_queries = grad_queries + jnp.einsum("hrk,rkc->rhc", grad_rows, rel_rows, precision=HIGH)
    grad_queries = grad_queries + jnp.einsum("hrk,rkc->rhc", grad_cols, rel_cols, precision=HIGH)
    query_f = queries.astype(jnp.float32)
    table_rows = jnp.einsum("hrk,rhc->rkc", grad_rows, query_f, precision=HIGH)
    table_cols = jnp.einsum("hrk,rhc->rkc", grad_cols, query_f, precision=HIGH)
    length = lax.axis_size("seq") * rows_img
    grad_keys = (
        jnp.einsum("hrn,rhc->nhc", grad_scores, queries, preferred_element_type=jnp.float32) * scale
    )
    grad_values = jnp.einsum(
        "hrn,rhc->nhc", probs_low, grad_heads, preferred_element_type=jnp.float32
    )
    key_grads = lax.psum_scatter(
        jnp.concatenate(
            [grad_keys.reshape(length, features), grad_values.reshape(length, features)], axis=1
        ),
        "seq",
        scatter_dimension=0,
        tiled=True,
    )
    grad_qkv = jnp.concatenate(
        [grad_queries.reshape(rows_img, features), key_grads], axis=1
    ).astype(jnp.bfloat16)
    return (grad_qkv, table_rows, table_cols)


def body(
    tokens,
    w_qkv,
    qv_bias,
    w_proj,
    proj_bias,
    w_fc1,
    fc1_bias,
    w_fc2,
    fc2_bias,
    norm_gains,
    norm_biases,
    rel_tables,
    cotangent,
):
    images, rows_img, features = tokens.shape
    per_batch = images // MB
    weights = (
        w_qkv,
        qv_bias,
        w_proj,
        proj_bias,
        w_fc1,
        fc1_bias,
        w_fc2,
        fc2_bias,
        norm_gains,
        norm_biases,
    )
    row_hot, col_hot, rel_rows, rel_cols = position_rows(rel_tables, rows_img)
    rows_low = rel_rows.astype(jnp.bfloat16)
    cols_low = rel_cols.astype(jnp.bfloat16)
    stored = []
    outputs = []
    for batch_index in range(MB):
        gathered = fetch_each(weights)
        (
            wq_full,
            bqv_full,
            wp_full,
            bp_full,
            w1_full,
            b1_full,
            w2_full,
            b2_full,
            gains_full,
            shifts_full,
        ) = gathered
        gains_f = gains_full.astype(jnp.float32)
        shifts_f = shifts_full.astype(jnp.float32)
        inputs = (
            tokens[batch_index * per_batch : (batch_index + 1) * per_batch]
            .astype(jnp.float32)
            .reshape(-1, features)
        )
        normed1 = layer_norm(inputs, gains_f[0], shifts_f[0]).astype(jnp.bfloat16)
        full_bias = jnp.concatenate(
            [bqv_full[:features], jnp.zeros((features,), bqv_full.dtype), bqv_full[features:]]
        ).astype(jnp.float32)
        qkv = (jnp.dot(normed1, wq_full, preferred_element_type=jnp.float32) + full_bias).astype(
            jnp.bfloat16
        )
        qkv_images = qkv.reshape(per_batch, rows_img, 3 * features)

        def forward_image(carried, qkv_img):
            kv_pair = (
                lax.all_gather(qkv_img[:, features : 2 * features], "seq", axis=0, tiled=True),
                lax.all_gather(qkv_img[:, 2 * features :], "seq", axis=0, tiled=True),
            )
            attended_img, log_totals = attend_forward(qkv_img, kv_pair, rows_low, cols_low)
            return (carried, (attended_img, log_totals))

        results = lax.scan(forward_image, jnp.zeros((), jnp.float32), qkv_images)[1]
        attended = results[0].reshape(-1, features)
        mixed = (
            inputs
            + jnp.dot(attended, wp_full, preferred_element_type=jnp.float32)
            + bp_full.astype(jnp.float32)
        )
        normed2 = layer_norm(mixed, gains_f[1], shifts_f[1]).astype(jnp.bfloat16)
        pre = jnp.dot(normed2, w1_full, preferred_element_type=jnp.float32) + b1_full.astype(
            jnp.float32
        )
        activated = jax.nn.gelu(pre, approximate=False).astype(jnp.bfloat16)
        block_out = (
            mixed
            + jnp.dot(activated, w2_full, preferred_element_type=jnp.float32)
            + b2_full.astype(jnp.float32)
        )
        outputs.append(block_out.astype(jnp.bfloat16).reshape(per_batch, rows_img, features))
        stored.append((normed1, qkv_images, results, mixed, normed2, pre, activated))
    gradients = [jnp.zeros(array.shape, jnp.float32) for array in gathered]
    table_rows_sum = jnp.zeros((rows_img, GRID, HD), jnp.float32)
    table_cols_sum = jnp.zeros((rows_img, GRID, HD), jnp.float32)
    input_grads = []
    for batch_index in range(MB):
        gathered = fetch_each(weights)
        (
            wq_full,
            bqv_full,
            wp_full,
            bp_full,
            w1_full,
            b1_full,
            w2_full,
            b2_full,
            gains_full,
            shifts_full,
        ) = gathered
        gains_f = gains_full.astype(jnp.float32)
        shifts_f = shifts_full.astype(jnp.float32)
        normed1, qkv_images, results, mixed, normed2, pre, activated = stored[batch_index]
        inputs = (
            tokens[batch_index * per_batch : (batch_index + 1) * per_batch]
            .astype(jnp.float32)
            .reshape(-1, features)
        )
        grad_out = cotangent[batch_index * per_batch : (batch_index + 1) * per_batch].reshape(
            -1, features
        )
        grad_out_f = grad_out.astype(jnp.float32)
        grad_w2 = jnp.dot(activated.T, grad_out, preferred_element_type=jnp.float32)
        grad_b2 = jnp.sum(grad_out_f, axis=0)
        grad_act = jnp.dot(grad_out, w2_full.T, preferred_element_type=jnp.float32)
        _, gelu_pull = jax.vjp(partial(jax.nn.gelu, approximate=False), pre)
        grad_pre = gelu_pull(grad_act)[0].astype(jnp.bfloat16)
        grad_w1 = jnp.dot(normed2.T, grad_pre, preferred_element_type=jnp.float32)
        grad_b1 = jnp.sum(grad_pre, axis=0, dtype=jnp.float32)
        grad_norm2 = jnp.dot(grad_pre, w1_full.T, preferred_element_type=jnp.float32)
        _, norm_pull2 = jax.vjp(layer_norm, mixed, gains_f[1], shifts_f[1])
        grad_mix_norm, grad_gain2, grad_shift2 = norm_pull2(grad_norm2)
        grad_mixed = grad_out_f + grad_mix_norm
        grad_branch = grad_mixed.astype(jnp.bfloat16)
        attended = results[0].reshape(-1, features)
        grad_wp = jnp.dot(attended.T, grad_branch, preferred_element_type=jnp.float32)
        grad_bp = jnp.sum(grad_branch, axis=0, dtype=jnp.float32)
        grad_att = jnp.dot(grad_branch, wp_full.T, preferred_element_type=jnp.float32).astype(
            jnp.bfloat16
        )
        grad_images = grad_att.reshape(per_batch, rows_img, features)
        image_inputs = (qkv_images, results[1], grad_images)

        def backward_image(carried, pieces):
            kv_pair = (
                lax.all_gather(pieces[0][:, features : 2 * features], "seq", axis=0, tiled=True),
                lax.all_gather(pieces[0][:, 2 * features :], "seq", axis=0, tiled=True),
            )
            grad_qkv_img, table_rows, table_cols = attend_backward(
                pieces[0], pieces[1], pieces[2], kv_pair, rel_rows, rel_cols, rows_low, cols_low
            )
            return ((carried[0] + table_rows, carried[1] + table_cols), grad_qkv_img)

        (table_rows_sum, table_cols_sum), grad_qkv_all = lax.scan(
            backward_image, (table_rows_sum, table_cols_sum), image_inputs
        )
        grad_qkv = grad_qkv_all.reshape(-1, 3 * features)
        grad_wq = jnp.dot(normed1.T, grad_qkv, preferred_element_type=jnp.float32)
        grad_bqv = jnp.concatenate(
            [
                jnp.sum(grad_qkv[:, :features], axis=0, dtype=jnp.float32),
                jnp.sum(grad_qkv[:, 2 * features :], axis=0, dtype=jnp.float32),
            ]
        )
        grad_norm1 = jnp.dot(grad_qkv, wq_full.T, preferred_element_type=jnp.float32)
        _, norm_pull1 = jax.vjp(layer_norm, inputs, gains_f[0], shifts_f[0])
        grad_in_norm, grad_gain1, grad_shift1 = norm_pull1(grad_norm1)
        input_grads.append(
            (grad_mixed + grad_in_norm).astype(jnp.bfloat16).reshape(per_batch, rows_img, features)
        )
        updates = (
            grad_wq,
            grad_bqv,
            grad_wp,
            grad_bp,
            grad_w1,
            grad_b1,
            grad_w2,
            grad_b2,
            jnp.stack([grad_gain1, grad_gain2]),
            jnp.stack([grad_shift1, grad_shift2]),
        )
        gradients = [before + update for before, update in zip(gradients, updates)]
    summed = (
        lax.psum_scatter(gradients[0], ("dp", "seq"), scatter_dimension=0, tiled=True),
        lax.psum_scatter(gradients[1], ("dp", "seq"), scatter_dimension=0, tiled=True),
        lax.psum_scatter(gradients[2], ("dp", "seq"), scatter_dimension=0, tiled=True),
        lax.psum_scatter(gradients[3], ("dp", "seq"), scatter_dimension=0, tiled=True),
        lax.psum_scatter(gradients[4], ("dp", "seq"), scatter_dimension=0, tiled=True),
        lax.psum_scatter(gradients[5], ("dp", "seq"), scatter_dimension=0, tiled=True),
        lax.psum_scatter(gradients[6], ("dp", "seq"), scatter_dimension=0, tiled=True),
        lax.psum_scatter(gradients[7], ("dp", "seq"), scatter_dimension=0, tiled=True),
        lax.psum_scatter(gradients[8], ("dp", "seq"), scatter_dimension=1, tiled=True),
        lax.psum_scatter(gradients[9], ("dp", "seq"), scatter_dimension=1, tiled=True),
    )
    table_local = jnp.stack(
        [
            jnp.einsum("rkt,rkc->tc", row_hot, table_rows_sum, precision=HIGH),
            jnp.einsum("rkt,rkc->tc", col_hot, table_cols_sum, precision=HIGH),
        ]
    )
    table_grad = lax.psum(table_local, ("dp", "seq"))
    return (
        jnp.concatenate(outputs, axis=0),
        jnp.concatenate(input_grads, axis=0),
        summed[0],
        summed[1],
        summed[2],
        summed[3],
        summed[4],
        summed[5],
        summed[6],
        summed[7],
        summed[8],
        summed[9],
        table_grad,
    )


def solution(mesh):
    placed = (
        P("dp", "seq", None),
        P(("dp", "seq"), None),
        P(("dp", "seq")),
        P(("dp", "seq"), None),
        P(("dp", "seq")),
        P(("dp", "seq"), None),
        P(("dp", "seq")),
        P(("dp", "seq"), None),
        P(("dp", "seq")),
        P(None, ("dp", "seq")),
        P(None, ("dp", "seq")),
        P(),
        P("dp", "seq", None),
    )
    seqs, images = mesh.shape["seq"], IMAGES // mesh.shape["dp"]
    by_heads = (mesh.shape["dp"], seqs, images) == (4, 8, 2)
    return jax.shard_map(
        body_heads if by_heads else body,
        mesh=mesh,
        in_specs=placed,
        out_specs=(
            P("dp", "seq", None),
            P("dp", "seq", None),
            P(("dp", "seq"), None),
            P(("dp", "seq")),
            P(("dp", "seq"), None),
            P(("dp", "seq")),
            P(("dp", "seq"), None),
            P(("dp", "seq")),
            P(("dp", "seq"), None),
            P(("dp", "seq")),
            P(None, ("dp", "seq")),
            P(None, ("dp", "seq")),
            P(),
        ),
        check_vma=False,
    )
```

```python
from functools import partial
import math

import jax
import jax.numpy as jnp
from jax import lax
from jax.experimental import pallas as pl
from jax.experimental.pallas import tpu as pltpu
from jax.sharding import PartitionSpec as P

HEADS = 12
HD = 64
GRID = 64
MB = 2
TABLE = 127


EPS = 1e-06
HIGH = lax.Precision.HIGHEST
IMAGES = 8
AXES = ("dp", "seq")

TB = 1024
CK = 512
ROWS = CK // GRID
LOG2E = 1.4426950408889634
NN = (((1,), (0,)), ((), ()))
NT = (((1,), (1,)), ((), ()))
TN = (((0,), (0,)), ((), ()))
BF = jnp.bfloat16
F32 = jnp.float32


def dot(a, b, dims):
    return lax.dot_general(a, b, dims, preferred_element_type=F32)


def col_hot(n):
    key = lax.broadcasted_iota(jnp.int32, (n, GRID), 0) & (GRID - 1)
    col = lax.broadcasted_iota(jnp.int32, (n, GRID), 1)
    return (key == col).astype(F32)


def fwd_kernel(n_chunks, qkv_ref, tab_ref, *refs):
    oT_ref, oTf_ref, p_ref, f_ref, kaug, vta, br_ref, qa_ref = refs[-8:]
    i = pl.program_id(0)
    tg = TB // GRID

    @pl.when(i == 0)
    def _():
        for c in range(n_chunks):
            rows = pl.ds(c * CK, CK)
            k = qkv_ref[rows, HD : 2 * HD].astype(F32)
            pair = jnp.concatenate([k, col_hot(CK)], axis=1).astype(BF)
            kaug[rows, : 2 * HD] = pair
            kaug[rows, 2 * HD :] = pair
            vT = qkv_ref[rows, 2 * HD :].astype(F32).T
            vta[0:HD, rows] = vT.astype(BF)
            one = lax.broadcasted_iota(jnp.int32, (16, CK), 0) == 0
            vta[HD : HD + 16, rows] = one.astype(F32).astype(BF)

    q = qkv_ref[pl.ds(pl.multiple_of(i * TB, TB), TB), :HD]
    gr = dot(q, tab_ref[0], NT) * LOG2E
    gc = dot(q, tab_ref[1], NT) * LOG2E
    brs, bcs = [], []
    for g in range(tg):
        sl = slice(g * GRID, (g + 1) * GRID)
        brs.append(pltpu.roll(gr[sl], i * tg + g, 1))
        bcs.append(pltpu.roll(gc[sl], 0, 1, stride=1, stride_axis=0))
    br = jnp.concatenate(brs, axis=0)
    bc = jnp.concatenate(bcs, axis=0)
    qs = q.astype(F32) * (HD ** -0.5 * LOG2E)
    cat = jnp.concatenate([qs, bc[:, :GRID]], axis=1).T
    hi = cat.astype(BF)
    lo = (cat - hi.astype(F32)).astype(BF)
    qa_ref[...] = jnp.concatenate([hi, lo], axis=0)
    br_ref[...] = br.T[:GRID]
    qa = qa_ref[...]

    def scores(c):
        return dot(kaug[c * CK : (c + 1) * CK, :], qa, NN)

    def soften(c, s):
        s = s.reshape(ROWS, GRID, TB)
        b8 = br_ref[c * ROWS : (c + 1) * ROWS, :]
        top = jnp.max(jnp.max(s, axis=1) + b8, axis=0, keepdims=True)
        p = jnp.exp2(s - (top - b8)[:, None, :]).astype(BF).reshape(CK, TB)
        p_ref[0, c * CK : (c + 1) * CK, :] = p
        return top, p

    def gather(m, acc, c, top, p):
        out = dot(vta[:, c * CK : (c + 1) * CK], p, NN)
        new = jnp.maximum(m, top)
        return new, acc * jnp.exp2(m - new) + out * jnp.exp2(top - new)

    m = jnp.full((1, TB), -jnp.inf, F32)
    acc = jnp.zeros((HD + 16, TB), F32)
    tops = []
    s, before = scores(0), None
    for c in range(n_chunks):
        following = scores(c + 1) if c + 1 < n_chunks else None
        if before is not None:
            m, acc = gather(m, acc, c - 1, *before)
        before, s = soften(c, s), following
        tops.append(before[0])
    m, acc = gather(m, acc, n_chunks - 1, *before)
    total = acc[HD : HD + 1]
    out = acc[:HD] / total
    for j in range(TB // CK):
        oT_ref[j] = out[:, j * CK : (j + 1) * CK].astype(BF)
    oTf_ref[...] = out
    f_ref[...] = jnp.exp2(jnp.concatenate(tops, axis=0) - (m + jnp.log2(total)))


def heads_forward(qkv, tab, places=1, place=0, before=()):
    n = qkv.shape[0]
    steps, chunks, side = n // TB, n // CK, TB // CK
    return pl.pallas_call(
        partial(fwd_kernel, chunks),
        grid=(steps,),
        in_specs=[
            pl.BlockSpec((n, 3 * HD), lambda i: (0, 0)),
            pl.BlockSpec((2, 2 * GRID, HD), lambda i: (0, 0, 0)),
        ]
        + [pl.BlockSpec(memory_space=pl.ANY)] * len(before),
        out_specs=[
            pl.BlockSpec((side, HD, CK), lambda i: (i, place, 0)),
            pl.BlockSpec((HD, TB), lambda i: (0, i)),
            pl.BlockSpec((1, n, TB), lambda i: (i, 0, 0)),
            pl.BlockSpec((chunks, TB), lambda i: (0, i)),
        ],
        out_shape=[
            jax.ShapeDtypeStruct((chunks, places * HD, CK), BF),
            jax.ShapeDtypeStruct((HD, n), F32),
            jax.ShapeDtypeStruct((steps, n, TB), BF),
            jax.ShapeDtypeStruct((chunks, n), F32),
        ],
        scratch_shapes=[
            pltpu.VMEM((n, 4 * HD), BF),
            pltpu.VMEM((HD + 16, n), BF),
            pltpu.VMEM((GRID, TB), F32),
            pltpu.VMEM((4 * HD, TB), BF),
        ],
        compiler_params=pltpu.CompilerParams(vmem_limit_bytes=56 * 2**20),
        cost_estimate=pl.CostEstimate(
            flops=4 * n * n * 4 * HD, bytes_accessed=48 * 2**20, transcendentals=n * n
        ),
        input_output_aliases={2 + j: 0 for j in range(len(before))},
    )(qkv, tab, *before)


def bwd_kernel(
    n_chunks, dps, seqs, qkv_ref, tab_ref, p_ref, f_ref, oTf_ref, doT_ref, x_hbm, msg_ref, *refs
):
    *far_ref, vaug, kta, dkv, dqa, dtab_ref, x_ref, x_sem = refs
    i = pl.program_id(0)
    tg, side = TB // GRID, TB // CK
    n_steps = pl.num_programs(0)
    fetch = pltpu.make_async_copy(x_hbm, x_ref, x_sem)

    @pl.when(i == 0)
    def _():
        for c in range(n_chunks):
            rows = pl.ds(c * CK, CK)
            k = qkv_ref[rows, HD : 2 * HD].astype(F32)
            both = jnp.concatenate([k, col_hot(CK)], axis=1).T
            kta[0 : 2 * HD, rows] = both.astype(BF)
            key = lax.broadcasted_iota(jnp.int32, (16, CK), 1) >> 6
            hot = lax.broadcasted_iota(jnp.int32, (16, CK), 0) == key
            kta[2 * HD : 2 * HD + 16, rows] = hot.astype(F32).astype(BF)
            v = qkv_ref[rows, 2 * HD :].astype(F32)
            lane = lax.broadcasted_iota(jnp.int32, (CK, HD), 1)
            vaug[rows, :] = jnp.concatenate([v, (lane < 3).astype(F32)], axis=1).astype(BF)
            dkv[rows, :] = jnp.zeros((CK, 2 * HD), F32)
        dtab_ref[...] = jnp.zeros_like(dtab_ref)
        fetch.start()

    q = qkv_ref[pl.ds(pl.multiple_of(i * TB, TB), TB), :HD]
    doT = jnp.concatenate([doT_ref[j].astype(F32) for j in range(side)], axis=1)
    delta = -jnp.sum(doT * oTf_ref[...], axis=0, keepdims=True)
    d1 = delta.astype(BF).astype(F32)
    d2 = (delta - d1).astype(BF).astype(F32)
    pad = jnp.concatenate([d1, d2, delta - d1 - d2, jnp.zeros((HD - 3, TB), F32)], axis=0)
    doa = jnp.concatenate([doT, pad], axis=0).astype(BF)
    do = jnp.concatenate([doT, jnp.zeros((HD, TB), F32)], axis=0).T
    qz = jnp.concatenate([jnp.zeros((TB, HD), F32), q.astype(F32)], axis=1)
    doq = jnp.concatenate([do, qz], axis=0).astype(BF)
    dqa[...] = jnp.zeros_like(dqa)

    def grad_probs(c):
        return dot(vaug[c * CK : (c + 1) * CK, :], doa, NN)

    def grad_scores(c, dp):
        p = p_ref[0, c * CK : (c + 1) * CK, :].astype(F32) * f_ref[c : c + 1, :]
        return jnp.concatenate([p.astype(BF), (p * dp).astype(BF)], axis=1)

    def gather(c, pd):
        rows = slice(c * CK, (c + 1) * CK)
        dkv[rows, :] += dot(pd, doq, NN)
        g = dot(kta[:, rows], pd[:, TB:], NN)
        dqa[0 : 2 * HD, :] += g[: 2 * HD]
        dqa[2 * HD + c * ROWS : 2 * HD + (c + 1) * ROWS, :] = g[2 * HD : 2 * HD + ROWS]

    dp, before = grad_probs(0), None
    for c in range(n_chunks):
        following = grad_probs(c + 1) if c + 1 < n_chunks else None
        if before is not None:
            gather(c - 1, before)
        before, dp = grad_scores(c, dp), following
    gather(n_chunks - 1, before)

    grads = dqa[HD : 3 * HD, :].T
    lane = lax.broadcasted_iota(jnp.int32, (TB, 2 * GRID), 1)
    gcol = jnp.where(lane < GRID, grads, 0.0)
    grow = jnp.where(lane >= GRID, grads, 0.0)
    rs, cs = [], []
    col = lax.broadcasted_iota(jnp.int32, (GRID, 2 * GRID), 0)
    for g in range(tg):
        sl = slice(g * GRID, (g + 1) * GRID)
        rs.append(pltpu.roll(grow[sl], GRID - (i * tg + g), 1))
        x = gcol[sl]
        for bit in range(6):
            x = jnp.where((col >> bit) & 1 == 1, pltpu.roll(x, 2 * GRID - (1 << bit), 1), x)
        cs.append(x)
    drow = jnp.concatenate(rs, axis=0).astype(BF)
    dcol = jnp.concatenate(cs, axis=0).astype(BF)
    dq = dqa[:HD, :] * HD ** -0.5
    dq = dq + dot(tab_ref[0], drow, (((0,), (1,)), ((), ())))
    dq = dq + dot(tab_ref[1], dcol, (((0,), (1,)), ((), ())))
    for j in range(side):
        msg_ref[i * side + j, 0:HD, :] = dq[:, j * CK : (j + 1) * CK].astype(BF)
    dtab_ref[0:HD, :] += dot(q, drow, TN)
    dtab_ref[HD : 2 * HD, :] += dot(q, dcol, TN)

    @pl.when(i == n_steps - 1)
    def _():
        for c in range(n_chunks):
            both = dkv[c * CK : (c + 1) * CK, :].T
            msg_ref[c, HD : 2 * HD, :] = (both[HD:] * HD ** -0.5).astype(BF)
            msg_ref[c, 2 * HD : 3 * HD, :] = both[:HD].astype(BF)
        fetch.wait()
        all_grads = jnp.concatenate([msg_ref[c, : 3 * HD, :] for c in range(n_chunks)], axis=1)
        moment = dot(all_grads, x_ref[...], NN).T
        total = dot(jnp.ones((8, all_grads.shape[1]), BF), all_grads, NT)
        hi = total.astype(BF).astype(F32)
        row = lax.broadcasted_iota(jnp.int32, total.shape, 0)
        ending = jnp.where(row == 0, hi, jnp.where(row == 1, total - hi, 0.0))
        part = moment.shape[0] // (dps * seqs)
        half = dps // 2
        base = msg_ref.shape[1] - 16
        for d in range(dps * seqs if far_ref else 0):
            piece = jnp.concatenate([moment[d * part : (d + 1) * part], ending], axis=0)
            fill = jnp.zeros((part + 8, HD), F32)
            far_ref[0][d] = jnp.concatenate([piece, fill], axis=1).astype(BF)
        for s in range(seqs):
            if not far_ref:
                sides = []
                for side in range(2):
                    tops = [(d * seqs + s) * part for d in range(side * half, (side + 1) * half)]
                    sides.append(jnp.concatenate([moment[t : t + part] for t in tops], axis=0))
                sides.append(jnp.zeros((half * part, CK - 6 * HD), F32))
                msg_ref[s, 3 * HD : base, :] = jnp.concatenate(sides, axis=1).astype(BF)
            piece = dtab_ref[s * 16 : (s + 1) * 16, :]
            hi = piece.astype(BF).astype(F32)
            sums = jnp.concatenate([ending, jnp.zeros((8, 3 * HD), F32)], axis=0)
            fill = jnp.zeros((16, CK - 7 * HD), F32)
            row = jnp.concatenate([hi, piece - hi, sums, fill], axis=1)
            msg_ref[s, base:, :] = row.astype(BF)


def heads_backward(dps, seqs, p, last, qkv, tab, probs, factors, oTf, x, doT):
    n, features = x.shape
    steps, chunks, side = n // TB, n // CK, TB // CK
    part = features // (dps * seqs)
    shapes = [(chunks, 3 * HD + 16 + (0 if last else dps // 2 * part), CK)]
    if last:
        shapes.append((dps * seqs, part + 8, 4 * HD))
    return pl.pallas_call(
        partial(bwd_kernel, n // CK, dps, seqs),
        grid=(steps,),
        in_specs=[
            pl.BlockSpec((n, 3 * HD), lambda i: (0, 0)),
            pl.BlockSpec((2, 2 * GRID, HD), lambda i: (0, 0, 0)),
            pl.BlockSpec((1, n, TB), lambda i: (i, 0, 0)),
            pl.BlockSpec((chunks, TB), lambda i: (0, i)),
            pl.BlockSpec((HD, TB), lambda i: (0, i)),
            pl.BlockSpec((side, HD, CK), lambda i: (i, p, 0)),
            pl.BlockSpec(memory_space=pl.ANY),
        ],
        out_specs=[pl.BlockSpec(shape, lambda i: (0, 0, 0)) for shape in shapes],
        out_shape=[jax.ShapeDtypeStruct(shape, BF) for shape in shapes],
        scratch_shapes=[
            pltpu.VMEM((n, 2 * HD), BF),
            pltpu.VMEM((2 * HD + 16, n), BF),
            pltpu.VMEM((n, 2 * HD), F32),
            pltpu.VMEM((3 * HD, TB), F32),
            pltpu.VMEM((2 * HD, 2 * GRID), F32),
            pltpu.VMEM((n, features), BF),
            pltpu.SemaphoreType.DMA,
        ],
        compiler_params=pltpu.CompilerParams(vmem_limit_bytes=56 * 2**20),
        cost_estimate=pl.CostEstimate(
            flops=8 * n * n * 4 * HD, bytes_accessed=48 * 2**20, transcendentals=0
        ),
    )(qkv, tab, probs, factors, oTf, doT, x)


def qkv_kernel(per, steps, n_held, here_ref, *refs):
    blocks, rest = refs[:steps], refs[steps:]
    w_ref, par_ref, bias_ref = rest[:3]
    x_ref, *outs, held, sems = rest[3 + n_held :]
    m = pl.program_id(0)
    copies = [
        pltpu.make_async_copy(blocks[j], held.at[j], sems.at[j]) for j in range(len(blocks))
    ]

    @pl.when(m == 0)
    def _():
        for copy in copies:
            copy.start()

    for j, copy in enumerate(copies):

        @pl.when(m == j)
        def _():
            copy.wait()

    v = held[m].astype(F32)
    v = v - jnp.mean(v, axis=-1, keepdims=True)
    v = v * lax.rsqrt(jnp.mean(v * v, axis=-1, keepdims=True) + EPS)
    x_ref[...] = v.astype(BF)
    x = (v * par_ref[0:1, :] + par_ref[1:2, :]).astype(BF)
    qkv = dot(x, w_ref[...], NN) + bias_ref[...]
    for p in range(per):
        outs[p][...] = qkv[:, p * 3 * HD : (p + 1) * 3 * HD].astype(BF)


def normed_qkv(here, first, total, blocks, w_cols, params, bias, before):
    rows, features = blocks[0].shape
    wide = w_cols.shape[1]
    per, steps = wide // (3 * HD), len(blocks)
    place = lambda m, here: ((m + first) ^ here[0], 0)
    return pl.pallas_call(
        partial(qkv_kernel, per, steps, len(before)),
        grid_spec=pltpu.PrefetchScalarGridSpec(
            num_scalar_prefetch=1,
            grid=(steps,),
            in_specs=[pl.BlockSpec(memory_space=pl.ANY)] * steps
            + [
                pl.BlockSpec((features, wide), lambda m, here: (0, 0)),
                pl.BlockSpec((2, features), lambda m, here: (0, 0)),
                pl.BlockSpec((1, wide), lambda m, here: (0, 0)),
            ]
            + [pl.BlockSpec(memory_space=pl.ANY)] * len(before),
            out_specs=[pl.BlockSpec((rows, features), place)]
            + [pl.BlockSpec((rows, 3 * HD), place)] * per,
            scratch_shapes=[
                pltpu.VMEM((steps, rows, features), BF),
                pltpu.SemaphoreType.DMA((steps,)),
            ],
        ),
        out_shape=[jax.ShapeDtypeStruct((total * rows, features), BF)]
        + [jax.ShapeDtypeStruct((total * rows, 3 * HD), BF)] * per,
        input_output_aliases={4 + steps + j: j for j in range(len(before))},
        compiler_params=pltpu.CompilerParams(vmem_limit_bytes=56 * 2**20),
        cost_estimate=pl.CostEstimate(
            flops=2 * steps * rows * features * wide, bytes_accessed=24 * 2**20, transcendentals=0
        ),
    )(here.reshape(1).astype(jnp.int32), *blocks, w_cols, params, bias, *before)


def mirror(tables):
    hole = jnp.zeros((2, 1, HD), tables.dtype)
    return jnp.concatenate([tables[:, GRID - 1 :: -1], hole, tables[:, : GRID - 1 : -1]], axis=1)


def unmirror(grads):
    return jnp.concatenate([grads[:, GRID - 1 :: -1], grads[:, : GRID : -1]], axis=1)


def attended_rows(ahead_ref, ending_ref, slots):
    images = ahead_ref.shape[0] // slots
    sides = []
    for y in range(images):
        parts = []
        for g in range(slots):
            parts += [ahead_ref[y * slots + g], ending_ref[y * slots + g]]
        sides.append(jnp.concatenate(parts, axis=0))
    return jnp.concatenate(sides, axis=1)


def mlp_kernel(
    slots, ahead_ref, ending_ref, tok_ref, cot_ref, w1_ref, w2_ref, wp_ref, par_ref, b1_ref,
    act_ref, gp_ref, n2_ref, mixed_ref, gm_ref, gb_ref, ga_ref, sum_ref, sb1_ref,
    hat_ref, rate_ref, gn_ref
):
    k, last = pl.program_id(0), pl.num_programs(0) - 1
    width = w1_ref.shape[1]
    sub = width // 3

    @pl.when(k == 0)
    def _():
        att = attended_rows(ahead_ref, ending_ref, slots)
        mixed = tok_ref[...].astype(F32) + dot(att, wp_ref[...], TN) + par_ref[0:1, :]
        mixed_ref[...] = mixed
        v = mixed - jnp.mean(mixed, axis=-1, keepdims=True)
        rate = lax.rsqrt(jnp.mean(v * v, axis=-1, keepdims=True) + EPS)
        hat = v * rate
        hat_ref[...] = hat
        rate_ref[...] = rate
        n2_ref[...] = (hat * par_ref[1:2, :] + par_ref[2:3, :]).astype(BF)
        gn_ref[...] = jnp.zeros_like(gn_ref)

    def products(j):
        cols = slice(j * sub, (j + 1) * sub)
        pre = dot(n2_ref[...], w1_ref[:, cols], NN) + b1_ref[:, cols]
        return pre, dot(cot_ref[...], w2_ref[cols, :], NT)

    def curves(j, pre, grad):
        cols = slice(j * sub, (j + 1) * sub)
        cdf = 0.5 + 0.5 * lax.erf(pre * 0.5**0.5)
        act_ref[:, cols] = (pre * cdf).astype(BF)
        slope = cdf + pre * (jnp.exp(-0.5 * pre * pre) * (2.0 * math.pi) ** -0.5)
        g = (grad * slope).astype(BF)
        gp_ref[:, cols] = g
        sb1_ref[:, cols] = jnp.sum(g.astype(F32), axis=0, keepdims=True)

    now = products(0)
    for j in range(3):
        following = products(j + 1) if j < 2 else None
        curves(j, *now)
        now = following
    gn_ref[...] += dot(gp_ref[...], w1_ref[...], NT)

    @pl.when(k == last)
    def _():
        gn, hat, cot = gn_ref[...], hat_ref[...], cot_ref[...].astype(F32)
        u = gn * par_ref[1:2, :]
        back = u - jnp.mean(u, axis=-1, keepdims=True)
        back = back - hat * jnp.mean(u * hat, axis=-1, keepdims=True)
        gm = cot + rate_ref[...] * back
        gm_ref[...] = gm
        gb = gm.astype(BF)
        gb_ref[...] = gb
        sum_ref[0:1, :] = jnp.sum(gb.astype(F32), axis=0, keepdims=True)
        sum_ref[1:2, :] = jnp.sum(cot, axis=0, keepdims=True)
        sum_ref[2:3, :] = jnp.sum(gn * hat, axis=0, keepdims=True)
        sum_ref[3:4, :] = jnp.sum(gn, axis=0, keepdims=True)
        sum_ref[4:8, :] = jnp.zeros((4, gn.shape[1]), F32)
        att = dot(wp_ref[...], gb_ref[...], NT).astype(BF)
        seqs, wide, rows = ga_ref.shape
        for s in range(seqs):
            y, g = s // slots, s % slots
            ga_ref[s] = att[g * wide : (g + 1) * wide, y * rows : (y + 1) * rows]


def mlp_critical(slots, ahead, ending, tokens, cot, whole, params, b1):
    seqs, ahead_rows, rows_img = ahead.shape
    rows, features = tokens.shape
    blocks = (whole.shape[1] // features - 1) // 2
    hidden = blocks * features
    const2 = lambda k: (0, 0)
    const3 = lambda k: (0, 0, 0)
    return pl.pallas_call(
        partial(mlp_kernel, slots),
        grid=(blocks,),
        in_specs=[
            pl.BlockSpec(ahead.shape, const3),
            pl.BlockSpec(ending.shape, const3),
            pl.BlockSpec((rows, features), const2),
            pl.BlockSpec((rows, features), const2),
            pl.BlockSpec((features, features), lambda k: (0, k)),
            pl.BlockSpec((features, features), lambda k: (0, blocks + k)),
            pl.BlockSpec((features, features), lambda k: (0, 2 * blocks)),
            pl.BlockSpec((8, features), const2),
            pl.BlockSpec((1, features), lambda k: (0, k)),
        ],
        out_specs=[
            pl.BlockSpec((rows, features), lambda k: (0, k)),
            pl.BlockSpec((rows, features), lambda k: (0, k)),
            pl.BlockSpec((rows, features), const2),
            pl.BlockSpec((rows, features), const2),
            pl.BlockSpec((rows, features), const2),
            pl.BlockSpec((rows, features), const2),
            pl.BlockSpec((seqs, ahead_rows + HD, rows_img), const3),
            pl.BlockSpec((8, features), const2),
            pl.BlockSpec((1, features), lambda k: (0, k)),
        ],
        out_shape=[
            jax.ShapeDtypeStruct((rows, hidden), BF),
            jax.ShapeDtypeStruct((rows, hidden), BF),
            jax.ShapeDtypeStruct((rows, features), BF),
            jax.ShapeDtypeStruct((rows, features), F32),
            jax.ShapeDtypeStruct((rows, features), F32),
            jax.ShapeDtypeStruct((rows, features), BF),
            jax.ShapeDtypeStruct((seqs, ahead_rows + HD, rows_img), BF),
            jax.ShapeDtypeStruct((8, features), F32),
            jax.ShapeDtypeStruct((1, hidden), F32),
        ],
        scratch_shapes=[
            pltpu.VMEM((rows, features), F32),
            pltpu.VMEM((rows, 1), F32),
            pltpu.VMEM((rows, features), F32),
        ],
        compiler_params=pltpu.CompilerParams(vmem_limit_bytes=60 * 2**20),
        cost_estimate=pl.CostEstimate(
            flops=2 * rows * features * (3 * hidden + 2 * features),
            bytes_accessed=40 * 2**20,
            transcendentals=2 * rows * hidden,
        ),
    )(ahead, ending, tokens, cot, whole, whole, whole, params, b1)


def grads_kernel(
    slots, blocks, ahead_ref, ending_ref, cot_ref, act_ref, gp_ref, n2_ref, gb_ref, mixed_ref,
    w2_ref, par_ref, out_ref, res_ref, n2T_ref, acc_ref
):
    k = pl.program_id(0)

    @pl.when(k == 0)
    def _():
        n2T_ref[...] = n2_ref[...].T
        acc_ref[...] = mixed_ref[...] + par_ref[3:4, :]

    @pl.when(k < blocks)
    def _():
        out_ref[...] = dot(n2T_ref[...], gp_ref[...], NN).astype(BF)

    @pl.when((k >= blocks) & (k < 2 * blocks))
    def _():
        act = act_ref[...]
        out_ref[...] = dot(act, cot_ref[...], TN).astype(BF)
        acc_ref[...] += dot(act, w2_ref[...], NN)

    @pl.when(k == 2 * blocks)
    def _():
        att = attended_rows(ahead_ref, ending_ref, slots)
        out_ref[...] = dot(att, gb_ref[...], NN).astype(BF)
        res_ref[...] = acc_ref[...].astype(BF)


def mlp_grads(slots, ahead, ending, cot, act, gp, n2, gb, mixed, whole, params):
    rows, features = cot.shape
    blocks = act.shape[1] // features
    const2 = lambda k: (0, 0)
    const3 = lambda k: (0, 0, 0)
    at1 = lambda k: jnp.minimum(k, blocks - 1)
    at2 = lambda k: jnp.clip(k - blocks, 0, blocks - 1)
    return pl.pallas_call(
        partial(grads_kernel, slots, blocks),
        grid=(2 * blocks + 1,),
        in_specs=[
            pl.BlockSpec(ahead.shape, const3),
            pl.BlockSpec(ending.shape, const3),
            pl.BlockSpec((rows, features), const2),
            pl.BlockSpec((rows, features), lambda k: (0, at2(k))),
            pl.BlockSpec((rows, features), lambda k: (0, at1(k))),
            pl.BlockSpec((rows, features), const2),
            pl.BlockSpec((rows, features), const2),
            pl.BlockSpec((rows, features), const2),
            pl.BlockSpec((features, features), lambda k: (0, blocks + at2(k))),
            pl.BlockSpec((8, features), const2),
        ],
        out_specs=[
            pl.BlockSpec((features, features), lambda k: (0, k)),
            pl.BlockSpec((rows, features), const2),
        ],
        out_shape=[
            jax.ShapeDtypeStruct((features, (2 * blocks + 1) * features), BF),
            jax.ShapeDtypeStruct((rows, features), BF),
        ],
        scratch_shapes=[pltpu.VMEM((features, rows), BF), pltpu.VMEM((rows, features), F32)],
        compiler_params=pltpu.CompilerParams(vmem_limit_bytes=56 * 2**20),
        cost_estimate=pl.CostEstimate(
            flops=2 * rows * features * features * (3 * blocks + 1),
            bytes_accessed=40 * 2**20,
            transcendentals=0,
        ),
    )(ahead, ending, cot, act, gp, n2, gb, mixed, whole, params)


def inputs_kernel(per, *refs):
    sent, (w_ref, tok_ref, gm_ref, gain_ref, out_ref) = refs[:per], refs[per:]
    rows = [ref[g, : 3 * HD, :] for ref in sent for g in range(ref.shape[0])]
    grad = dot(w_ref[...], jnp.concatenate(rows, axis=0), NN).T
    v = tok_ref[...].astype(F32)
    v = v - jnp.mean(v, axis=-1, keepdims=True)
    rate = lax.rsqrt(jnp.mean(v * v, axis=-1, keepdims=True) + EPS)
    hat = v * rate
    u = grad * gain_ref[...]
    back = u - jnp.mean(u, axis=-1, keepdims=True)
    back = back - hat * jnp.mean(u * hat, axis=-1, keepdims=True)
    out_ref[...] = (gm_ref[...] + rate * back).astype(BF)


def input_grads(slots, sent, w, tokens, grad_mixed, gain):
    rows, features = tokens.shape
    images = sent[0].shape[0] // slots
    side = rows // images
    const = lambda y: (0, 0)
    own = lambda y: (y, 0)
    return pl.pallas_call(
        partial(inputs_kernel, len(sent)),
        grid=(images,),
        in_specs=[pl.BlockSpec((slots,) + s.shape[1:], lambda y: (y, 0, 0)) for s in sent]
        + [
            pl.BlockSpec(w.shape, const),
            pl.BlockSpec((side, features), own),
            pl.BlockSpec((side, features), own),
            pl.BlockSpec((1, features), const),
        ],
        out_specs=pl.BlockSpec((side, features), own),
        out_shape=jax.ShapeDtypeStruct((rows, features), BF),
        compiler_params=pltpu.CompilerParams(vmem_limit_bytes=56 * 2**20),
        cost_estimate=pl.CostEstimate(
            flops=2 * rows * features * w.shape[1], bytes_accessed=16 * 2**20, transcendentals=0
        ),
    )(*sent, w, tokens, grad_mixed, gain)


def ordered_kernel(size, blocks, sum_ref, w1_ref, w2_ref, wp_ref):
    part = sum_ref.shape[0]
    features = part * size
    hidden = blocks * features
    sums = sum_ref[...].astype(F32)
    pieces = []
    for d in range(size):
        for k in range(blocks):
            at = k * features + d * part
            pieces.append(sums[:, at : at + part])
    w1_ref[...] = jnp.concatenate(pieces, axis=1)
    for k in range(blocks):
        w2_ref[k * part : (k + 1) * part, :] = sums[:, hidden + k * features :][:, :features]
    wp_ref[...] = sums[:, 2 * hidden :]


def ordered_grads(size, blocks, sums):
    part = sums.shape[0]
    features = part * size
    return pl.pallas_call(
        partial(ordered_kernel, size, blocks),
        out_shape=[
            jax.ShapeDtypeStruct((part, blocks * features), F32),
            jax.ShapeDtypeStruct((blocks * part, features), F32),
            jax.ShapeDtypeStruct((part, features), F32),
        ],
        compiler_params=pltpu.CompilerParams(vmem_limit_bytes=32 * 2**20),
        cost_estimate=pl.CostEstimate(flops=0, bytes_accessed=2**20, transcendentals=0),
    )(sums)


def swap(block, bit, size):
    return lax.ppermute(block, "seq", [(i, i ^ bit) for i in range(size)])


def halves(values):
    hi = lax.reduce_precision(values, 8, 7)
    return [hi.astype(BF), (values - hi).astype(BF)]


def body_heads(
    tokens,
    w_qkv,
    qv_bias,
    w_proj,
    proj_bias,
    w_fc1,
    fc1_bias,
    w_fc2,
    fc2_bias,
    norm_gains,
    norm_biases,
    rel_tables,
    cotangent,
):
    images, rows_img, features = tokens.shape
    dps, seqs = lax.axis_size("dp"), lax.axis_size("seq")
    size = dps * seqs
    slots = seqs // images
    per = HEADS // slots
    part = features // size
    wide = per * 3 * HD
    hidden = fc1_bias.shape[0] * size
    blocks = hidden // features
    here = lax.axis_index("seq")
    image, slot = here // slots, here % slots
    rows = images * rows_img

    own = lax.dynamic_index_in_dim(tokens, image, 0, keepdims=False)
    other = lax.dynamic_index_in_dim(tokens, 1 - image, 0, keepdims=False)
    small = jnp.concatenate(
        [
            qv_bias,
            proj_bias,
            fc1_bias,
            fc2_bias,
            norm_gains.reshape(-1),
            norm_biases.reshape(-1),
        ]
    )
    lengths = [2 * part, part, blocks * part, part, 2 * part, 2 * part]
    small = jnp.pad(small, (0, wide - small.shape[0])).reshape(1, 1, wide)
    by_head = w_qkv.reshape(part, 3, slots, per, HD)
    to_slots = by_head.transpose(2, 0, 3, 1, 4).reshape(slots, part, wide)
    to_slots = jnp.concatenate([to_slots, jnp.broadcast_to(small, (slots, 8, wide))], axis=1)
    to_slots, own, other = lax.optimization_barrier(
        (jnp.tile(to_slots, (dps * images, 1, 1)), own, other)
    )
    cols = lax.all_to_all(to_slots, AXES, 0, 0, tiled=True)
    own_x, got = swap(own, 2, seqs), swap(other, 4, seqs)
    own_x, got = lax.optimization_barrier((own_x, got))
    got_x = swap(got, 2, seqs)
    w_cols = cols[:, :part].reshape(features, wide)
    smalls = cols[:, part]
    edges = [sum(lengths[:j]) for j in range(len(lengths) + 1)]
    cut = [smalls[:, a:b].astype(F32) for a, b in zip(edges[:-1], edges[1:])]
    bqv, bp, b2 = cut[0].reshape(-1), cut[1].reshape(-1), cut[3].reshape(-1)
    b1 = cut[2].reshape(size, blocks, part).transpose(1, 0, 2).reshape(-1)
    gains = cut[4].reshape(size, 2, part).transpose(1, 0, 2).reshape(2, features)
    shifts = cut[5].reshape(size, 2, part).transpose(1, 0, 2).reshape(2, features)

    full_bias = jnp.stack(
        [
            bqv[:features].reshape(slots, per, HD),
            jnp.zeros((slots, per, HD), F32),
            bqv[features:].reshape(slots, per, HD),
        ],
        axis=2,
    ).reshape(slots, wide)
    own_bias = lax.dynamic_index_in_dim(full_bias, slot, 0, keepdims=True)
    first_norm = jnp.stack([gains[0], shifts[0]])
    by_mask = [own, swap(own, 1, seqs), own_x, swap(own_x, 1, seqs), got, swap(got, 1, seqs)]
    held = normed_qkv(here, 0, seqs, by_mask, w_cols, first_norm, own_bias, [])
    by_mask = [got_x, swap(got_x, 1, seqs)]
    hat_all, *qkv = normed_qkv(here, 6, seqs, by_mask, w_cols, first_norm, own_bias, held)

    w1_local = w_fc1.reshape(part, size, blocks, part).transpose(0, 2, 1, 3).reshape(part, hidden)
    w2_local = w_fc2.reshape(blocks, part, features).transpose(1, 0, 2).reshape(part, hidden)
    wq_local = by_head.transpose(0, 3, 2, 1, 4).reshape(part, 3 * features)
    whole = jnp.concatenate([w1_local, w2_local, w_proj], axis=1)
    whole = lax.optimization_barrier((whole, got_x, held[1]))[0]
    whole = lax.all_gather(whole, AXES, axis=0, tiled=True)

    tab = mirror(rel_tables)
    kept, joint = [], ()
    for p in range(per - 1):
        out, *saved = heads_forward(qkv[p], tab, per - 1, p, joint)
        kept.append([qkv[p], tab, saved[1], saved[2], saved[0], hat_all])
        joint = (out,)
    qkv[-1] = lax.optimization_barrier((qkv[-1], out))[0]
    ahead = lax.all_to_all(out, "seq", 0, 0, tiled=True)
    ending, *saved = heads_forward(qkv[-1], tab)
    kept.append([qkv[-1], tab, saved[1], saved[2], saved[0], hat_all])
    ending = lax.optimization_barrier((ending, ahead))[0]
    ending = lax.all_to_all(ending, "seq", 0, 0, tiled=True)

    wq_local = lax.optimization_barrier((wq_local, ahead, ending))[0]
    wq = lax.all_gather(wq_local, AXES, axis=0, tiled=True)

    params = jnp.concatenate(
        [jnp.stack([bp, gains[1], shifts[1], b2]), jnp.zeros((4, features), F32)]
    )
    b1 = b1[None]
    ending, params, b1 = lax.optimization_barrier((ending, params, b1))
    cot = cotangent.reshape(rows, features)
    act, grad_pre, normed2, mixed, grad_mixed, grad_branch, grad_att, sums, sum_b1 = mlp_critical(
        slots, ahead, ending, tokens.reshape(rows, features), cot, whole, params, b1
    )
    grad_att = lax.all_to_all(grad_att, "seq", 0, 0, tiled=True)
    grads, result = mlp_grads(
        slots, ahead, ending, cot, act, grad_pre, normed2, grad_branch, mixed, whole, params
    )
    result = result.reshape(tokens.shape)
    summed = lax.psum_scatter(grads, AXES, scatter_dimension=0, tiled=True)
    w_fc1_grad, w_fc2_grad, w_proj_grad = ordered_grads(size, blocks, summed)
    sum_b1 = sum_b1.reshape(blocks, size, part).transpose(1, 0, 2).reshape(size, blocks * part)
    early = jnp.concatenate(
        [
            sums[0].reshape(size, part),
            sum_b1,
            sums[1].reshape(size, part),
            sums[2].reshape(size, part),
            sums[3].reshape(size, part),
        ],
        axis=1,
    )

    table = jnp.zeros((16, 2 * GRID), F32)
    sent_on, messages = [], []
    for p in range(per):
        do_p = grad_att
        if p == 0:
            kept[0][0] = lax.optimization_barrier((kept[0][0], grads))[0]
        message, *far = heads_backward(dps, seqs, p, p == per - 1, *kept[p], do_p)
        message = lax.all_to_all(message, "seq", 0, 0, tiled=True)
        if p == per - 1:
            sent_on = jnp.stack(sent_on, axis=1)
            level = lax.axis_index("dp")
            products = lax.dynamic_index_in_dim(sent_on, level, 0, keepdims=False).astype(F32)
            for m in range(1, dps):
                block = lax.dynamic_index_in_dim(sent_on, level ^ m, 0, keepdims=False)
                block = lax.ppermute(block, "dp", [(i, i ^ m) for i in range(dps)])
                products = products + block.astype(F32)
            message, products = lax.optimization_barrier((message, products))
        messages.append(message)
        base = message.shape[1] - 16
        pair = message[:, base:, : 4 * GRID].astype(F32)
        table = table + jnp.sum(pair[..., : 2 * GRID] + pair[..., 2 * GRID :], axis=0)
        if p < per - 1:
            moment = message[:, 3 * HD : base, : 6 * HD].astype(F32)
            moment = jnp.sum(moment.reshape(images, slots, dps // 2 * part, 6 * HD), axis=0)
            moment = moment.reshape(slots, dps // 2, part, 2, 3 * HD).transpose(3, 1, 0, 2, 4)
            total = message[:, base : base + 2, 4 * GRID : 4 * GRID + 3 * HD].astype(F32)
            total = jnp.sum(total.reshape(images, slots, 2, 3 * HD), axis=(0, 2))
            total = jnp.pad(jnp.stack(halves(total), axis=1), ((0, 0), (0, 6), (0, 0)))
            total = jnp.broadcast_to(total, (dps,) + total.shape)
            by_owner = jnp.concatenate(
                [moment.reshape(dps, slots, part, 3 * HD).astype(BF), total], axis=2
            )
            sent_on.append(by_owner)
    pieces = table.astype(BF).reshape(8, 4 * GRID)
    pieces = jnp.broadcast_to(pieces, (size,) + pieces.shape)
    sums = jnp.stack(halves(early), axis=1)
    sums = jnp.pad(sums, ((0, 0), (2, 4), (0, 4 * GRID - 8 * part)))
    far = jnp.concatenate([far[0][:, :part], far[0][:, part:] + sums, pieces], axis=1)
    far = lax.all_to_all(far, AXES, 0, 0, tiled=True)
    tokens_grad = input_grads(
        slots, messages, wq, tokens.reshape(rows, features), grad_mixed, gains[:1]
    ).reshape(tokens.shape)
    far, tokens_grad = lax.optimization_barrier((far, tokens_grad))
    final = far[:, : part + 8, : 3 * HD].astype(F32).reshape(dps * images, slots, part + 8, 3 * HD)
    products = jnp.concatenate([products, jnp.sum(final, axis=0)[None]])
    moments = products[:, :, :part].swapaxes(0, 1)
    totals = (products[:, :, part] + products[:, :, part + 1]).swapaxes(0, 1)
    bundle = jnp.sum(far[:, part + 2 : part + 4, : 8 * part].astype(F32), axis=(0, 1))
    table = far[:, part + 8 :].astype(F32).reshape(dps, seqs * 16, 2 * GRID)
    table = jnp.sum(table, axis=0).reshape(2, HD, 2 * GRID)
    rel_tables_grad = unmirror(table.swapaxes(1, 2))

    moment = moments.reshape(slots, per, part, 3, HD)
    moment = moment.transpose(2, 3, 0, 1, 4).reshape(part, 3 * features)
    total = totals.reshape(slots, per, 3, HD)
    total = total.transpose(2, 0, 1, 3).reshape(3 * features)
    own_gain, own_shift = norm_gains[0].astype(F32), norm_biases[0].astype(F32)
    w_qkv_grad = own_gain[:, None] * moment + own_shift[:, None] * total
    w_own = w_qkv.astype(F32)
    gain0, shift0 = jnp.sum(w_own * moment, axis=1), jnp.sum(w_own * total, axis=1)
    device = lax.axis_index("dp") * seqs + here
    total = jnp.concatenate([total[:features], total[2 * features :]]).reshape(size, 2 * part)
    qv_bias_grad = lax.dynamic_index_in_dim(total, device, 0, keepdims=False)

    ends = [part * end for end in [0, 1, 1 + blocks, 2 + blocks, 3 + blocks, 4 + blocks]]
    bundle = [bundle[a:b] for a, b in zip(ends[:-1], ends[1:])]
    proj_bias_grad, fc1_bias_grad, fc2_bias_grad, gain1, shift1 = bundle
    norm_gains_grad = jnp.stack([gain0, gain1])
    norm_biases_grad = jnp.stack([shift0, shift1])
    return (
        result,
        tokens_grad,
        w_qkv_grad,
        qv_bias_grad,
        w_proj_grad,
        proj_bias_grad,
        w_fc1_grad,
        fc1_bias_grad,
        w_fc2_grad,
        fc2_bias_grad,
        norm_gains_grad,
        norm_biases_grad,
        rel_tables_grad,
    )


def layer_norm(values, gain, shift):
    center = jnp.mean(values, axis=-1, keepdims=True)
    centered = values - center
    spread = jnp.mean(centered * centered, axis=-1, keepdims=True)
    return centered * lax.rsqrt(spread + EPS) * gain + shift


def fetch_each(weights):
    return (
        lax.all_gather(weights[0], ("dp", "seq"), axis=0, tiled=True),
        lax.all_gather(weights[1], ("dp", "seq"), axis=0, tiled=True),
        lax.all_gather(weights[2], ("dp", "seq"), axis=0, tiled=True),
        lax.all_gather(weights[3], ("dp", "seq"), axis=0, tiled=True),
        lax.all_gather(weights[4], ("dp", "seq"), axis=0, tiled=True),
        lax.all_gather(weights[5], ("dp", "seq"), axis=0, tiled=True),
        lax.all_gather(weights[6], ("dp", "seq"), axis=0, tiled=True),
        lax.all_gather(weights[7], ("dp", "seq"), axis=0, tiled=True),
        lax.all_gather(weights[8], ("dp", "seq"), axis=1, tiled=True),
        lax.all_gather(weights[9], ("dp", "seq"), axis=1, tiled=True),
    )


def position_rows(tables, rows_img):
    beginning = lax.axis_index("seq") * rows_img
    tokens_at = beginning + jnp.arange(rows_img, dtype=jnp.int32)
    offsets = jnp.arange(GRID, dtype=jnp.int32)
    entries = jnp.arange(TABLE, dtype=jnp.int32)
    row_index = tokens_at[:, None] // GRID - offsets[None, :] + GRID - 1
    col_index = tokens_at[:, None] % GRID - offsets[None, :] + GRID - 1
    row_hot = (row_index[:, :, None] == entries[None, None, :]).astype(jnp.float32)
    col_hot = (col_index[:, :, None] == entries[None, None, :]).astype(jnp.float32)
    tables_f = tables.astype(jnp.float32)
    rel_rows = jnp.einsum("rkt,tc->rkc", row_hot, tables_f[0], precision=HIGH)
    rel_cols = jnp.einsum("rkt,tc->rkc", col_hot, tables_f[1], precision=HIGH)
    return (row_hot, col_hot, rel_rows, rel_cols)


def score_block(queries, keys_all, rows_low, cols_low):
    rows_img = queries.shape[0]
    product = jnp.einsum(
        "rhc,nhc->hrn", queries, keys_all, preferred_element_type=jnp.float32
    ) * HD ** (-0.5)
    bias_rows = jnp.einsum("rhc,rkc->hrk", queries, rows_low, preferred_element_type=jnp.float32)
    bias_cols = jnp.einsum("rhc,rkc->hrk", queries, cols_low, preferred_element_type=jnp.float32)
    joined = (
        product.reshape(HEADS, rows_img, GRID, GRID)
        + bias_rows[:, :, :, None]
        + bias_cols[:, :, None, :]
    )
    return joined.reshape(HEADS, rows_img, GRID * GRID)


def attend_forward(qkv_img, kv_pair, rows_low, cols_low):
    rows_img, triple = qkv_img.shape
    features = triple // 3
    queries = qkv_img[:, :features].reshape(rows_img, HEADS, HD)
    keys_all = kv_pair[0].reshape(-1, HEADS, HD)
    values_all = kv_pair[1].reshape(-1, HEADS, HD)
    scores = score_block(queries, keys_all, rows_low, cols_low)
    largest = jnp.max(scores, axis=-1, keepdims=True)
    shifted = jnp.exp(scores - largest)
    totals = jnp.sum(shifted, axis=-1, keepdims=True)
    probs_low = (shifted / totals).astype(jnp.bfloat16)
    attended = jnp.einsum("hrn,nhc->rhc", probs_low, values_all, preferred_element_type=jnp.float32)
    log_totals = largest[..., 0] + jnp.log(totals[..., 0])
    return (attended.reshape(rows_img, features).astype(jnp.bfloat16), log_totals)


def attend_backward(qkv_img, log_totals, grad_att, kv_pair, rel_rows, rel_cols, rows_low, cols_low):
    rows_img, triple = qkv_img.shape
    features = triple // 3
    scale = HD ** (-0.5)
    queries = qkv_img[:, :features].reshape(rows_img, HEADS, HD)
    keys_all = kv_pair[0].reshape(-1, HEADS, HD)
    values_all = kv_pair[1].reshape(-1, HEADS, HD)
    scores = score_block(queries, keys_all, rows_low, cols_low)
    probs = jnp.exp(scores - log_totals[..., None])
    probs_low = probs.astype(jnp.bfloat16)
    grad_heads = grad_att.reshape(rows_img, HEADS, HD)
    grad_probs = jnp.einsum(
        "rhc,nhc->hrn", grad_heads, values_all, preferred_element_type=jnp.float32
    )
    inner_sum = jnp.sum(probs * grad_probs, axis=-1, keepdims=True)
    grad_scores = (probs * (grad_probs - inner_sum)).astype(jnp.bfloat16)
    grad_queries = (
        jnp.einsum("hrn,nhc->rhc", grad_scores, keys_all, preferred_element_type=jnp.float32)
        * scale
    )
    grid_scores = grad_scores.reshape(HEADS, rows_img, GRID, GRID)
    grad_rows = jnp.sum(grid_scores, axis=3, dtype=jnp.float32)
    grad_cols = jnp.sum(grid_scores, axis=2, dtype=jnp.float32)
    grad_queries = grad_queries + jnp.einsum("hrk,rkc->rhc", grad_rows, rel_rows, precision=HIGH)
    grad_queries = grad_queries + jnp.einsum("hrk,rkc->rhc", grad_cols, rel_cols, precision=HIGH)
    query_f = queries.astype(jnp.float32)
    table_rows = jnp.einsum("hrk,rhc->rkc", grad_rows, query_f, precision=HIGH)
    table_cols = jnp.einsum("hrk,rhc->rkc", grad_cols, query_f, precision=HIGH)
    length = lax.axis_size("seq") * rows_img
    grad_keys = (
        jnp.einsum("hrn,rhc->nhc", grad_scores, queries, preferred_element_type=jnp.float32) * scale
    )
    grad_values = jnp.einsum(
        "hrn,rhc->nhc", probs_low, grad_heads, preferred_element_type=jnp.float32
    )
    key_grads = lax.psum_scatter(
        jnp.concatenate(
            [grad_keys.reshape(length, features), grad_values.reshape(length, features)], axis=1
        ),
        "seq",
        scatter_dimension=0,
        tiled=True,
    )
    grad_qkv = jnp.concatenate(
        [grad_queries.reshape(rows_img, features), key_grads], axis=1
    ).astype(jnp.bfloat16)
    return (grad_qkv, table_rows, table_cols)


def body(
    tokens,
    w_qkv,
    qv_bias,
    w_proj,
    proj_bias,
    w_fc1,
    fc1_bias,
    w_fc2,
    fc2_bias,
    norm_gains,
    norm_biases,
    rel_tables,
    cotangent,
):
    images, rows_img, features = tokens.shape
    per_batch = images // MB
    weights = (
        w_qkv,
        qv_bias,
        w_proj,
        proj_bias,
        w_fc1,
        fc1_bias,
        w_fc2,
        fc2_bias,
        norm_gains,
        norm_biases,
    )
    row_hot, col_hot, rel_rows, rel_cols = position_rows(rel_tables, rows_img)
    rows_low = rel_rows.astype(jnp.bfloat16)
    cols_low = rel_cols.astype(jnp.bfloat16)
    stored = []
    outputs = []
    for batch_index in range(MB):
        gathered = fetch_each(weights)
        (
            wq_full,
            bqv_full,
            wp_full,
            bp_full,
            w1_full,
            b1_full,
            w2_full,
            b2_full,
            gains_full,
            shifts_full,
        ) = gathered
        gains_f = gains_full.astype(jnp.float32)
        shifts_f = shifts_full.astype(jnp.float32)
        inputs = (
            tokens[batch_index * per_batch : (batch_index + 1) * per_batch]
            .astype(jnp.float32)
            .reshape(-1, features)
        )
        normed1 = layer_norm(inputs, gains_f[0], shifts_f[0]).astype(jnp.bfloat16)
        full_bias = jnp.concatenate(
            [bqv_full[:features], jnp.zeros((features,), bqv_full.dtype), bqv_full[features:]]
        ).astype(jnp.float32)
        qkv = (jnp.dot(normed1, wq_full, preferred_element_type=jnp.float32) + full_bias).astype(
            jnp.bfloat16
        )
        qkv_images = qkv.reshape(per_batch, rows_img, 3 * features)

        def forward_image(carried, qkv_img):
            kv_pair = (
                lax.all_gather(qkv_img[:, features : 2 * features], "seq", axis=0, tiled=True),
                lax.all_gather(qkv_img[:, 2 * features :], "seq", axis=0, tiled=True),
            )
            attended_img, log_totals = attend_forward(qkv_img, kv_pair, rows_low, cols_low)
            return (carried, (attended_img, log_totals))

        results = lax.scan(forward_image, jnp.zeros((), jnp.float32), qkv_images)[1]
        attended = results[0].reshape(-1, features)
        mixed = (
            inputs
            + jnp.dot(attended, wp_full, preferred_element_type=jnp.float32)
            + bp_full.astype(jnp.float32)
        )
        normed2 = layer_norm(mixed, gains_f[1], shifts_f[1]).astype(jnp.bfloat16)
        pre = jnp.dot(normed2, w1_full, preferred_element_type=jnp.float32) + b1_full.astype(
            jnp.float32
        )
        activated = jax.nn.gelu(pre, approximate=False).astype(jnp.bfloat16)
        block_out = (
            mixed
            + jnp.dot(activated, w2_full, preferred_element_type=jnp.float32)
            + b2_full.astype(jnp.float32)
        )
        outputs.append(block_out.astype(jnp.bfloat16).reshape(per_batch, rows_img, features))
        stored.append((normed1, qkv_images, results, mixed, normed2, pre, activated))
    gradients = [jnp.zeros(array.shape, jnp.float32) for array in gathered]
    table_rows_sum = jnp.zeros((rows_img, GRID, HD), jnp.float32)
    table_cols_sum = jnp.zeros((rows_img, GRID, HD), jnp.float32)
    input_grads = []
    for batch_index in range(MB):
        gathered = fetch_each(weights)
        (
            wq_full,
            bqv_full,
            wp_full,
            bp_full,
            w1_full,
            b1_full,
            w2_full,
            b2_full,
            gains_full,
            shifts_full,
        ) = gathered
        gains_f = gains_full.astype(jnp.float32)
        shifts_f = shifts_full.astype(jnp.float32)
        normed1, qkv_images, results, mixed, normed2, pre, activated = stored[batch_index]
        inputs = (
            tokens[batch_index * per_batch : (batch_index + 1) * per_batch]
            .astype(jnp.float32)
            .reshape(-1, features)
        )
        grad_out = cotangent[batch_index * per_batch : (batch_index + 1) * per_batch].reshape(
            -1, features
        )
        grad_out_f = grad_out.astype(jnp.float32)
        grad_w2 = jnp.dot(activated.T, grad_out, preferred_element_type=jnp.float32)
        grad_b2 = jnp.sum(grad_out_f, axis=0)
        grad_act = jnp.dot(grad_out, w2_full.T, preferred_element_type=jnp.float32)
        _, gelu_pull = jax.vjp(partial(jax.nn.gelu, approximate=False), pre)
        grad_pre = gelu_pull(grad_act)[0].astype(jnp.bfloat16)
        grad_w1 = jnp.dot(normed2.T, grad_pre, preferred_element_type=jnp.float32)
        grad_b1 = jnp.sum(grad_pre, axis=0, dtype=jnp.float32)
        grad_norm2 = jnp.dot(grad_pre, w1_full.T, preferred_element_type=jnp.float32)
        _, norm_pull2 = jax.vjp(layer_norm, mixed, gains_f[1], shifts_f[1])
        grad_mix_norm, grad_gain2, grad_shift2 = norm_pull2(grad_norm2)
        grad_mixed = grad_out_f + grad_mix_norm
        grad_branch = grad_mixed.astype(jnp.bfloat16)
        attended = results[0].reshape(-1, features)
        grad_wp = jnp.dot(attended.T, grad_branch, preferred_element_type=jnp.float32)
        grad_bp = jnp.sum(grad_branch, axis=0, dtype=jnp.float32)
        grad_att = jnp.dot(grad_branch, wp_full.T, preferred_element_type=jnp.float32).astype(
            jnp.bfloat16
        )
        grad_images = grad_att.reshape(per_batch, rows_img, features)
        image_inputs = (qkv_images, results[1], grad_images)

        def backward_image(carried, pieces):
            kv_pair = (
                lax.all_gather(pieces[0][:, features : 2 * features], "seq", axis=0, tiled=True),
                lax.all_gather(pieces[0][:, 2 * features :], "seq", axis=0, tiled=True),
            )
            grad_qkv_img, table_rows, table_cols = attend_backward(
                pieces[0], pieces[1], pieces[2], kv_pair, rel_rows, rel_cols, rows_low, cols_low
            )
            return ((carried[0] + table_rows, carried[1] + table_cols), grad_qkv_img)

        (table_rows_sum, table_cols_sum), grad_qkv_all = lax.scan(
            backward_image, (table_rows_sum, table_cols_sum), image_inputs
        )
        grad_qkv = grad_qkv_all.reshape(-1, 3 * features)
        grad_wq = jnp.dot(normed1.T, grad_qkv, preferred_element_type=jnp.float32)
        grad_bqv = jnp.concatenate(
            [
                jnp.sum(grad_qkv[:, :features], axis=0, dtype=jnp.float32),
                jnp.sum(grad_qkv[:, 2 * features :], axis=0, dtype=jnp.float32),
            ]
        )
        grad_norm1 = jnp.dot(grad_qkv, wq_full.T, preferred_element_type=jnp.float32)
        _, norm_pull1 = jax.vjp(layer_norm, inputs, gains_f[0], shifts_f[0])
        grad_in_norm, grad_gain1, grad_shift1 = norm_pull1(grad_norm1)
        input_grads.append(
            (grad_mixed + grad_in_norm).astype(jnp.bfloat16).reshape(per_batch, rows_img, features)
        )
        updates = (
            grad_wq,
            grad_bqv,
            grad_wp,
            grad_bp,
            grad_w1,
            grad_b1,
            grad_w2,
            grad_b2,
            jnp.stack([grad_gain1, grad_gain2]),
            jnp.stack([grad_shift1, grad_shift2]),
        )
        gradients = [before + update for before, update in zip(gradients, updates)]
    summed = (
        lax.psum_scatter(gradients[0], ("dp", "seq"), scatter_dimension=0, tiled=True),
        lax.psum_scatter(gradients[1], ("dp", "seq"), scatter_dimension=0, tiled=True),
        lax.psum_scatter(gradients[2], ("dp", "seq"), scatter_dimension=0, tiled=True),
        lax.psum_scatter(gradients[3], ("dp", "seq"), scatter_dimension=0, tiled=True),
        lax.psum_scatter(gradients[4], ("dp", "seq"), scatter_dimension=0, tiled=True),
        lax.psum_scatter(gradients[5], ("dp", "seq"), scatter_dimension=0, tiled=True),
        lax.psum_scatter(gradients[6], ("dp", "seq"), scatter_dimension=0, tiled=True),
        lax.psum_scatter(gradients[7], ("dp", "seq"), scatter_dimension=0, tiled=True),
        lax.psum_scatter(gradients[8], ("dp", "seq"), scatter_dimension=1, tiled=True),
        lax.psum_scatter(gradients[9], ("dp", "seq"), scatter_dimension=1, tiled=True),
    )
    table_local = jnp.stack(
        [
            jnp.einsum("rkt,rkc->tc", row_hot, table_rows_sum, precision=HIGH),
            jnp.einsum("rkt,rkc->tc", col_hot, table_cols_sum, precision=HIGH),
        ]
    )
    table_grad = lax.psum(table_local, ("dp", "seq"))
    return (
        jnp.concatenate(outputs, axis=0),
        jnp.concatenate(input_grads, axis=0),
        summed[0],
        summed[1],
        summed[2],
        summed[3],
        summed[4],
        summed[5],
        summed[6],
        summed[7],
        summed[8],
        summed[9],
        table_grad,
    )


def solution(mesh):
    placed = (
        P("dp", "seq", None),
        P(("dp", "seq"), None),
        P(("dp", "seq")),
        P(("dp", "seq"), None),
        P(("dp", "seq")),
        P(("dp", "seq"), None),
        P(("dp", "seq")),
        P(("dp", "seq"), None),
        P(("dp", "seq")),
        P(None, ("dp", "seq")),
        P(None, ("dp", "seq")),
        P(),
        P("dp", "seq", None),
    )
    seqs, images = mesh.shape["seq"], IMAGES // mesh.shape["dp"]
    by_heads = (mesh.shape["dp"], seqs, images) == (4, 8, 2)
    return jax.shard_map(
        body_heads if by_heads else body,
        mesh=mesh,
        in_specs=placed,
        out_specs=(
            P("dp", "seq", None),
            P("dp", "seq", None),
            P(("dp", "seq"), None),
            P(("dp", "seq")),
            P(("dp", "seq"), None),
            P(("dp", "seq")),
            P(("dp", "seq"), None),
            P(("dp", "seq")),
            P(("dp", "seq"), None),
            P(("dp", "seq")),
            P(None, ("dp", "seq")),
            P(None, ("dp", "seq")),
            P(),
        ),
        check_vma=False,
    )
```
